32 devices in a mesh: groups: 2 (over y), row: 4 (over z), col: 4 (over x, core).
Axes of the slice: x: 2, y: 2, z: 4, core: 2. Of those that a mesh axis runs over, the one named last changes fastest.
Arguments:
- a_tiles: bfloat16 [16, 16, 128, 128], P(('groups', 'row'), 'col'), parts along dimension 0, may hold values from -0.1875 to 0.1875
- a_cols: int32 [16, 16], P(('groups', 'row'), 'col'), parts along dimension 0, may hold values from -1 to 7, as said below
- b_tiles: bfloat16 [16, 32, 128, 128], P(('groups', 'row'), 'col'), parts along dimension 0, may hold values from -6 to 6
- b_cols: int32 [16, 32], P(('groups', 'row'), 'col'), parts along dimension 0, may hold values from 0 to 63, as said below
- c_cols: int32 [16, 24], P(('groups', 'row'), 'col'), parts along dimension 0, may hold values from 0 to 63, as said below
Outputs:
- c_tiles: bfloat16 [16, 24, 128, 128], P(('groups', 'row'), 'col'), parts along dimension 0
The draws below stay inside these ranges and needn't reach their ends.
There are 2 independent parts, one for each index of `groups`. The reference program is written for one: setup_inputs(seed, part) draws one part's arguments, and reference() takes and returns one part's arrays. A program takes and returns all parts, laid end to end along the dimension named above; each array names one. Nothing has to cross between parts.
Inputs may be any that keep to these rules, and one draw needn't show every extreme that they name: `a_cols`: within a row the indices that are not -1 are distinct; -1 marks an empty slot and row 0 has no empty slot among its first min(16, 8) slots. `b_cols`: slots q * 8 to (q + 1) * 8 - 1 of a row hold distinct columns of q * 16 to (q + 1) * 16 - 1. `c_cols`: slots q * 6 to (q + 1) * 6 - 1 of a row hold distinct columns of q * 16 to (q + 1) * 16 - 1.
All inputs are finite; a program needn't handle non-finite values.
Results may differ from the reference program's by a relative error of at most 0.001.
Values may be sent and summed in bfloat16 or wider, within the bound.
No kernel may reach another device: no remote copies, remote signals or barrier semaphores. Data moves between devices by JAX's collectives and lax.ppermute only.
A program may use at most 192 MiB of HBM per device.

```python
import jax
import jax.numpy as jnp
from jax import lax

B = 128
B_SLOTS_DEV = 8
COLS_DEV = 16
C_SLOTS_DEV = 6
NW = 8
NI = 8
KA = 16
KB = 32
NO = 64
KC = 24


def permuted_rows(key, rows, count, take):
    keys = jax.random.split(key, rows)
    return jax.vmap(lambda single: jax.random.permutation(single, count)[:take])(keys).astype(jnp.int32)


def quarter_columns(key, rows, slots_dev, total_slots):
    quarters = total_slots // slots_dev
    picks = permuted_rows(key, rows * quarters, COLS_DEV, slots_dev)
    picks = picks.reshape(rows, quarters, slots_dev)
    ends = jnp.arange(slots_dev, dtype=jnp.int32) - 1
    ends = jnp.where(ends < 0, COLS_DEV - 1, ends).astype(jnp.int32)
    picks = picks.at[0].set(jnp.broadcast_to(ends[None, :], (quarters, slots_dev)))
    offsets = (jnp.arange(quarters, dtype=jnp.int32) * COLS_DEV)[None, :, None]
    return (picks + offsets).reshape(rows, total_slots).astype(jnp.int32)


def draw_a_cols(key, part):
    key = jax.random.fold_in(key, 11)
    pool = max(KA, NI)
    limit = min(KA, NI)
    order_key, count_key, first_key = jax.random.split(key, 3)
    picks = permuted_rows(order_key, NW, pool, KA)
    first = (NI - 1 - jax.random.permutation(first_key, limit)).astype(jnp.int32)
    first_row = jnp.concatenate([first, jnp.full((KA - limit,), NI, jnp.int32)])
    picks = picks.at[0].set(first_row)
    counts = jax.random.randint(count_key, (NW,), limit // 2 + 1, limit + 1).astype(jnp.int32)
    counts = counts.at[0].set(limit)
    counts = counts.at[1].set(jnp.minimum(counts[1], KA - 1))
    slots = jnp.arange(KA, dtype=jnp.int32)[None, :]
    keep = (slots < counts[:, None]) & (picks < NI)
    return jnp.where(keep, picks, -1).astype(jnp.int32)


def draw_b_cols(key, part):
    key = jax.random.fold_in(key, 23)
    return quarter_columns(key, NI, B_SLOTS_DEV, KB)


def draw_c_cols(key, part):
    key = jax.random.fold_in(key, 37)
    return quarter_columns(key, NW, C_SLOTS_DEV, KC)


def block_levels(stream_key, dims, cuts, smallest, top_value):
    gain = 1.0
    for dim, blocks in cuts:
        draws = jax.random.uniform(jax.random.fold_in(jax.random.fold_in(stream_key, 6), dim), (blocks,), jnp.float32, smallest / len(cuts), top_value / len(cuts))
        gain = gain * jnp.repeat(jnp.exp(draws), dims[dim] // blocks).reshape((-1,) + (1,) * (len(dims) - 1 - dim))
    return gain


def noise(stream_key, dims, deviation, reach, cuts=(), held_as=jnp.bfloat16):
    loudness = block_levels(stream_key, dims, cuts, -0.22, 0.18) if cuts else 1.0
    values = jax.random.normal(stream_key, dims, jnp.float32) * deviation * loudness
    return jnp.minimum(jnp.maximum(values, -reach), reach).astype(held_as)


def setup_inputs(seed: int = 0, part: int = 0) -> dict:
    key_list = jax.random.split(jax.random.key(seed), 6)
    part_splits = jax.random.split(jax.random.fold_in(key_list[5], part), 6)
    a_tiles = noise(part_splits[0], (NW, KA, B, B), (KA * B // 2) ** -0.5, 0.1875, ((0, 4), (1, 4)))
    a_cols = draw_a_cols(jax.random.fold_in(jax.random.fold_in(key_list[5], part), 71), part)
    b_tiles = noise(part_splits[2], (NI, KB, B, B), 1.0, 6.0, ((0, 4), (1, 4)))
    b_cols = draw_b_cols(jax.random.fold_in(jax.random.fold_in(key_list[5], part), 71), part)
    c_cols = draw_c_cols(jax.random.fold_in(jax.random.fold_in(key_list[5], part), 71), part)
    return dict(a_tiles=a_tiles, a_cols=a_cols, b_tiles=b_tiles, b_cols=b_cols, c_cols=c_cols)


def reference(a_tiles, a_cols, b_tiles, b_cols, c_cols):
    span = jnp.arange(NO, dtype=jnp.int32)

    def expand_row(items):
        tiles, cols = items
        pick = (cols[:, None] == span[None, :]).astype(jnp.float32)
        full = jnp.einsum("lc,lyz->cyz", pick, tiles.astype(jnp.float32), precision=lax.Precision.HIGHEST)
        return full.astype(jnp.bfloat16)

    inner_dense = lax.map(expand_row, (b_tiles, b_cols))

    def one_row(items):
        tiles, inner, cols = items
        valid = inner >= 0
        safe = jnp.where(valid, inner, 0).astype(jnp.int32)
        chosen = inner_dense[safe[:, None], cols[None, :]]
        left = tiles.astype(jnp.float32) * valid.astype(jnp.float32)[:, None, None]
        total = jnp.einsum("kxy,kjyz->jxz", left, chosen.astype(jnp.float32), precision=lax.Precision.HIGHEST)
        return total.astype(jnp.bfloat16)

    return lax.map(one_row, (a_tiles, a_cols, c_cols))
```

```python
import functools

import jax
import jax.numpy as jnp
from jax import lax
from jax.experimental import pallas as pl
from jax.experimental.pallas import tpu as pltpu
from jax.sharding import PartitionSpec as P

COLS_DEV = 16

SMEM = pl.BlockSpec(memory_space=pltpu.SMEM)
VMEM = pl.BlockSpec(memory_space=pltpu.VMEM)


def left_kernel(parts, *refs):
    cols, tiles, dense = refs[:parts], refs[parts : 2 * parts], refs[2 * parts]
    dense[...] = jnp.zeros_like(dense)
    for index, source in zip(cols, tiles):
        for i in range(index.shape[0]):
            for s in range(index.shape[1]):
                inner = index[i, s]

                @pl.when(inner >= 0)
                def _():
                    dense[i, inner] = source[i, s]


def step_kernel(parts, last, place, wanted, *refs):
    cols, refs = refs[:parts], refs[parts:]
    tiles, refs = refs[:parts], refs[parts:]
    dense, before, out, total, right, slot = refs
    first = place[0]
    rows, slots = wanted.shape
    inner_rows, inner_slots, block, _ = tiles[0].shape
    total[...] = before[...]

    for p in range(parts):
        source = place[1 + p]

        @pl.when(source >= 0)
        def _():
            for m in range(inner_rows):
                for c in range(COLS_DEV):
                    slot[m, c] = -1
                for l in range(inner_slots):
                    slot[m, cols[p][m, l] - first] = l
            for i in range(rows):
                for m in range(inner_rows):
                    for j in range(slots):
                        l = slot[m, wanted[i, j] - first]
                        tile = tiles[p][m, jnp.maximum(l, 0)]
                        right[m * block : (m + 1) * block, j * block : (j + 1) * block] = jnp.where(
                            l >= 0, tile, jnp.zeros_like(tile)
                        )
                left = jnp.concatenate(
                    [dense[i, source * inner_rows + m] for m in range(inner_rows)], axis=1
                )
                total[i] += jnp.dot(left, right[...], preferred_element_type=jnp.float32)

    if last:
        for i in range(rows):
            for j in range(slots):
                out[i, j] = total[i, :, j * block : (j + 1) * block].astype(out.dtype)
    else:
        out[...] = total[...]


def body(row_count, col_count, a_tiles, a_cols, b_tiles, b_cols, c_cols):
    rows, slots = c_cols.shape
    inner_rows = b_tiles.shape[0]
    block = a_tiles.shape[-1]
    r = lax.axis_index("row")
    first = lax.axis_index("col") * COLS_DEV

    def ring(x, axis, n, shift):
        return lax.ppermute(x, axis, [(k, (k + shift) % n) for k in range(n)])

    def up(x, s):
        return lax.ppermute(x, "row", [(k, k + 1) for k in range(s, row_count - 1)])

    def down(x, s):
        return lax.ppermute(x, "row", [(k, k - 1) for k in range(1, row_count - s)])

    ups, downs = [b_tiles], [b_tiles]
    for s in range(row_count - 1):
        ups.append(up(ups[-1], s))
        downs.append(down(downs[-1], s))
    b_index = [b_cols] + [ring(b_cols, "row", row_count, s) for s in range(1, row_count)]
    a_index = [a_cols] + [ring(a_cols, "col", col_count, s) for s in range(1, col_count)]
    a_parts = [a_tiles] + [ring(a_tiles, "col", col_count, s) for s in range(1, col_count)]

    dense = pl.pallas_call(
        functools.partial(left_kernel, col_count),
        out_shape=jax.ShapeDtypeStruct((rows, inner_rows * row_count, block, block), a_tiles.dtype),
        in_specs=[SMEM] * col_count + [VMEM] * col_count,
        out_specs=VMEM,
        compiler_params=pltpu.CompilerParams(vmem_limit_bytes=32 * 2**20),
    )(*a_index, *a_parts)

    def step(sources, cols, tiles, before, last):
        parts = len(tiles)
        place = jnp.stack([first] + sources).astype(jnp.int32)
        if last:
            out = jax.ShapeDtypeStruct((rows, slots, block, block), a_tiles.dtype)
        else:
            out = jax.ShapeDtypeStruct((rows, block, slots * block), jnp.float32)
        flops = 2 * rows * parts * inner_rows * slots * block**3
        return pl.pallas_call(
            functools.partial(step_kernel, parts, last),
            out_shape=out,
            in_specs=[SMEM] * (2 + parts) + [VMEM] * (parts + 2),
            out_specs=VMEM,
            scratch_shapes=[
                pltpu.VMEM((rows, block, slots * block), jnp.float32),
                pltpu.VMEM((inner_rows * block, slots * block), b_tiles.dtype),
                pltpu.SMEM((inner_rows, COLS_DEV), jnp.int32),
            ],
            compiler_params=pltpu.CompilerParams(vmem_limit_bytes=32 * 2**20),
            cost_estimate=pl.CostEstimate(flops=flops, bytes_accessed=2**21, transcendentals=0),
        )(place, c_cols, *cols, *tiles, dense, before)

    total = jnp.zeros((rows, block, slots * block), jnp.float32)
    for s in range(1, row_count):
        below = r - s
        above = jnp.where(r + s < row_count, r + s, -1)
        sources, cols, tiles = [below, above], [b_index[s], b_index[row_count - s]], [ups[s], downs[s]]
        if s == 1:
            sources, cols, tiles = [r] + sources, [b_cols] + cols, [b_tiles] + tiles
        total = step(sources, cols, tiles, total, s == row_count - 1)
    return total


def solution(mesh):
    return jax.shard_map(
        functools.partial(body, mesh.shape["row"], mesh.shape["col"]),
        mesh=mesh,
        in_specs=(
            P(("groups", "row"), "col", None, None),
            P(("groups", "row"), "col"),
            P(("groups", "row"), "col", None, None),
            P(("groups", "row"), "col"),
            P(("groups", "row"), "col"),
        ),
        out_specs=P(("groups", "row"), "col", None, None),
        check_vma=False,
    )
```

```python
import functools

import jax
import jax.numpy as jnp
from jax import lax
from jax.experimental import pallas as pl
from jax.experimental.pallas import tpu as pltpu
from jax.sharding import PartitionSpec as P

COLS_DEV = 16

SMEM = pl.BlockSpec(memory_space=pltpu.SMEM)
VMEM = pl.BlockSpec(memory_space=pltpu.VMEM)
PARAMS = pltpu.CompilerParams(vmem_limit_bytes=32 * 2**20)


def left_kernel(index, *refs):
    tiles, dense = refs[:-1], refs[-1]
    dense[...] = jnp.zeros_like(dense)
    rows, slots = tiles[0].shape[:2]
    for p, source in enumerate(tiles):
        for i in range(rows):
            for s in range(slots):
                inner = index[i, p * slots + s]

                @pl.when(inner >= 0)
                def _():
                    dense[i, inner] = source[i, s]


def step_kernel(parts, last, place, wanted, index, *refs):
    tiles, refs = refs[:parts], refs[parts:]
    if last:
        dense, before, out, total, right, slot = refs
        total[...] = before[...]
    elif len(refs) == 5:
        dense, before, total, right, slot = refs
        total[...] = before[...]
    else:
        dense, total, right, slot = refs
        total[...] = jnp.zeros_like(total)
    first, me = place[0], place[1]
    rows, slots = wanted.shape
    inner_slots, block, _ = tiles[0].shape[-3:]

    for p in range(parts):
        source = place[2 + 2 * p]

        @pl.when(source >= 0)
        def _():
            chunk = tiles[p].shape[0]
            held = source ^ me
            per = index.shape[1]
            start = place[3 + 2 * p]
            for m in range(chunk):
                for c in range(COLS_DEV):
                    slot[m, c] = -1
                for l in range(inner_slots):
                    slot[m, index[held, (start + m) * inner_slots + l] - first] = l
            for i in range(rows):
                for m in range(chunk):
                    for j in range(slots):
                        l = slot[m, wanted[i, j] - first]
                        tile = tiles[p][m, jnp.maximum(l, 0)]
                        right[m * block : (m + 1) * block, j * block : (j + 1) * block] = jnp.where(
                            l >= 0, tile, jnp.zeros_like(tile)
                        )
                inner = source * (per // inner_slots) + start
                left = jnp.concatenate([dense[i, inner + m] for m in range(chunk)], axis=1)
                total[i] += jnp.dot(
                    left, right[: chunk * block, :], preferred_element_type=jnp.float32
                )

    if last:
        for i in range(rows):
            for j in range(slots):
                out[i, j] = total[i, :, j * block : (j + 1) * block].astype(out.dtype)


def butterfly(x, axis, n):
    d = 1
    while d < n:
        other = lax.ppermute(x, axis, [(k, k ^ d) for k in range(n)])
        x = jnp.concatenate([x, other], axis=0)
        d *= 2
    return x


def body(row_count, col_count, a_tiles, a_cols, b_tiles, b_cols, c_cols):
    rows, slots = c_cols.shape
    inner_rows, inner_slots = b_cols.shape
    block = a_tiles.shape[-1]
    r = lax.axis_index("row")
    first = lax.axis_index("col") * COLS_DEV
    odd = r % 2

    def pairs(kind, t):
        found = []
        for k in range(row_count):
            side = 1 if k % 2 == kind else -1
            if 0 <= k + side < row_count and 0 <= k + side * t < row_count:
                found.append((k + side, k))
        return found

    def origin(kind, t):
        side = jnp.where(odd == kind, 1, -1)
        row = r + side * t
        return jnp.where((row >= 0) & (row < row_count), row, -1)

    def send(x, kind, t):
        return lax.ppermute(x, "row", pairs(kind, t))

    chunks = [b_tiles[m : m + 1] for m in range(inner_rows)]
    rounds = {1: {}}
    whole = send(b_tiles, 0, 1)
    rounds[1][1] = [send(c, 1, 1) for c in chunks]
    rounds[1][0] = [whole[m : m + 1] for m in range(inner_rows)]
    b_index = butterfly(b_cols.reshape(1, -1), "row", row_count)
    a_index = butterfly(a_cols[None], "col", col_count)
    a_index = a_index.transpose(1, 0, 2).reshape(rows, -1)
    a_parts = [a_tiles] + [
        lax.ppermute(a_tiles, "col", [(k, k ^ d) for k in range(col_count)]) for d in range(1, col_count)
    ]
    dense = pl.pallas_call(
        left_kernel,
        out_shape=jax.ShapeDtypeStruct((rows, inner_rows * row_count, block, block), a_tiles.dtype),
        in_specs=[SMEM] + [VMEM] * col_count,
        out_specs=VMEM,
        compiler_params=PARAMS,
    )(a_index, *a_parts)

    def step(pieces, before, last):
        parts = len(pieces)
        place = [first, r]
        for source, start, _ in pieces:
            place += [source, jnp.int32(start)]
        place = jnp.stack(place).astype(jnp.int32)
        if last:
            out = jax.ShapeDtypeStruct((rows, slots, block, block), a_tiles.dtype)
        else:
            out = jax.ShapeDtypeStruct((rows, block, slots * block), jnp.float32)
        scratch = [
            pltpu.VMEM((inner_rows * block, slots * block), b_tiles.dtype),
            pltpu.SMEM((inner_rows, COLS_DEV), jnp.int32),
        ]
        if last:
            scratch = [pltpu.VMEM((rows, block, slots * block), jnp.float32)] + scratch
        flops = 2 * rows * parts * inner_rows * slots * block**3
        held = [dense] if before is None else [dense, before]
        return pl.pallas_call(
            functools.partial(step_kernel, parts, last),
            out_shape=out,
            in_specs=[SMEM] * 3 + [VMEM] * (parts + len(held)),
            out_specs=VMEM,
            scratch_shapes=scratch,
            compiler_params=PARAMS,
            cost_estimate=pl.CostEstimate(flops=flops, bytes_accessed=2**21, transcendentals=0),
        )(place, c_cols, b_index, *[tiles for _, _, tiles in pieces], *held)

    total = None
    for t in range(1, row_count):
        pieces = [(r, 0, b_tiles), (origin(0, 1), 0, whole)] if t == 1 else []
        for kind in (0, 1):
            if not pairs(kind, t) or (kind, t) == (0, 1):
                continue
            pieces += [(origin(kind, t), m, c) for m, c in enumerate(rounds[t][kind])]
        if t + 1 < row_count:
            rounds[t + 1] = {
                kind: [send(c, kind, t + 1) for c in rounds[t][1 - kind]]
                for kind in (0, 1)
                if pairs(kind, t + 1)
            }
        total = step(pieces, total, t + 1 == row_count)
    return total


def solution(mesh):
    return jax.shard_map(
        functools.partial(body, mesh.shape["row"], mesh.shape["col"]),
        mesh=mesh,
        in_specs=(
            P(("groups", "row"), "col", None, None),
            P(("groups", "row"), "col"),
            P(("groups", "row"), "col", None, None),
            P(("groups", "row"), "col"),
            P(("groups", "row"), "col"),
        ),
        out_specs=P(("groups", "row"), "col", None, None),
        check_vma=False,
    )
```

```python
import functools

import jax
import jax.numpy as jnp
from jax import lax
from jax.experimental import pallas as pl
from jax.experimental.pallas import tpu as pltpu
from jax.sharding import PartitionSpec as P

COLS_DEV = 16

SMEM = pl.BlockSpec(memory_space=pltpu.SMEM)
VMEM = pl.BlockSpec(memory_space=pltpu.VMEM)
PARAMS = pltpu.CompilerParams(vmem_limit_bytes=32 * 2**20)


def prepare_kernel(row_count, col_count, place, wanted, a_index, b_index, *refs):
    tiles, refs = refs[:col_count], refs[col_count:]
    dense, table, slot = refs
    first, r = place[0], place[1]
    rows, slots = wanted.shape
    inner_rows, inner_slots = b_index.shape[0] // row_count, b_index.shape[1]
    for s in range(row_count):
        source = r ^ s
        for m in range(inner_rows):
            for c in range(COLS_DEV):
                slot[c] = -1
            for l in range(inner_slots):
                slot[b_index[s * inner_rows + m, l] - first] = l
            for i in range(rows):
                for j in range(slots):
                    table[i, (source * inner_rows + m) * slots + j] = slot[wanted[i, j] - first]
    dense[...] = jnp.zeros_like(dense)
    for p, source in enumerate(tiles):
        for i in range(rows):
            for s in range(a_index.shape[1]):
                inner = a_index[p * rows + i, s]

                @pl.when(inner >= 0)
                def _():
                    dense[i, inner] = source[i, s]


def step_kernel(parts, last, place, table, *refs):
    tiles, refs = refs[:parts], refs[parts:]
    if last:
        dense, before, out, total, right = refs
        total[...] = before[...]
    elif len(refs) == 4:
        dense, before, total, right = refs
        total[...] = before[...]
    else:
        dense, total, right = refs
        total[...] = jnp.zeros_like(total)
    rows, _, block, _ = dense.shape
    inner_rows = tiles[0].shape[0]
    slots = right.shape[1] // block

    for p in range(parts):
        source = place[2 + p]

        @pl.when(source >= 0)
        def _():
            for i in range(rows):
                for m in range(inner_rows):
                    for j in range(slots):
                        l = table[i, (source * inner_rows + m) * slots + j]
                        tile = tiles[p][m, jnp.maximum(l, 0)]
                        right[m * block : (m + 1) * block, j * block : (j + 1) * block] = jnp.where(
                            l >= 0, tile, jnp.zeros_like(tile)
                        )
                left = jnp.concatenate(
                    [dense[i, source * inner_rows + m] for m in range(inner_rows)], axis=1
                )
                total[i] += jnp.dot(left, right[...], preferred_element_type=jnp.float32)

    if last:
        for i in range(rows):
            for j in range(slots):
                out[i, j] = total[i, :, j * block : (j + 1) * block].astype(out.dtype)


def body(row_count, col_count, a_tiles, a_cols, b_tiles, b_cols, c_cols):
    rows, slots = c_cols.shape
    inner_rows = b_tiles.shape[0]
    block = a_tiles.shape[-1]
    inner_count = inner_rows * row_count
    r = lax.axis_index("row")
    first = lax.axis_index("col") * COLS_DEV
    sides = [jnp.where(r % 2 == kind, 1, -1) for kind in (0, 1)]

    def pairs(kind, t):
        found = []
        for k in range(row_count):
            side = 1 if k % 2 == kind else -1
            if 0 <= k + side < row_count and 0 <= k + side * t < row_count:
                found.append((k + side, k))
        return found

    def origin(kind, t):
        row = r + sides[kind] * t
        return jnp.where((row >= 0) & (row < row_count), row, -1)

    def swap(x, axis, n, d):
        return lax.ppermute(x, axis, [(k, k ^ d) for k in range(n)])

    def halves(n):
        d = n // 2
        while d:
            yield d
            d //= 2

    def gather(x, axis, n, stages):
        for d in stages:
            x = jnp.concatenate([x, swap(x, axis, n, d)], axis=0)
            yield x

    rounds = [[lax.ppermute(b_tiles, "row", pairs(kind, 1)) for kind in (0, 1)]]
    a_parts = [a_tiles]
    for d in halves(col_count):
        a_parts = a_parts + [swap(x, "col", col_count, d) for x in a_parts]
    a_index = list(gather(a_cols, "col", col_count, halves(col_count)))
    b_index = list(gather(b_cols, "row", row_count, reversed(list(halves(row_count)))))
    for t in range(2, row_count):
        even, odd = rounds[-1]
        if t == 2:
            early = (even, odd, a_index[0], b_index[0], a_parts[1])
            even, odd, a_index[0], b_index[0], a_parts[1] = lax.optimization_barrier(early)
        if t == 3:
            odd, a_index, b_index, a_parts = lax.optimization_barrier((odd, a_index, b_index, a_parts))
        rounds[-1] = [even, odd]
        rounds.append(
            [
                lax.ppermute(x, "row", pairs(kind, t)) if pairs(kind, t) else None
                for kind, x in ((0, odd), (1, even))
            ]
        )

    here = jnp.stack([first, r]).astype(jnp.int32)
    dense, table = pl.pallas_call(
        functools.partial(prepare_kernel, row_count, col_count),
        out_shape=(
            jax.ShapeDtypeStruct((rows, inner_count, block, block), a_tiles.dtype),
            jax.ShapeDtypeStruct((rows, inner_count * slots), jnp.int32),
        ),
        in_specs=[SMEM] * 4 + [VMEM] * col_count,
        out_specs=(VMEM, SMEM),
        scratch_shapes=[pltpu.SMEM((COLS_DEV,), jnp.int32)],
        compiler_params=PARAMS,
    )(here, c_cols, a_index[-1], b_index[-1], *a_parts)

    def step(pieces, before, last):
        parts = len(pieces)
        place = jnp.stack([first, r] + [source for source, _ in pieces]).astype(jnp.int32)
        if last:
            out = jax.ShapeDtypeStruct((rows, slots, block, block), a_tiles.dtype)
        else:
            out = jax.ShapeDtypeStruct((rows, block, slots * block), jnp.float32)
        scratch = [pltpu.VMEM((inner_rows * block, slots * block), b_tiles.dtype)]
        if last:
            scratch = [pltpu.VMEM((rows, block, slots * block), jnp.float32)] + scratch
        flops = 2 * rows * parts * inner_rows * slots * block**3
        held = [dense] if before is None else [dense, before]
        return pl.pallas_call(
            functools.partial(step_kernel, parts, last),
            out_shape=out,
            in_specs=[SMEM] * 2 + [VMEM] * (parts + len(held)),
            out_specs=VMEM,
            scratch_shapes=scratch,
            compiler_params=PARAMS,
            cost_estimate=pl.CostEstimate(flops=flops, bytes_accessed=2**21, transcendentals=0),
        )(place, table, *[tiles for _, tiles in pieces], *held)

    total = None
    for t in range(1, row_count):
        pieces = [(r, b_tiles)] if t == 1 else []
        for kind in (0, 1):
            if rounds[t - 1][kind] is not None:
                pieces.append((origin(kind, t), rounds[t - 1][kind]))
        total = step(pieces, total, t + 1 == row_count)
    return total


def solution(mesh):
    return jax.shard_map(
        functools.partial(body, mesh.shape["row"], mesh.shape["col"]),
        mesh=mesh,
        in_specs=(
            P(("groups", "row"), "col", None, None),
            P(("groups", "row"), "col"),
            P(("groups", "row"), "col", None, None),
            P(("groups", "row"), "col"),
            P(("groups", "row"), "col"),
        ),
        out_specs=P(("groups", "row"), "col", None, None),
        check_vma=False,
    )
```

```python
import functools

import jax
import jax.numpy as jnp
from jax import lax
from jax.experimental import pallas as pl
from jax.experimental.pallas import tpu as pltpu
from jax.sharding import PartitionSpec as P

COLS_DEV = 16

HBM = pl.BlockSpec(memory_space=pltpu.HBM)
SMEM = pl.BlockSpec(memory_space=pltpu.SMEM)
VMEM = pl.BlockSpec(memory_space=pltpu.VMEM)
PARAMS = pltpu.CompilerParams(vmem_limit_bytes=32 * 2**20)


def tail(count):
    return -(-count // 16) * 16


def pack_kernel(a_index, b_index, a_tiles, b_tiles, a_out, *refs):
    b_outs, sems = refs[:-1], refs[-1]
    size = a_tiles.shape[0]
    copies = [pltpu.make_async_copy(a_tiles, a_out.at[:size], sems.at[0])]
    size = b_tiles.shape[1]
    for m, out in enumerate(b_outs):
        copies.append(pltpu.make_async_copy(b_tiles.at[m], out.at[:size], sems.at[1 + m]))
    for copy in copies:
        copy.start()
    for index, out in ((a_index, a_out), (b_index, b_outs[0])):
        count = index.shape[0] * index.shape[1]
        rows = tail(count)
        row = lax.broadcasted_iota(jnp.int32, (rows, out.shape[1]), 0)
        found = jnp.zeros(row.shape, jnp.float32)
        for k in range(count):
            value = index[k // index.shape[1], k % index.shape[1]].astype(jnp.float32)
            found = jnp.where(row == k, value, found)
        out[out.shape[0] - rows :, :] = found.astype(out.dtype)
    for copy in copies:
        copy.wait()


def left_kernel(index, own, *refs):
    parts, dense = (own,) + refs[:-1], refs[-1]
    dense[...] = jnp.zeros_like(dense)
    rows, _, block, _ = dense.shape
    slots = index.shape[1] // rows
    for p, part in enumerate(parts):
        for i in range(rows):
            for s in range(slots):
                inner = index[p, i * slots + s]
                start = (i * slots + s) * block

                @pl.when(inner >= 0)
                def _():
                    dense[i, inner] = part[start : start + block, :]


def step_kernel(which, last, first_step, place, wanted, index, *refs):
    parts = len(which)
    tiles, refs = refs[:parts], refs[parts:]
    dense, refs = refs[0], refs[1:]
    before, refs = (None, refs) if first_step else (refs[0], refs[1:])
    if last:
        out, total, right, slot = refs
    else:
        total, right, slot = refs
    total[...] = jnp.zeros_like(total) if first_step else before[...]
    first = place[0]
    rows, slots = wanted.shape
    block = dense.shape[2]
    inner_slots = tiles[0].shape[0] // block

    for p, (at, m) in enumerate(which):
        inner = place[1 + p]

        @pl.when(inner >= 0)
        def _():
            for c in range(COLS_DEV):
                slot[c] = -1
            for l in range(inner_slots):
                slot[index[at, m * inner_slots + l] - first] = l
            for i in range(rows):
                for j in range(slots):
                    l = slot[wanted[i, j] - first]
                    start = pl.multiple_of(jnp.maximum(l, 0) * block, block)
                    tile = tiles[p][pl.ds(start, block), :]
                    right[i, :, j * block : (j + 1) * block] = jnp.where(l >= 0, tile, jnp.zeros_like(tile))
            for i in range(rows):
                total[i] += jnp.dot(dense[i, inner], right[i], preferred_element_type=jnp.float32)

    if last:
        for i in range(rows):
            for j in range(slots):
                out[i, j] = total[i, :, j * block : (j + 1) * block].astype(out.dtype)


def body(row_count, col_count, a_tiles, a_cols, b_tiles, b_cols, c_cols):
    rows, slots = c_cols.shape
    inner_rows, inner_slots = b_cols.shape
    block = a_tiles.shape[-1]
    dtype = b_tiles.dtype
    a_count, b_count = a_cols.size, b_cols.size
    r = lax.axis_index("row")
    first = lax.axis_index("col") * COLS_DEV
    sides = [jnp.where(r % 2 == kind, 1, -1) for kind in (0, 1)]

    sizes = [inner_slots * block] * inner_rows
    sizes[0] += tail(b_count)
    packed = pl.pallas_call(
        pack_kernel,
        out_shape=[
            jax.ShapeDtypeStruct((size, block), dtype) for size in [a_count * block + tail(a_count)] + sizes
        ],
        in_specs=[SMEM, SMEM, HBM, HBM],
        out_specs=[VMEM] * (1 + inner_rows),
        scratch_shapes=[pltpu.SemaphoreType.DMA((1 + inner_rows,))],
        compiler_params=PARAMS,
    )(a_cols, b_cols, a_tiles.reshape(-1, block), b_tiles.reshape(inner_rows, -1, block))
    a_own, b_own = packed[0], packed[1:]

    def exchange(x, kind):
        pairs = []
        for k in range(row_count):
            other = k + (1 if k % 2 == kind else -1)
            pairs.append((k, other if 0 <= other < row_count else k))
        return lax.ppermute(x, "row", pairs)

    def useful(kind, t):
        return any(0 <= k + (t if k % 2 == kind else -t) < row_count for k in range(row_count))

    def origin(kind, t):
        row = r + sides[kind] * t
        return jnp.where((row >= 0) & (row < row_count), row, -1)

    def in_order(chunks):
        chunks = list(chunks)
        for m in range(1, len(chunks)):
            chunks[m] = lax.optimization_barrier((chunks[m - 1], chunks[m]))[1]
        return chunks

    rounds = [[[None] * inner_rows, [None] * inner_rows]]
    for m in range(inner_rows):
        for kind in (0, 1):
            rounds[0][kind][m] = exchange(b_own[m], kind)
    a_parts = [a_own]
    d = col_count // 2
    while d:
        sent = a_parts
        if d < col_count // 2:
            sent = lax.optimization_barrier((a_parts, rounds[0][0][-1]))[0]
        a_parts = a_parts + [lax.ppermute(x, "col", [(k, k ^ d) for k in range(col_count)]) for x in sent]
        d //= 2
    for t in range(2, row_count):
        before = [None if chunks is None else in_order(chunks) for chunks in rounds[-1]]
        if t == 3:
            before[1][-1] = lax.optimization_barrier((before[1][-1], a_parts))[0]
        rounds[-1] = before
        rounds.append(
            [[exchange(x, kind) for x in before[1 - kind]] if useful(kind, t) else None for kind in (0, 1)]
        )

    def index_of(parts, count):
        rows_of = [x[x.shape[0] - tail(count) :, 0][:count] for x in parts]
        return jnp.stack(rows_of).astype(jnp.int32)

    dense = pl.pallas_call(
        left_kernel,
        out_shape=jax.ShapeDtypeStruct((rows, inner_rows * row_count, block, block), dtype),
        in_specs=[SMEM] + [VMEM] * col_count,
        out_specs=VMEM,
        compiler_params=PARAMS,
    )(index_of(a_parts, a_count), *a_parts)

    def step(groups, picks, before, last):
        place = jnp.stack([first] + [groups[g][0] * inner_rows + m for g, m, _ in picks]).astype(jnp.int32)
        valid = [jnp.int32(0)] + [groups[g][0] for g, _, _ in picks]
        place = jnp.where(jnp.stack(valid) >= 0, place, -1)
        if last:
            out = jax.ShapeDtypeStruct((rows, slots, block, block), dtype)
        else:
            out = jax.ShapeDtypeStruct((rows, block, slots * block), jnp.float32)
        scratch = [pltpu.VMEM((rows, block, slots * block), dtype), pltpu.SMEM((COLS_DEV,), jnp.int32)]
        if last:
            scratch = [pltpu.VMEM((rows, block, slots * block), jnp.float32)] + scratch
        flops = 2 * rows * len(picks) * slots * block**3
        held = [dense] if before is None else [dense, before]
        return pl.pallas_call(
            functools.partial(step_kernel, [(g, m) for g, m, _ in picks], last, before is None),
            out_shape=out,
            in_specs=[SMEM] * 3 + [VMEM] * (len(picks) + len(held)),
            out_specs=VMEM,
            scratch_shapes=scratch,
            compiler_params=PARAMS,
            cost_estimate=pl.CostEstimate(flops=flops, bytes_accessed=2**21, transcendentals=0),
        )(place, c_cols, index_of([x for _, x in groups], b_count), *[x for _, _, x in picks], *held)

    def of_round(t):
        return [(origin(kind, t), chunks) for kind, chunks in enumerate(rounds[t - 1]) if chunks is not None]

    total = None
    for t in range(1, row_count):
        pieces = ([(r, b_own)] if t == 1 else []) + of_round(t)
        groups = [(source, chunks[0]) for source, chunks in pieces]
        picks = [(g, m, x) for g, (_, chunks) in enumerate(pieces) for m, x in enumerate(chunks)]
        if t + 1 < row_count:
            total = step(groups, picks, total, False)
        else:
            if len(picks) > 1:
                total = step(groups, picks[:-1], total, False)
            total = step(groups, picks[-1:], total, True)
    return total


def solution(mesh):
    return jax.shard_map(
        functools.partial(body, mesh.shape["row"], mesh.shape["col"]),
        mesh=mesh,
        in_specs=(
            P(("groups", "row"), "col", None, None),
            P(("groups", "row"), "col"),
            P(("groups", "row"), "col", None, None),
            P(("groups", "row"), "col"),
            P(("groups", "row"), "col"),
        ),
        out_specs=P(("groups", "row"), "col", None, None),
        check_vma=False,
    )
```

```python
import functools

import jax
import jax.numpy as jnp
from jax import lax
from jax.experimental import pallas as pl
from jax.experimental.pallas import tpu as pltpu
from jax.sharding import PartitionSpec as P

COLS_DEV = 16

SMEM = pl.BlockSpec(memory_space=pltpu.SMEM)
VMEM = pl.BlockSpec(memory_space=pltpu.VMEM)
PARAMS = pltpu.CompilerParams(vmem_limit_bytes=32 * 2**20)


def prepare_kernel(row_count, col_count, place, wanted, a_index, b_index, *refs):
    tiles, refs = refs[:col_count], refs[col_count:]
    dense, table, slot = refs
    first, r = place[0], place[1]
    rows, slots = wanted.shape
    inner_rows, inner_slots = b_index.shape[0] // row_count, b_index.shape[1]
    for s in range(row_count):
        source = r ^ s
        for m in range(inner_rows):
            for c in range(COLS_DEV):
                slot[c] = -1
            for l in range(inner_slots):
                slot[b_index[s * inner_rows + m, l] - first] = l
            for i in range(rows):
                for j in range(slots):
                    table[i, (source * inner_rows + m) * slots + j] = slot[wanted[i, j] - first]
    dense[...] = jnp.zeros_like(dense)
    for p, source in enumerate(tiles):
        for i in range(rows):
            for s in range(a_index.shape[1]):
                inner = a_index[p * rows + i, s]

                @pl.when(inner >= 0)
                def _():
                    dense[i, inner] = source[i, s]


def step_kernel(parts, last, place, table, *refs):
    tiles, refs = refs[:parts], refs[parts:]
    if last:
        dense, before, out, total, right = refs
        total[...] = before[...]
    elif len(refs) == 4:
        dense, before, total, right = refs
        total[...] = before[...]
    else:
        dense, total, right = refs
        total[...] = jnp.zeros_like(total)
    rows, _, block, _ = dense.shape
    inner_rows = tiles[0].shape[0]
    slots = right.shape[1] // block

    for p in range(parts):
        source = place[2 + p]

        @pl.when(source >= 0)
        def _():
            for i in range(rows):
                for m in range(inner_rows):
                    for j in range(slots):
                        l = table[i, (source * inner_rows + m) * slots + j]
                        tile = tiles[p][m, jnp.maximum(l, 0)]
                        right[m * block : (m + 1) * block, j * block : (j + 1) * block] = jnp.where(
                            l >= 0, tile, jnp.zeros_like(tile)
                        )
                left = jnp.concatenate(
                    [dense[i, source * inner_rows + m] for m in range(inner_rows)], axis=1
                )
                total[i] += jnp.dot(left, right[...], preferred_element_type=jnp.float32)

    if last:
        for i in range(rows):
            for j in range(slots):
                out[i, j] = total[i, :, j * block : (j + 1) * block].astype(out.dtype)


def body(row_count, col_count, a_tiles, a_cols, b_tiles, b_cols, c_cols):
    rows, slots = c_cols.shape
    inner_rows = b_tiles.shape[0]
    block = a_tiles.shape[-1]
    inner_count = inner_rows * row_count
    r = lax.axis_index("row")
    first = lax.axis_index("col") * COLS_DEV
    q = lax.axis_index("col")

    def side_of(kind, row, col):
        return 1 - 2 * ((row + col + kind) % 2)

    def exchange(x, kind, t):
        pairs = []
        for k in range(row_count):
            for c in range(col_count):
                side = side_of(kind, k, c)
                other = k + side
                inside = 0 <= other < row_count
                wanted = inside and (0 <= k + side * t < row_count or 0 <= other - side * t < row_count)
                pairs.append(((other if wanted else k) * col_count + c, k * col_count + c))
        return lax.ppermute(x, ("row", "col"), pairs)

    def origin(kind, t):
        row = r + side_of(kind, r, q) * t
        return jnp.where((row >= 0) & (row < row_count), row, -1)

    def swap(x, axis, n, d):
        return lax.ppermute(x, axis, [(k, k ^ d) for k in range(n)])

    def halves(n):
        d = n // 2
        while d:
            yield d
            d //= 2

    def gather(x, axis, n, stages):
        for d in stages:
            x = jnp.concatenate([x, swap(x, axis, n, d)], axis=0)
            yield x

    def kinds(t):
        return (0, 1) if t % 2 else (1, 0)

    rounds = [[exchange(b_tiles, kind, 1) for kind in kinds(1)]]
    a_parts = [a_tiles]
    for d in halves(col_count):
        a_parts = a_parts + [swap(x, "col", col_count, d) for x in a_parts]
    a_index = list(gather(a_cols, "col", col_count, halves(col_count)))
    b_index = list(gather(b_cols, "row", row_count, reversed(list(halves(row_count)))))
    for t in range(2, row_count):
        one, two = rounds[-1]
        if t == 2:
            two = lax.optimization_barrier((two, a_index[0], b_index[0], a_parts[1]))[0]
        if t == 3:
            two = lax.optimization_barrier((two, a_index, b_index, a_parts))[0]
        rounds.append([exchange(x, kind, t) for kind, x in zip(kinds(t), (one, two))])

    here = jnp.stack([first, r]).astype(jnp.int32)
    dense, table = pl.pallas_call(
        functools.partial(prepare_kernel, row_count, col_count),
        out_shape=(
            jax.ShapeDtypeStruct((rows, inner_count, block, block), a_tiles.dtype),
            jax.ShapeDtypeStruct((rows, inner_count * slots), jnp.int32),
        ),
        in_specs=[SMEM] * 4 + [VMEM] * col_count,
        out_specs=(VMEM, SMEM),
        scratch_shapes=[pltpu.SMEM((COLS_DEV,), jnp.int32)],
        compiler_params=PARAMS,
    )(here, c_cols, a_index[-1], b_index[-1], *a_parts)

    def step(pieces, before, last):
        parts = len(pieces)
        place = jnp.stack([first, r] + [source for source, _ in pieces]).astype(jnp.int32)
        if last:
            out = jax.ShapeDtypeStruct((rows, slots, block, block), a_tiles.dtype)
        else:
            out = jax.ShapeDtypeStruct((rows, block, slots * block), jnp.float32)
        scratch = [pltpu.VMEM((inner_rows * block, slots * block), b_tiles.dtype)]
        if last:
            scratch = [pltpu.VMEM((rows, block, slots * block), jnp.float32)] + scratch
        flops = 2 * rows * parts * inner_rows * slots * block**3
        held = [dense] if before is None else [dense, before]
        return pl.pallas_call(
            functools.partial(step_kernel, parts, last),
            out_shape=out,
            in_specs=[SMEM] * 2 + [VMEM] * (parts + len(held)),
            out_specs=VMEM,
            scratch_shapes=scratch,
            compiler_params=PARAMS,
            cost_estimate=pl.CostEstimate(flops=flops, bytes_accessed=2**21, transcendentals=0),
        )(place, table, *[tiles for _, tiles in pieces], *held)

    total = None
    for t in range(1, row_count):
        pieces = [(origin(kind, t), x) for kind, x in zip(kinds(t), rounds[t - 1])]
        if t == 1:
            pieces = [(r, b_tiles)] + pieces
        if t + 1 < row_count:
            total = step(pieces, total, False)
        else:
            total = step(pieces[:-1], total, False)
            total = step(pieces[-1:], total, True)
    return total


def solution(mesh):
    return jax.shard_map(
        functools.partial(body, mesh.shape["row"], mesh.shape["col"]),
        mesh=mesh,
        in_specs=(
            P(("groups", "row"), "col", None, None),
            P(("groups", "row"), "col"),
            P(("groups", "row"), "col", None, None),
            P(("groups", "row"), "col"),
            P(("groups", "row"), "col"),
        ),
        out_specs=P(("groups", "row"), "col", None, None),
        check_vma=False,
    )
```

```python
import functools

import jax
import jax.numpy as jnp
from jax import lax
from jax.experimental import pallas as pl
from jax.experimental.pallas import tpu as pltpu
from jax.sharding import PartitionSpec as P

COLS_DEV = 16

SMEM = pl.BlockSpec(memory_space=pltpu.SMEM)
VMEM = pl.BlockSpec(memory_space=pltpu.VMEM)
PARAMS = pltpu.CompilerParams(vmem_limit_bytes=32 * 2**20)


def tail(count):
    return -(-count // 16) * 16


def pack_kernel(index, tiles, out):
    size = tiles.shape[0]
    out[:size, :] = tiles[...]
    row = lax.broadcasted_iota(jnp.int32, (out.shape[0] - size, out.shape[1]), 0)
    found = jnp.zeros(row.shape, jnp.float32)
    slots = index.shape[1]
    for k in range(index.shape[0] * slots):
        found = jnp.where(row == k, index[k // slots, k % slots].astype(jnp.float32), found)
    out[size:, :] = found.astype(out.dtype)


def left_kernel(index, *refs):
    parts, dense = refs[:-1], refs[-1]
    dense[...] = jnp.zeros_like(dense)
    rows, _, block, _ = dense.shape
    slots = index.shape[1] // rows
    for p, part in enumerate(parts):
        for i in range(rows):
            for s in range(slots):
                inner = index[p, i * slots + s]
                start = (i * slots + s) * block

                @pl.when(inner >= 0)
                def _():
                    dense[i, inner] = part[start : start + block, :]


def step_kernel(parts, last, place, wanted, *refs):
    cols, refs = refs[:parts], refs[parts:]
    tiles, refs = refs[:parts], refs[parts:]
    dense, refs = refs[0], refs[1:]
    before, out, right, slot = refs if len(refs) == 4 else (None,) + refs
    first = place[0]
    rows, slots = wanted.shape
    inner_rows, inner_slots, block, _ = tiles[0].shape

    sums = [None if before is None else before[i] for i in range(rows)]
    for p in range(parts):
        for m in range(inner_rows):
            for c in range(COLS_DEV):
                slot[m, c] = -1
            for l in range(inner_slots):
                slot[m, cols[p][m, l] - first] = l
        for i in range(rows):
            for m in range(inner_rows):
                for j in range(slots):
                    l = slot[m, wanted[i, j] - first]
                    tile = tiles[p][m, jnp.maximum(l, 0)]
                    right[i, m * block : (m + 1) * block, j * block : (j + 1) * block] = jnp.where(
                        l >= 0, tile, jnp.zeros_like(tile)
                    )
        for i in range(rows):
            left = jnp.concatenate(
                [dense[i, place[1 + p] * inner_rows + m] for m in range(inner_rows)], axis=1
            )
            product = jnp.dot(left, right[i], preferred_element_type=jnp.float32)
            sums[i] = product if sums[i] is None else sums[i] + product
    for i in range(rows):
        if last:
            for j in range(slots):
                out[i, j] = sums[i][:, j * block : (j + 1) * block].astype(out.dtype)
        else:
            out[i] = sums[i]


def body(row_count, col_count, a_tiles, a_cols, b_tiles, b_cols, c_cols):
    rows, slots = c_cols.shape
    inner_rows = b_tiles.shape[0]
    block = a_tiles.shape[-1]
    dtype = b_tiles.dtype
    r = lax.axis_index("row")
    first = lax.axis_index("col") * COLS_DEV

    def swap(x, axis, n, d):
        return lax.ppermute(x, axis, [(k, k ^ d) for k in range(n)])

    def spans(n):
        while n > 1:
            yield n - 1
            n //= 2

    def pack(index, tiles):
        size = index.size * block
        return pl.pallas_call(
            pack_kernel,
            out_shape=jax.ShapeDtypeStruct((size + tail(index.size), block), dtype),
            in_specs=[SMEM, VMEM],
            out_specs=VMEM,
            compiler_params=PARAMS,
        )(index, tiles.reshape(size, block))

    dists, cols, tiles = [0], [b_cols], [b_tiles]
    a_parts = [pack(a_cols, a_tiles)]
    col_spans = [col_count >> k for k in range(1, col_count.bit_length())]
    for stage, d in enumerate(spans(row_count)):
        if stage == 1:
            tiles.append(swap(b_tiles, "row", row_count, d))
            cols.append(swap(b_cols, "row", row_count, d))
            a_parts.append(swap(a_parts[0], "col", col_count, col_spans[0]))
            cols, tiles, a_parts = lax.optimization_barrier((cols, tiles, a_parts))
            far_tiles, far_cols = tiles[1:2], cols[1:2]
        else:
            far_tiles, far_cols = tiles, cols
        dists = dists + [e ^ d for e in dists]
        tiles = tiles + [swap(x, "row", row_count, d) for x in far_tiles]
        cols = cols + [swap(x, "row", row_count, d) for x in far_cols]
    for d in col_spans[len(a_parts) - 1 :]:
        a_parts = a_parts + [swap(x, "col", col_count, d) for x in a_parts]
    shards = list(zip(dists, cols, tiles))

    size = a_cols.size * block
    a_index = jnp.stack([x[size:, 0][: a_cols.size] for x in a_parts]).astype(jnp.int32)
    dense = pl.pallas_call(
        left_kernel,
        out_shape=jax.ShapeDtypeStruct((rows, inner_rows * row_count, block, block), dtype),
        in_specs=[SMEM] + [VMEM] * col_count,
        out_specs=VMEM,
        compiler_params=PARAMS,
    )(a_index, *a_parts)

    def step(pieces, before, last):
        parts = len(pieces)
        place = jnp.stack([first] + [r ^ d for d, _, _ in pieces]).astype(jnp.int32)
        if last:
            out = jax.ShapeDtypeStruct((rows, slots, block, block), dtype)
        else:
            out = jax.ShapeDtypeStruct((rows, block, slots * block), jnp.float32)
        held = [dense] if before is None else [dense, before]
        return pl.pallas_call(
            functools.partial(step_kernel, parts, last),
            out_shape=out,
            in_specs=[SMEM] * (2 + parts) + [VMEM] * (parts + len(held)),
            out_specs=VMEM,
            scratch_shapes=[
                pltpu.VMEM((rows, inner_rows * block, slots * block), dtype),
                pltpu.SMEM((inner_rows, COLS_DEV), jnp.int32),
            ],
            compiler_params=PARAMS,
            cost_estimate=pl.CostEstimate(
                flops=2 * rows * parts * inner_rows * slots * block**3, bytes_accessed=2**21, transcendentals=0
            ),
        )(place, c_cols, *[c for _, c, _ in pieces], *[x for _, _, x in pieces], *held)

    total = None
    for p in range(0, row_count - 1, 3):
        total = step(shards[p : min(p + 3, row_count - 1)], total, False)
    return step(shards[-1:], total, True)


def solution(mesh):
    return jax.shard_map(
        functools.partial(body, mesh.shape["row"], mesh.shape["col"]),
        mesh=mesh,
        in_specs=(
            P(("groups", "row"), "col", None, None),
            P(("groups", "row"), "col"),
            P(("groups", "row"), "col", None, None),
            P(("groups", "row"), "col"),
            P(("groups", "row"), "col"),
        ),
        out_specs=P(("groups", "row"), "col", None, None),
        check_vma=False,
    )
```

```python
import functools

import jax
import jax.numpy as jnp
from jax import lax
from jax.experimental import pallas as pl
from jax.experimental.pallas import tpu as pltpu
from jax.sharding import PartitionSpec as P

COLS_DEV = 16

SMEM = pl.BlockSpec(memory_space=pltpu.SMEM)
VMEM = pl.BlockSpec(memory_space=pltpu.VMEM)
PARAMS = pltpu.CompilerParams(vmem_limit_bytes=32 * 2**20)


def pack_kernel(*refs):
    indices, tiles, out = refs[:-2], refs[-2], refs[-1]
    size = tiles.shape[0]
    out[:size, :] = tiles[...]
    row = lax.broadcasted_iota(jnp.int32, (out.shape[0] - size, out.shape[1]), 0)
    found = jnp.zeros(row.shape, jnp.float32)
    at = 0
    for index in indices:
        for i in range(index.shape[0]):
            for k in range(index.shape[1]):
                found = jnp.where(row == at, index[i, k].astype(jnp.float32), found)
                at += 1
    out[size:, :] = found.astype(out.dtype)


def left_kernel(slots, index, *refs):
    parts, dense = refs[:-1], refs[-1]
    dense[...] = jnp.zeros_like(dense)
    rows, _, block, _ = dense.shape
    for p, part in enumerate(parts):
        for i in range(rows):
            for s in range(slots):
                inner = index[p, i * slots + s]
                start = (i * slots + s) * block

                @pl.when(inner >= 0)
                def _():
                    dense[i, inner] = part[start : start + block, :]


def step_kernel(parts, groups, starts, slots, last, place, *refs):
    wanted, refs = refs[:groups], refs[groups:]
    cols, refs = refs[:parts], refs[parts:]
    tiles, refs = refs[:parts], refs[parts:]
    dense, refs = refs[:groups], refs[groups:]
    before, refs = (refs[:groups], refs[groups:]) if len(refs) > groups + 2 else ([None] * groups, refs)
    outs, right, slot = refs[:groups], refs[groups], refs[groups + 1]
    first = place[0]
    rows = dense[0].shape[0]
    inner_rows, inner_slots, block, _ = tiles[0].shape

    def read(ref, start, i, k, width):
        return ref[i, k] if start is None else ref[0, start + i * width + k]

    sums = [[None if total is None else total[i] for i in range(rows)] for total in before]
    for p in range(parts):
        for m in range(inner_rows):
            for c in range(COLS_DEV):
                slot[m, c] = -1
            for l in range(inner_slots):
                slot[m, read(cols[p], starts[groups + p], m, l, inner_slots) - first] = l
        for g in range(groups):
            for i in range(rows):
                for j in range(slots):
                    column = read(wanted[g], starts[g], i, j, slots) - first
                    for m in range(inner_rows):
                        l = slot[m, column]
                        tile = tiles[p][m, jnp.maximum(l, 0)]
                        right[g, i, m * block : (m + 1) * block, j * block : (j + 1) * block] = jnp.where(
                            l >= 0, tile, jnp.zeros_like(tile)
                        )
            for i in range(rows):
                left = jnp.concatenate(
                    [dense[g][i, place[1 + p] * inner_rows + m] for m in range(inner_rows)], axis=1
                )
                product = jnp.dot(left, right[g, i], preferred_element_type=jnp.float32)
                sums[g][i] = product if sums[g][i] is None else sums[g][i] + product
    for g in range(groups):
        for i in range(rows):
            if last:
                for j in range(slots):
                    outs[g][i, j] = sums[g][i][:, j * block : (j + 1) * block].astype(outs[g].dtype)
            else:
                outs[g][i] = sums[g][i]


def parity(k):
    return bin(k).count("1") % 2


def body(row_count, col_count, a_tiles, a_cols, b_tiles, b_cols, c_cols):
    rows, slots = c_cols.shape
    inner_rows = b_tiles.shape[0]
    block = a_tiles.shape[-1]
    dtype = b_tiles.dtype
    r, q = lax.axis_index("row"), lax.axis_index("col")
    first = q * COLS_DEV
    bits = sum((r >> k) & 1 for k in range(row_count.bit_length()))
    working = (bits + q) % 2 == 0

    def works(k, c):
        return parity(k) == c % 2

    def swap(x, axis, n, d):
        return lax.ppermute(x, axis, [(k, k ^ d) for k in range(n)])

    def permute(x, target):
        pairs = []
        for k in range(row_count):
            for c in range(col_count):
                to, at = target(k, c)
                pairs.append((k * col_count + c, to * col_count + at))
        return lax.ppermute(x, ("row", "col"), pairs)

    def deliver(x, d):
        def target(k, c):
            if parity(d):
                return (k, c ^ 1) if works(k, c) else (k ^ d, c)
            return (k ^ d, c) if works(k, c) else (k, c ^ (col_count // 2))

        return permute(x, target)

    def give_back(x):
        return permute(x, lambda k, c: (k ^ 1, c) if works(k, c) else (k, c ^ 1))

    size = a_cols.size * block
    count = a_cols.size + c_cols.size + b_cols.size
    own = pl.pallas_call(
        pack_kernel,
        out_shape=jax.ShapeDtypeStruct((size + -(-count // 16) * 16, block), dtype),
        in_specs=[SMEM] * 3 + [VMEM],
        out_specs=VMEM,
        compiler_params=PARAMS,
    )(a_cols, c_cols, b_cols, a_tiles.reshape(size, block))
    c_start, b_start = a_cols.size, a_cols.size + c_cols.size

    shards = {d: deliver(b_tiles, d) for d in range(row_count - 1, 1, -1)}
    other = swap(own, "row", row_count, 1)
    shards[1] = deliver(lax.optimization_barrier((b_tiles, own))[0], 1)

    def across(x):
        parts, d = [x], col_count // 2
        while d:
            parts = parts + [swap(part, "col", col_count, d) for part in parts]
            d //= 2
        return parts

    def index_of(packs):
        return jnp.stack([x[size:, 0] for x in packs]).astype(jnp.int32)

    def dense_of(packs):
        return pl.pallas_call(
            functools.partial(left_kernel, a_cols.shape[1]),
            out_shape=jax.ShapeDtypeStruct((rows, inner_rows * row_count, block, block), dtype),
            in_specs=[SMEM] + [VMEM] * len(packs),
            out_specs=VMEM,
            compiler_params=PARAMS,
        )(index_of(packs), *packs)

    own_packs, other_packs = across(own), across(other)
    own_dense, other_dense = dense_of(own_packs), dense_of(other_packs)
    behind = index_of([other])
    late_cols = lax.optimization_barrier((b_cols, other_packs))[0]
    cols = {0: (None, b_cols), 1: (b_start, behind)}
    for d in range(row_count - 1, 1, -1):
        cols[d] = (None, swap(late_cols, "row", row_count, d))
    shards[0] = b_tiles
    own_rows, other_rows = (None, c_cols, own_dense), (c_start, behind, other_dense)

    def step(dists, groups, before, last):
        place = jnp.stack([first] + [r ^ d for d in dists]).astype(jnp.int32)
        parts, count = len(dists), len(groups)
        if last:
            out = jax.ShapeDtypeStruct((rows, slots, block, block), dtype)
        else:
            out = jax.ShapeDtypeStruct((rows, block, slots * block), jnp.float32)
        starts = [start for start, _, _ in groups] + [cols[d][0] for d in dists]
        return pl.pallas_call(
            functools.partial(step_kernel, parts, count, starts, slots, last),
            out_shape=[out] * count,
            in_specs=[SMEM] * (1 + count + parts) + [VMEM] * (parts + count + len(before)),
            out_specs=[VMEM] * count,
            scratch_shapes=[
                pltpu.VMEM((count, rows, inner_rows * block, slots * block), dtype),
                pltpu.SMEM((inner_rows, COLS_DEV), jnp.int32),
            ],
            compiler_params=PARAMS,
            cost_estimate=pl.CostEstimate(
                flops=2 * count * rows * parts * inner_rows * slots * block**3,
                bytes_accessed=2**21,
                transcendentals=0,
            ),
        )(
            place,
            *[x for _, x, _ in groups],
            *[cols[d][1] for d in dists],
            *[shards[d] for d in dists],
            *[x for _, _, x in groups],
            *before,
        )

    order = [0, 1] + list(range(2, row_count))
    totals = step(order[:2], [own_rows, other_rows], [], False)
    for at in range(2, row_count - 2, 2):
        totals = step(order[at : at + 2], [own_rows, other_rows], totals, False)
    final = order[-2:] if row_count > 2 else []
    (given,) = step(final, [other_rows], totals[1:], True)
    given = give_back(given)
    (kept,) = step(final, [own_rows], totals[:1], True)
    return jnp.where(working, kept, given)


def solution(mesh):
    return jax.shard_map(
        functools.partial(body, mesh.shape["row"], mesh.shape["col"]),
        mesh=mesh,
        in_specs=(
            P(("groups", "row"), "col", None, None),
            P(("groups", "row"), "col"),
            P(("groups", "row"), "col", None, None),
            P(("groups", "row"), "col"),
            P(("groups", "row"), "col"),
        ),
        out_specs=P(("groups", "row"), "col", None, None),
        check_vma=False,
    )
```

```python
import functools

import jax
import jax.numpy as jnp
from jax import lax
from jax.experimental import pallas as pl
from jax.experimental.pallas import tpu as pltpu
from jax.sharding import PartitionSpec as P

COLS_DEV = 16

SMEM = pl.BlockSpec(memory_space=pltpu.SMEM)
VMEM = pl.BlockSpec(memory_space=pltpu.VMEM)
PARAMS = pltpu.CompilerParams(vmem_limit_bytes=32 * 2**20)


def pack_kernel(*refs):
    indices, tiles, out = refs[:-2], refs[-2], refs[-1]
    size = tiles.shape[0]
    out[:size, :] = tiles[...]
    row = lax.broadcasted_iota(jnp.int32, (out.shape[0] - size, out.shape[1]), 0)
    found = jnp.zeros(row.shape, jnp.float32)
    at = 0
    for index in indices:
        for i in range(index.shape[0]):
            for k in range(index.shape[1]):
                found = jnp.where(row == at, index[i, k].astype(jnp.float32), found)
                at += 1
    out[size:, :] = found.astype(out.dtype)


def left_kernel(slots, index, *refs):
    parts, dense = refs[:-1], refs[-1]
    dense[...] = jnp.zeros_like(dense)
    rows, _, block, _ = dense.shape
    for p, part in enumerate(parts):
        for i in range(rows):
            for s in range(slots):
                inner = index[p, i * slots + s]
                start = (i * slots + s) * block

                @pl.when(inner >= 0)
                def _():
                    dense[i, inner] = part[start : start + block, :]


def step_kernel(parts, groups, starts, slots, last, place, *refs):
    wanted, refs = refs[:groups], refs[groups:]
    cols, refs = refs[:parts], refs[parts:]
    tiles, refs = refs[:parts], refs[parts:]
    dense, refs = refs[:groups], refs[groups:]
    before, refs = (refs[:groups], refs[groups:]) if len(refs) > groups + 2 else ([None] * groups, refs)
    outs, right, slot = refs[:groups], refs[groups], refs[groups + 1]
    first = place[0]
    rows = dense[0].shape[0]
    inner_rows, inner_slots, block, _ = tiles[0].shape

    def read(ref, start, i, k, width):
        return ref[i, k] if start is None else ref[0, start + i * width + k]

    sums = [[None if total is None else total[i] for i in range(rows)] for total in before]
    for p in range(parts):
        for m in range(inner_rows):
            for c in range(COLS_DEV):
                slot[m, c] = -1
            for l in range(inner_slots):
                slot[m, read(cols[p], starts[groups + p], m, l, inner_slots) - first] = l
        for g in range(groups):
            for i in range(rows):
                for j in range(slots):
                    column = read(wanted[g], starts[g], i, j, slots) - first
                    for m in range(inner_rows):
                        l = slot[m, column]
                        tile = tiles[p][m, jnp.maximum(l, 0)]
                        right[g, i, m * block : (m + 1) * block, j * block : (j + 1) * block] = jnp.where(
                            l >= 0, tile, jnp.zeros_like(tile)
                        )
            for i in range(rows):
                left = jnp.concatenate(
                    [dense[g][i, place[1 + p] * inner_rows + m] for m in range(inner_rows)], axis=1
                )
                product = jnp.dot(left, right[g, i], preferred_element_type=jnp.float32)
                sums[g][i] = product if sums[g][i] is None else sums[g][i] + product
    for g in range(groups):
        for i in range(rows):
            if last:
                for j in range(slots):
                    outs[g][i, j] = sums[g][i][:, j * block : (j + 1) * block].astype(outs[g].dtype)
            else:
                outs[g][i] = sums[g][i]


def parity(k):
    return bin(k).count("1") % 2


def body(row_count, col_count, a_tiles, a_cols, b_tiles, b_cols, c_cols):
    rows, slots = c_cols.shape
    inner_rows = b_tiles.shape[0]
    block = a_tiles.shape[-1]
    dtype = b_tiles.dtype
    r, q = lax.axis_index("row"), lax.axis_index("col")
    first = q * COLS_DEV
    bits = sum((r >> k) & 1 for k in range(row_count.bit_length()))
    working = (bits + q) % 2 == 0

    def works(k, c):
        return parity(k) == c % 2

    def swap(x, axis, n, d):
        return lax.ppermute(x, axis, [(k, k ^ d) for k in range(n)])

    def permute(x, target):
        pairs = []
        for k in range(row_count):
            for c in range(col_count):
                to, at = target(k, c)
                pairs.append((k * col_count + c, to * col_count + at))
        return lax.ppermute(x, ("row", "col"), pairs)

    def deliver(x, d):
        def target(k, c):
            if parity(d):
                return (k, c ^ 1) if works(k, c) else (k ^ d, c)
            return (k ^ d, c) if works(k, c) else (k, c ^ (col_count // 2))

        return permute(x, target)

    def give_back(x):
        return permute(x, lambda k, c: (k ^ 1, c) if works(k, c) else (k, c ^ 1))

    size = a_cols.size * block
    count = a_cols.size + c_cols.size + b_cols.size
    own = pl.pallas_call(
        pack_kernel,
        out_shape=jax.ShapeDtypeStruct((size + -(-count // 16) * 16, block), dtype),
        in_specs=[SMEM] * 3 + [VMEM],
        out_specs=VMEM,
        compiler_params=PARAMS,
    )(a_cols, c_cols, b_cols, a_tiles.reshape(size, block))
    c_start, b_start = a_cols.size, a_cols.size + c_cols.size

    def across(parts, d):
        while d:
            parts = parts + [swap(part, "col", col_count, d) for part in parts]
            d //= 2
        return parts

    far = col_count // 2
    shards = {0: b_tiles, row_count - 1: deliver(b_tiles, row_count - 1)}
    cols = {0: (None, b_cols)}
    for d in range(row_count - 1, 1, -1):
        cols[d] = (None, swap(b_cols, "row", row_count, d))
    own_packs = [own, swap(own, "col", col_count, far)]
    other = swap(own, "row", row_count, 1)
    next_tiles = lax.optimization_barrier((b_tiles, own_packs[1]))[0]
    for d in range(row_count - 2, 1, -1):
        shards[d] = deliver(next_tiles, d)
    last_tiles, other, _, _ = lax.optimization_barrier((b_tiles, other, shards[row_count - 1], cols))
    shards[1] = deliver(last_tiles, 1)
    own_packs = across(own_packs, far // 2)
    other_packs = across([other], far)

    def index_of(packs):
        return jnp.stack([x[size:, 0] for x in packs]).astype(jnp.int32)

    def dense_of(packs):
        return pl.pallas_call(
            functools.partial(left_kernel, a_cols.shape[1]),
            out_shape=jax.ShapeDtypeStruct((rows, inner_rows * row_count, block, block), dtype),
            in_specs=[SMEM] + [VMEM] * len(packs),
            out_specs=VMEM,
            compiler_params=PARAMS,
        )(index_of(packs), *packs)

    own_dense, other_dense = dense_of(own_packs), dense_of(other_packs)
    behind = index_of([other])
    cols[1] = (b_start, behind)
    own_rows, other_rows = (None, c_cols, own_dense), (c_start, behind, other_dense)

    def step(dists, groups, before, last):
        place = jnp.stack([first] + [r ^ d for d in dists]).astype(jnp.int32)
        parts, count = len(dists), len(groups)
        if last:
            out = jax.ShapeDtypeStruct((rows, slots, block, block), dtype)
        else:
            out = jax.ShapeDtypeStruct((rows, block, slots * block), jnp.float32)
        starts = [start for start, _, _ in groups] + [cols[d][0] for d in dists]
        return pl.pallas_call(
            functools.partial(step_kernel, parts, count, starts, slots, last),
            out_shape=[out] * count,
            in_specs=[SMEM] * (1 + count + parts) + [VMEM] * (parts + count + len(before)),
            out_specs=[VMEM] * count,
            scratch_shapes=[
                pltpu.VMEM((count, rows, inner_rows * block, slots * block), dtype),
                pltpu.SMEM((inner_rows, COLS_DEV), jnp.int32),
            ],
            compiler_params=PARAMS,
            cost_estimate=pl.CostEstimate(
                flops=2 * count * rows * parts * inner_rows * slots * block**3,
                bytes_accessed=2**21,
                transcendentals=0,
            ),
        )(
            place,
            *[x for _, x, _ in groups],
            *[cols[d][1] for d in dists],
            *[shards[d] for d in dists],
            *[x for _, _, x in groups],
            *before,
        )

    def products(group):
        order, totals = [0] + list(range(row_count - 1, 0, -1)), []
        for at in range(0, row_count, 2):
            totals = step(order[at : at + 2], [group], totals, at + 2 >= row_count)
        return totals[0]

    given = give_back(products(other_rows))
    kept = products(own_rows)
    return jnp.where(working, kept, given)


def solution(mesh):
    return jax.shard_map(
        functools.partial(body, mesh.shape["row"], mesh.shape["col"]),
        mesh=mesh,
        in_specs=(
            P(("groups", "row"), "col", None, None),
            P(("groups", "row"), "col"),
            P(("groups", "row"), "col", None, None),
            P(("groups", "row"), "col"),
            P(("groups", "row"), "col"),
        ),
        out_specs=P(("groups", "row"), "col", None, None),
        check_vma=False,
    )
```

```python
import functools

import jax
import jax.numpy as jnp
from jax import lax
from jax.experimental import pallas as pl
from jax.experimental.pallas import tpu as pltpu
from jax.sharding import PartitionSpec as P

COLS_DEV = 16

SMEM = pl.BlockSpec(memory_space=pltpu.SMEM)
VMEM = pl.BlockSpec(memory_space=pltpu.VMEM)
PARAMS = pltpu.CompilerParams(vmem_limit_bytes=32 * 2**20)
FREE = pl.CostEstimate(flops=1, bytes_accessed=1, transcendentals=0)


def pack_kernel(*refs):
    indices, tiles, out = refs[:-2], refs[-2], refs[-1]
    size = tiles.shape[0]
    out[:size, :] = tiles[...]
    row = lax.broadcasted_iota(jnp.int32, (out.shape[0] - size, out.shape[1]), 0)
    found = jnp.zeros(row.shape, jnp.float32)
    at = 0
    for index in indices:
        for i in range(index.shape[0]):
            for k in range(index.shape[1]):
                found = jnp.where(row == at, index[i, k].astype(jnp.float32), found)
                at += 1
    out[size:, :] = found.astype(out.dtype)


def left_kernel(slots, index, *refs):
    parts, dense = refs[:-1], refs[-1]
    dense[...] = jnp.zeros_like(dense)
    rows, _, block, _ = dense.shape
    for p, part in enumerate(parts):
        for i in range(rows):
            for s in range(slots):
                inner = index[p, i * slots + s]
                start = (i * slots + s) * block

                @pl.when(inner >= 0)
                def _():
                    dense[i, inner] = part[start : start + block, :]


def step_kernel(starts, span, last, place, *refs):
    parts = len(starts) - 1
    wanted, refs = refs[0], refs[1:]
    cols, refs = refs[:parts], refs[parts:]
    tiles, refs = refs[:parts], refs[parts:]
    dense, refs = refs[0], refs[1:]
    before, out, right, slot = refs if len(refs) == 4 else (None,) + refs
    @pl.when(place[0] >= 0)
    def _():
        first = place[0]
        inner_rows = slot.shape[0]
        block = dense.shape[-1]
        slots = right.shape[2] // block
        inner_slots = tiles[0].shape[0] // block // inner_rows

        def read(ref, start, i, k, width):
            return ref[i, k] if start is None else ref[0, start + i * width + k]

        sums = {i: None if before is None else before[i] for i in span}
        for p in range(parts):
            for m in range(inner_rows):
                for c in range(COLS_DEV):
                    slot[m, c] = -1
                for l in range(inner_slots):
                    slot[m, read(cols[p], starts[1 + p], m, l, inner_slots) - first] = l
            for i in span:
                for j in range(slots):
                    column = read(wanted, starts[0], i, j, slots) - first
                    for m in range(inner_rows):
                        l = slot[m, column]
                        start = pl.multiple_of((m * inner_slots + jnp.maximum(l, 0)) * block, block)
                        tile = tiles[p][pl.ds(start, block), :]
                        right[i, m * block : (m + 1) * block, j * block : (j + 1) * block] = jnp.where(
                            l >= 0, tile, jnp.zeros_like(tile)
                        )
            for i in span:
                left = jnp.concatenate(
                    [dense[i, place[1 + p] * inner_rows + m] for m in range(inner_rows)], axis=1
                )
                product = jnp.dot(left, right[i], preferred_element_type=jnp.float32)
                sums[i] = product if sums[i] is None else sums[i] + product
        for at, i in enumerate(span):
            if last:
                for j in range(slots):
                    out[at, j] = sums[i][:, j * block : (j + 1) * block].astype(out.dtype)
            else:
                out[i] = sums[i]


def parity(k):
    return bin(k).count("1") % 2


def body(row_count, col_count, a_tiles, a_cols, b_tiles, b_cols, c_cols):
    rows, slots = c_cols.shape
    inner_rows = b_tiles.shape[0]
    block = a_tiles.shape[-1]
    dtype = b_tiles.dtype
    r, q = lax.axis_index("row"), lax.axis_index("col")
    first = q * COLS_DEV
    bits = sum((r >> k) & 1 for k in range(row_count.bit_length()))
    working = (bits + q) % 2 == 0

    def works(k, c):
        return parity(k) == c % 2

    def swap(x, axis, n, d):
        return lax.ppermute(x, axis, [(k, k ^ d) for k in range(n)])

    def permute(x, target):
        pairs = []
        for k in range(row_count):
            for c in range(col_count):
                to, at = target(k, c)
                pairs.append((k * col_count + c, to * col_count + at))
        return lax.ppermute(x, ("row", "col"), pairs)

    def deliver(x, d):
        def target(k, c):
            if parity(d):
                return (k, c ^ 1) if works(k, c) else (k ^ d, c)
            return (k ^ d, c) if works(k, c) else (k, c ^ (col_count // 2))

        return permute(x, target)

    def give_back(x):
        return permute(x, lambda k, c: (k ^ 1, c) if works(k, c) else (k, c ^ 1))

    def pack(tiles, *indices):
        size = tiles.size // block
        count = sum(x.size for x in indices)
        return pl.pallas_call(
            pack_kernel,
            out_shape=jax.ShapeDtypeStruct((size + -(-count // 16) * 16, block), dtype),
            in_specs=[SMEM] * len(indices) + [VMEM],
            out_specs=VMEM,
            compiler_params=PARAMS,
            cost_estimate=FREE,
        )(*indices, tiles.reshape(size, block))

    def index_of(packs, tiles):
        return jnp.stack([x[tiles.size // block :, 0] for x in packs]).astype(jnp.int32)

    def across(parts, d):
        while d:
            parts = parts + [swap(part, "col", col_count, d) for part in parts]
            d //= 2
        return parts

    far, end = col_count // 2, row_count - 1
    flat = b_tiles.reshape(-1, block)
    own, packed = pack(a_tiles, a_cols, c_cols), pack(b_tiles, b_cols)
    shards = {0: flat, end: deliver(flat, end)}
    cols = {0: (None, b_cols), end: (None, swap(b_cols, "row", row_count, end))}
    own_packs = [own, swap(own, "col", col_count, far)]
    other = swap(own, "row", row_count, 1)
    ready = lax.optimization_barrier((packed, own_packs[1]))[0]
    for d in range(end - 1, 1, -1):
        shards[d] = deliver(ready, d)
    ready, other, _, _ = lax.optimization_barrier((packed, other, shards[end], cols[end][1]))
    shards[1] = deliver(ready, 1)
    own_packs, other_packs = across(own_packs, far // 2), across([other], far)
    def dense_of(packs):
        return pl.pallas_call(
            functools.partial(left_kernel, a_cols.shape[1]),
            out_shape=jax.ShapeDtypeStruct((rows, inner_rows * row_count, block, block), dtype),
            in_specs=[SMEM] + [VMEM] * len(packs),
            out_specs=VMEM,
            compiler_params=PARAMS,
            cost_estimate=FREE,
        )(index_of(packs, a_tiles), *packs)

    def step(dists, wanted, dense, before, span, last):
        place = jnp.stack([jnp.where(working, first, -1)] + [r ^ d for d in dists]).astype(jnp.int32)
        if last:
            out = jax.ShapeDtypeStruct((len(span), slots, block, block), dtype)
        else:
            out = jax.ShapeDtypeStruct((rows, block, slots * block), jnp.float32)
        held = [dense] if before is None else [dense, before]
        return pl.pallas_call(
            functools.partial(step_kernel, [wanted[0]] + [cols[d][0] for d in dists], span, last),
            out_shape=out,
            in_specs=[SMEM] * (2 + len(dists)) + [VMEM] * (len(dists) + len(held)),
            out_specs=VMEM,
            scratch_shapes=[
                pltpu.VMEM((rows, inner_rows * block, slots * block), dtype),
                pltpu.SMEM((inner_rows, COLS_DEV), jnp.int32),
            ],
            compiler_params=PARAMS,
            cost_estimate=FREE,
        )(place, wanted[1], *[cols[d][1] for d in dists], *[shards[d] for d in dists], *held)

    order, every = list(range(1, end)) + [0, end], list(range(rows))
    early, late = order[:-4], order[-4:]
    for d in range(1, end):
        cols[d] = (0, index_of([shards[d]], b_tiles))

    def products(wanted, packs, spans):
        dense, total = dense_of(packs), None
        for at in range(0, len(early), 4):
            total = step(early[at : at + 4], wanted, dense, total, every, False)
        return [step(late, wanted, dense, total, span, True) for span in spans]

    given = products((a_cols.size, index_of([other], a_tiles)), other_packs, [[i] for i in every])
    given = [give_back(x) for x in given]
    (kept,) = products((None, c_cols), own_packs, [every])
    return jnp.where(working, kept, jnp.concatenate(given, axis=0))


def solution(mesh):
    return jax.shard_map(
        functools.partial(body, mesh.shape["row"], mesh.shape["col"]),
        mesh=mesh,
        in_specs=(
            P(("groups", "row"), "col", None, None),
            P(("groups", "row"), "col"),
            P(("groups", "row"), "col", None, None),
            P(("groups", "row"), "col"),
            P(("groups", "row"), "col"),
        ),
        out_specs=P(("groups", "row"), "col", None, None),
        check_vma=False,
    )
```

```python
import functools

import jax
import jax.numpy as jnp
from jax import lax
from jax.experimental import pallas as pl
from jax.experimental.pallas import tpu as pltpu
from jax.sharding import PartitionSpec as P

COLS_DEV = 16

SMEM = pl.BlockSpec(memory_space=pltpu.SMEM)
VMEM = pl.BlockSpec(memory_space=pltpu.VMEM)
PARAMS = pltpu.CompilerParams(vmem_limit_bytes=32 * 2**20)
FREE = pl.CostEstimate(flops=1, bytes_accessed=1, transcendentals=0)


def pack_kernel(*refs):
    indices, tiles, out = refs[:-2], refs[-2], refs[-1]
    size = tiles.shape[0]
    out[:size, :] = tiles[...]
    row = lax.broadcasted_iota(jnp.int32, (out.shape[0] - size, out.shape[1]), 0)
    found = jnp.zeros(row.shape, jnp.float32)
    at = 0
    for index in indices:
        for i in range(index.shape[0]):
            for k in range(index.shape[1]):
                found = jnp.where(row == at, index[i, k].astype(jnp.float32), found)
                at += 1
    out[size:, :] = found.astype(out.dtype)


def left_kernel(slots, index, *refs):
    parts, dense = refs[:-1], refs[-1]
    dense[...] = jnp.zeros_like(dense)
    rows, _, block, _ = dense.shape
    for p, part in enumerate(parts):
        for i in range(rows):
            for s in range(slots):
                inner = index[p, i * slots + s]
                start = (i * slots + s) * block

                @pl.when(inner >= 0)
                def _():
                    dense[i, inner] = part[start : start + block, :]


def step_kernel(starts, span, last, place, *refs):
    parts = len(starts) - 1
    wanted, refs = refs[0], refs[1:]
    cols, refs = refs[:parts], refs[parts:]
    tiles, refs = refs[:parts], refs[parts:]
    dense, refs = refs[0], refs[1:]
    before, out, right, slot = refs if len(refs) == 4 else (None,) + refs
    @pl.when(place[0] >= 0)
    def _():
        first = place[0]
        inner_rows = slot.shape[0]
        block = dense.shape[-1]
        slots = right.shape[2] // block
        inner_slots = tiles[0].shape[0] // block // inner_rows

        def read(ref, start, i, k, width):
            return ref[i, k] if start is None else ref[0, start + i * width + k]

        sums = {i: None if before is None else before[i] for i in span}
        for p in range(parts):
            for m in range(inner_rows):
                for c in range(COLS_DEV):
                    slot[m, c] = -1
                for l in range(inner_slots):
                    slot[m, read(cols[p], starts[1 + p], m, l, inner_slots) - first] = l
            for i in span:
                for j in range(slots):
                    column = read(wanted, starts[0], i, j, slots) - first
                    for m in range(inner_rows):
                        l = slot[m, column]
                        start = pl.multiple_of((m * inner_slots + jnp.maximum(l, 0)) * block, block)
                        tile = tiles[p][pl.ds(start, block), :]
                        right[i, m * block : (m + 1) * block, j * block : (j + 1) * block] = jnp.where(
                            l >= 0, tile, jnp.zeros_like(tile)
                        )
            for i in span:
                left = jnp.concatenate(
                    [dense[i, place[1 + p] * inner_rows + m] for m in range(inner_rows)], axis=1
                )
                product = jnp.dot(left, right[i], preferred_element_type=jnp.float32)
                sums[i] = product if sums[i] is None else sums[i] + product
        for at, i in enumerate(span):
            if last:
                for j in range(slots):
                    out[at, j] = sums[i][:, j * block : (j + 1) * block].astype(out.dtype)
            else:
                out[i] = sums[i]


def parity(k):
    return bin(k).count("1") % 2


def body(row_count, col_count, a_tiles, a_cols, b_tiles, b_cols, c_cols):
    rows, slots = c_cols.shape
    inner_rows = b_tiles.shape[0]
    block = a_tiles.shape[-1]
    dtype = b_tiles.dtype
    r, q = lax.axis_index("row"), lax.axis_index("col")
    first = q * COLS_DEV
    bits = sum((r >> k) & 1 for k in range(row_count.bit_length()))
    working = (bits + q) % 2 == 0

    def works(k, c):
        return parity(k) == c % 2

    def swap(x, axis, n, d):
        return lax.ppermute(x, axis, [(k, k ^ d) for k in range(n)])

    def permute(x, target):
        pairs = []
        for k in range(row_count):
            for c in range(col_count):
                to, at = target(k, c)
                pairs.append((k * col_count + c, to * col_count + at))
        return lax.ppermute(x, ("row", "col"), pairs)

    def deliver(x, d):
        def target(k, c):
            if parity(d):
                return (k, c ^ 1) if works(k, c) else (k ^ d, c)
            return (k ^ d, c) if works(k, c) else (k, c ^ (col_count // 2))

        return permute(x, target)

    def give_back(x):
        return permute(x, lambda k, c: (k ^ 1, c) if works(k, c) else (k, c ^ 1))

    def pack(tiles, *indices):
        size = tiles.size // block
        count = sum(x.size for x in indices)
        return pl.pallas_call(
            pack_kernel,
            out_shape=jax.ShapeDtypeStruct((size + -(-count // 16) * 16, block), dtype),
            in_specs=[SMEM] * len(indices) + [VMEM],
            out_specs=VMEM,
            compiler_params=PARAMS,
            cost_estimate=FREE,
        )(*indices, tiles.reshape(size, block))

    def index_of(packs, tiles):
        return jnp.stack([x[tiles.size // block :, 0] for x in packs]).astype(jnp.int32)

    def across(parts, d):
        while d:
            parts = parts + [swap(part, "col", col_count, d) for part in parts]
            d //= 2
        return parts

    far, end = col_count // 2, row_count - 1
    flat = b_tiles.reshape(-1, block)
    own, packed = pack(a_tiles, a_cols, c_cols), pack(b_tiles, b_cols)
    shards = {0: flat, end: deliver(flat, end)}
    cols = {0: (None, b_cols), end: (None, swap(b_cols, "row", row_count, end))}
    own_packs = [own, swap(own, "col", col_count, far)]
    other = swap(own, "row", row_count, 1)
    ready = lax.optimization_barrier((packed, own_packs[1]))[0]
    for d in range(end - 1, 0, -1):
        shards[d] = deliver(ready, d)
    other = lax.optimization_barrier((other, shards[end]))[0]
    own_packs, other_packs = across(own_packs, far // 2), across([other], far)
    def dense_of(packs):
        return pl.pallas_call(
            functools.partial(left_kernel, a_cols.shape[1]),
            out_shape=jax.ShapeDtypeStruct((rows, inner_rows * row_count, block, block), dtype),
            in_specs=[SMEM] + [VMEM] * len(packs),
            out_specs=VMEM,
            compiler_params=PARAMS,
            cost_estimate=FREE,
        )(index_of(packs, a_tiles), *packs)

    def step(dists, wanted, dense, before, span, last):
        place = jnp.stack([jnp.where(working, first, -1)] + [r ^ d for d in dists]).astype(jnp.int32)
        if last:
            out = jax.ShapeDtypeStruct((len(span), slots, block, block), dtype)
        else:
            out = jax.ShapeDtypeStruct((rows, block, slots * block), jnp.float32)
        held = [dense] if before is None else [dense, before]
        return pl.pallas_call(
            functools.partial(step_kernel, [wanted[0]] + [cols[d][0] for d in dists], span, last),
            out_shape=out,
            in_specs=[SMEM] * (2 + len(dists)) + [VMEM] * (len(dists) + len(held)),
            out_specs=VMEM,
            scratch_shapes=[
                pltpu.VMEM((rows, inner_rows * block, slots * block), dtype),
                pltpu.SMEM((inner_rows, COLS_DEV), jnp.int32),
            ],
            compiler_params=PARAMS,
            cost_estimate=FREE,
        )(place, wanted[1], *[cols[d][1] for d in dists], *[shards[d] for d in dists], *held)

    order, every = list(range(1, end)) + [0, end], list(range(rows))
    early, late = order[:-4], order[-4:]
    for d in range(1, end):
        cols[d] = (0, index_of([shards[d]], b_tiles))

    def products(wanted, packs, spans):
        dense, total = dense_of(packs), None
        for at in range(0, len(early), 4):
            total = step(early[at : at + 4], wanted, dense, total, every, False)
        return [step(late, wanted, dense, total, span, True) for span in spans]

    given = products((a_cols.size, index_of([other], a_tiles)), other_packs, [[i] for i in every])
    given = [give_back(x) for x in given]
    (kept,) = products((None, c_cols), own_packs, [every])
    return jnp.where(working, kept, jnp.concatenate(given, axis=0))


def solution(mesh):
    return jax.shard_map(
        functools.partial(body, mesh.shape["row"], mesh.shape["col"]),
        mesh=mesh,
        in_specs=(
            P(("groups", "row"), "col", None, None),
            P(("groups", "row"), "col"),
            P(("groups", "row"), "col", None, None),
            P(("groups", "row"), "col"),
            P(("groups", "row"), "col"),
        ),
        out_specs=P(("groups", "row"), "col", None, None),
        check_vma=False,
    )
```

```python
import functools

import jax
import jax.numpy as jnp
from jax import lax
from jax.experimental import pallas as pl
from jax.experimental.pallas import tpu as pltpu
from jax.sharding import PartitionSpec as P

COLS_DEV = 16

SMEM = pl.BlockSpec(memory_space=pltpu.SMEM)
VMEM = pl.BlockSpec(memory_space=pltpu.VMEM)
PARAMS = pltpu.CompilerParams(vmem_limit_bytes=32 * 2**20)
FREE = pl.CostEstimate(flops=1, bytes_accessed=1, transcendentals=0)


def pack_kernel(*refs):
    indices, tiles, out = refs[:-2], refs[-2], refs[-1]
    size = tiles.shape[0]
    out[:size, :] = tiles[...]
    row = lax.broadcasted_iota(jnp.int32, (out.shape[0] - size, out.shape[1]), 0)
    found = jnp.zeros(row.shape, jnp.float32)
    at = 0
    for index in indices:
        for i in range(index.shape[0]):
            for k in range(index.shape[1]):
                found = jnp.where(row == at, index[i, k].astype(jnp.float32), found)
                at += 1
    out[size:, :] = found.astype(out.dtype)


def left_kernel(slots, index, *refs):
    parts, dense = refs[:-1], refs[-1]
    dense[...] = jnp.zeros_like(dense)
    rows, _, block, _ = dense.shape
    for p, part in enumerate(parts):
        for i in range(rows):
            for s in range(slots):
                inner = index[p, i * slots + s]
                start = (i * slots + s) * block

                @pl.when(inner >= 0)
                def _():
                    dense[i, inner] = part[start : start + block, :]


def step_kernel(starts, span, last, place, *refs):
    parts = len(starts) - 1
    wanted, refs = refs[0], refs[1:]
    cols, refs = refs[:parts], refs[parts:]
    tiles, refs = refs[:parts], refs[parts:]
    dense, refs = refs[0], refs[1:]
    before, out, right, slot = refs if len(refs) == 4 else (None,) + refs
    @pl.when(place[0] >= 0)
    def _():
        first = place[0]
        inner_rows = slot.shape[0]
        block = dense.shape[-1]
        slots = right.shape[2] // block
        inner_slots = tiles[0].shape[0] // block // inner_rows

        def read(ref, start, i, k, width):
            return ref[i, k] if start is None else ref[0, start + i * width + k]

        sums = {i: None if before is None else before[i] for i in span}
        for p in range(parts):
            for m in range(inner_rows):
                for c in range(COLS_DEV):
                    slot[m, c] = -1
                for l in range(inner_slots):
                    slot[m, read(cols[p], starts[1 + p], m, l, inner_slots) - first] = l
            for i in span:
                for j in range(slots):
                    column = read(wanted, starts[0], i, j, slots) - first
                    for m in range(inner_rows):
                        l = slot[m, column]
                        start = pl.multiple_of((m * inner_slots + jnp.maximum(l, 0)) * block, block)
                        tile = tiles[p][pl.ds(start, block), :]
                        right[i, m * block : (m + 1) * block, j * block : (j + 1) * block] = jnp.where(
                            l >= 0, tile, jnp.zeros_like(tile)
                        )
            for i in span:
                left = jnp.concatenate(
                    [dense[i, place[1 + p] * inner_rows + m] for m in range(inner_rows)], axis=1
                )
                product = jnp.dot(left, right[i], preferred_element_type=jnp.float32)
                sums[i] = product if sums[i] is None else sums[i] + product
        for at, i in enumerate(span):
            if last:
                for j in range(slots):
                    out[at, j] = sums[i][:, j * block : (j + 1) * block].astype(out.dtype)
            else:
                out[i] = sums[i]


def parity(k):
    return bin(k).count("1") % 2


def body(row_count, col_count, a_tiles, a_cols, b_tiles, b_cols, c_cols):
    rows, slots = c_cols.shape
    inner_rows = b_tiles.shape[0]
    block = a_tiles.shape[-1]
    dtype = b_tiles.dtype
    r, q = lax.axis_index("row"), lax.axis_index("col")
    first = q * COLS_DEV
    bits = sum((r >> k) & 1 for k in range(row_count.bit_length()))
    working = (bits + q) % 2 == 0

    def works(k, c):
        return parity(k) == c % 2

    def swap(x, axis, n, d):
        return lax.ppermute(x, axis, [(k, k ^ d) for k in range(n)])

    def permute(x, target):
        pairs = []
        for k in range(row_count):
            for c in range(col_count):
                to, at = target(k, c)
                pairs.append((k * col_count + c, to * col_count + at))
        return lax.ppermute(x, ("row", "col"), pairs)

    def deliver(x, d):
        def target(k, c):
            if parity(d):
                return (k, c ^ 1) if works(k, c) else (k ^ d, c)
            return (k ^ d, c) if works(k, c) else (k, c ^ (col_count // 2))

        return permute(x, target)

    def give_back(x):
        return permute(x, lambda k, c: (k ^ 1, c) if works(k, c) else (k, c ^ 1))

    def pack(tiles, *indices):
        size = tiles.size // block
        count = sum(x.size for x in indices)
        return pl.pallas_call(
            pack_kernel,
            out_shape=jax.ShapeDtypeStruct((size + -(-count // 16) * 16, block), dtype),
            in_specs=[SMEM] * len(indices) + [VMEM],
            out_specs=VMEM,
            compiler_params=PARAMS,
            cost_estimate=FREE,
        )(*indices, tiles.reshape(size, block))

    def index_of(packs, tiles):
        return jnp.stack([x[tiles.size // block :, 0] for x in packs]).astype(jnp.int32)

    def across(parts, d):
        while d:
            parts = parts + [swap(part, "col", col_count, d) for part in parts]
            d //= 2
        return parts

    far, end = col_count // 2, row_count - 1
    flat = b_tiles.reshape(-1, block)
    own, packed = pack(a_tiles, a_cols, c_cols), pack(b_tiles, b_cols)
    shards = {0: flat, end: deliver(flat, end)}
    own_packs = [own, swap(own, "col", col_count, far)]
    late_cols = lax.optimization_barrier((b_cols, own_packs[1]))[0]
    cols = {0: (None, b_cols), end: (None, swap(late_cols, "row", row_count, end))}
    other = swap(own, "row", row_count, 1)
    ready = packed
    for d in range(end - 1, 0, -1):
        shards[d] = deliver(ready, d)
    other = lax.optimization_barrier((other, shards[end]))[0]
    own_packs, other_packs = across(own_packs, far // 2), across([other], far)
    def dense_of(packs):
        return pl.pallas_call(
            functools.partial(left_kernel, a_cols.shape[1]),
            out_shape=jax.ShapeDtypeStruct((rows, inner_rows * row_count, block, block), dtype),
            in_specs=[SMEM] + [VMEM] * len(packs),
            out_specs=VMEM,
            compiler_params=PARAMS,
            cost_estimate=FREE,
        )(index_of(packs, a_tiles), *packs)

    def step(dists, wanted, dense, before, span, last):
        place = jnp.stack([jnp.where(working, first, -1)] + [r ^ d for d in dists]).astype(jnp.int32)
        if last:
            out = jax.ShapeDtypeStruct((len(span), slots, block, block), dtype)
        else:
            out = jax.ShapeDtypeStruct((rows, block, slots * block), jnp.float32)
        held = [dense] if before is None else [dense, before]
        return pl.pallas_call(
            functools.partial(step_kernel, [wanted[0]] + [cols[d][0] for d in dists], span, last),
            out_shape=out,
            in_specs=[SMEM] * (2 + len(dists)) + [VMEM] * (len(dists) + len(held)),
            out_specs=VMEM,
            scratch_shapes=[
                pltpu.VMEM((rows, inner_rows * block, slots * block), dtype),
                pltpu.SMEM((inner_rows, COLS_DEV), jnp.int32),
            ],
            compiler_params=PARAMS,
            cost_estimate=FREE,
        )(place, wanted[1], *[cols[d][1] for d in dists], *[shards[d] for d in dists], *held)

    order, every = list(range(1, end)) + [0, end], list(range(rows))
    order = order[-2:] + order[:-2]
    early, late = order[:-2], order[-2:]
    for d in range(1, end):
        cols[d] = None

    def products(wanted, packs, spans):
        dense, total = dense_of(packs), None
        for d in range(1, end):
            if cols[d] is None:
                cols[d] = (0, index_of(lax.optimization_barrier(([shards[d]], dense))[0], b_tiles))
        for at in range(0, len(early), 4):
            total = step(early[at : at + 4], wanted, dense, total, every, False)
        return [step(late, wanted, dense, total, span, True) for span in spans]

    given = products((a_cols.size, index_of([other], a_tiles)), other_packs, [[i] for i in every])
    given = [give_back(x) for x in given]
    (kept,) = products((None, c_cols), own_packs, [every])
    return jnp.where(working, kept, jnp.concatenate(given, axis=0))


def solution(mesh):
    return jax.shard_map(
        functools.partial(body, mesh.shape["row"], mesh.shape["col"]),
        mesh=mesh,
        in_specs=(
            P(("groups", "row"), "col", None, None),
            P(("groups", "row"), "col"),
            P(("groups", "row"), "col", None, None),
            P(("groups", "row"), "col"),
            P(("groups", "row"), "col"),
        ),
        out_specs=P(("groups", "row"), "col", None, None),
        check_vma=False,
    )
```

```python
import functools

import jax
import jax.numpy as jnp
from jax import lax
from jax.experimental import pallas as pl
from jax.experimental.pallas import tpu as pltpu
from jax.sharding import PartitionSpec as P

COLS_DEV = 16

SMEM = pl.BlockSpec(memory_space=pltpu.SMEM)
VMEM = pl.BlockSpec(memory_space=pltpu.VMEM)
PARAMS = pltpu.CompilerParams(vmem_limit_bytes=32 * 2**20)
FREE = pl.CostEstimate(flops=1, bytes_accessed=1, transcendentals=0)


def pack_kernel(*refs):
    indices, tiles, out = refs[:-2], refs[-2], refs[-1]
    size = tiles.shape[0]
    out[:size, :] = tiles[...]
    row = lax.broadcasted_iota(jnp.int32, (out.shape[0] - size, out.shape[1]), 0)
    found = jnp.zeros(row.shape, jnp.float32)
    at = 0
    for index in indices:
        for i in range(index.shape[0]):
            for k in range(index.shape[1]):
                found = jnp.where(row == at, index[i, k].astype(jnp.float32), found)
                at += 1
    out[size:, :] = found.astype(out.dtype)


def left_kernel(slots, index, *refs):
    parts, dense = refs[:-1], refs[-1]
    dense[...] = jnp.zeros_like(dense)
    rows, _, block, _ = dense.shape
    for p, part in enumerate(parts):
        for i in range(rows):
            for s in range(slots):
                inner = index[p, i * slots + s]
                start = (i * slots + s) * block

                @pl.when(inner >= 0)
                def _():
                    dense[i, inner] = part[start : start + block, :]


def step_kernel(starts, span, last, place, *refs):
    parts = len(starts) - 1
    wanted, refs = refs[0], refs[1:]
    cols, refs = refs[:parts], refs[parts:]
    tiles, refs = refs[:parts], refs[parts:]
    dense, refs = refs[0], refs[1:]
    before, out, right, slot = refs if len(refs) == 4 else (None,) + refs
    @pl.when(place[0] >= 0)
    def _():
        first = place[0]
        inner_rows = slot.shape[0]
        block = dense.shape[-1]
        slots = right.shape[2] // block
        inner_slots = tiles[0].shape[0] // block // inner_rows

        def read(ref, start, i, k, width):
            return ref[i, k] if start is None else ref[0, start + i * width + k]

        sums = {i: None if before is None else before[i] for i in span}
        for p in range(parts):
            for m in range(inner_rows):
                for c in range(COLS_DEV):
                    slot[m, c] = -1
                for l in range(inner_slots):
                    slot[m, read(cols[p], starts[1 + p], m, l, inner_slots) - first] = l
            for i in span:
                for j in range(slots):
                    column = read(wanted, starts[0], i, j, slots) - first
                    for m in range(inner_rows):
                        l = slot[m, column]
                        start = pl.multiple_of((m * inner_slots + jnp.maximum(l, 0)) * block, block)
                        tile = tiles[p][pl.ds(start, block), :]
                        right[i, m * block : (m + 1) * block, j * block : (j + 1) * block] = jnp.where(
                            l >= 0, tile, jnp.zeros_like(tile)
                        )
            for i in span:
                left = jnp.concatenate(
                    [dense[i, place[1 + p] * inner_rows + m] for m in range(inner_rows)], axis=1
                )
                product = jnp.dot(left, right[i], preferred_element_type=jnp.float32)
                sums[i] = product if sums[i] is None else sums[i] + product
        for at, i in enumerate(span):
            if last:
                for j in range(slots):
                    out[at, j] = sums[i][:, j * block : (j + 1) * block].astype(out.dtype)
            else:
                out[i] = sums[i]


def parity(k):
    return bin(k).count("1") % 2


def body(row_count, col_count, a_tiles, a_cols, b_tiles, b_cols, c_cols):
    rows, slots = c_cols.shape
    inner_rows = b_tiles.shape[0]
    block = a_tiles.shape[-1]
    dtype = b_tiles.dtype
    r, q = lax.axis_index("row"), lax.axis_index("col")
    first = q * COLS_DEV
    bits = sum((r >> k) & 1 for k in range(row_count.bit_length()))
    working = (bits + q) % 2 == 0

    def works(k, c):
        return parity(k) == c % 2

    def swap(x, axis, n, d):
        return lax.ppermute(x, axis, [(k, k ^ d) for k in range(n)])

    def permute(x, target):
        pairs = []
        for k in range(row_count):
            for c in range(col_count):
                to, at = target(k, c)
                pairs.append((k * col_count + c, to * col_count + at))
        return lax.ppermute(x, ("row", "col"), pairs)

    def deliver(x, dists):
        def target(k, c):
            d = dists[c % 2]
            if parity(d):
                return (k, c ^ 1) if works(k, c) else (k ^ d, c)
            return (k ^ d, c) if works(k, c) else (k, c ^ (col_count // 2))

        return permute(x, target)

    def give_back(x):
        return permute(x, lambda k, c: (k ^ 1, c) if works(k, c) else (k, c ^ 1))

    def pack(tiles, *indices):
        size = tiles.size // block
        count = sum(x.size for x in indices)
        return pl.pallas_call(
            pack_kernel,
            out_shape=jax.ShapeDtypeStruct((size + -(-count // 16) * 16, block), dtype),
            in_specs=[SMEM] * len(indices) + [VMEM],
            out_specs=VMEM,
            compiler_params=PARAMS,
            cost_estimate=FREE,
        )(*indices, tiles.reshape(size, block))

    def index_of(packs, tiles):
        return jnp.stack([x[tiles.size // block :, 0] for x in packs]).astype(jnp.int32)

    def across(parts, d):
        while d:
            parts = parts + [swap(part, "col", col_count, d) for part in parts]
            d //= 2
        return parts

    odd = [d for d in range(1, row_count) if parity(d)]
    deliveries = [(d, e) for d, e in zip(reversed(odd), odd)]
    deliveries[1:1] = [(d, d) for d in range(row_count - 1, 0, -1) if not parity(d)]
    start, far = deliveries[0], col_count // 2
    flat = b_tiles.reshape(-1, block)
    own, packed = pack(a_tiles, a_cols, c_cols), pack(b_tiles, b_cols)
    shards = {(0, 0): flat, start: deliver(flat, start)}
    own_packs = [own, swap(own, "col", col_count, far)]
    late_cols = lax.optimization_barrier((b_cols, own_packs[1]))[0]
    cols = {(0, 0): (None, b_cols), start: (None, deliver(late_cols, start))}
    other = swap(own, "row", row_count, 1)
    for dists in deliveries[1:]:
        shards[dists] = deliver(packed, dists)
    other = lax.optimization_barrier((other, shards[start]))[0]
    own_packs, other_packs = across(own_packs, far // 2), across([other], far)

    def dense_of(packs):
        return pl.pallas_call(
            functools.partial(left_kernel, a_cols.shape[1]),
            out_shape=jax.ShapeDtypeStruct((rows, inner_rows * row_count, block, block), dtype),
            in_specs=[SMEM] + [VMEM] * len(packs),
            out_specs=VMEM,
            compiler_params=PARAMS,
            cost_estimate=FREE,
        )(index_of(packs, a_tiles), *packs)

    def step(dists, wanted, dense, before, span, last):
        sources = [r ^ jnp.where(q % 2 == 0, d, e) for d, e in dists]
        place = jnp.stack([jnp.where(working, first, -1)] + sources).astype(jnp.int32)
        if last:
            out = jax.ShapeDtypeStruct((len(span), slots, block, block), dtype)
        else:
            out = jax.ShapeDtypeStruct((rows, block, slots * block), jnp.float32)
        held = [dense] if before is None else [dense, before]
        return pl.pallas_call(
            functools.partial(step_kernel, [wanted[0]] + [cols[d][0] for d in dists], span, last),
            out_shape=out,
            in_specs=[SMEM] * (2 + len(dists)) + [VMEM] * (len(dists) + len(held)),
            out_specs=VMEM,
            scratch_shapes=[
                pltpu.VMEM((rows, inner_rows * block, slots * block), dtype),
                pltpu.SMEM((inner_rows, COLS_DEV), jnp.int32),
            ],
            compiler_params=PARAMS,
            cost_estimate=FREE,
        )(place, wanted[1], *[cols[d][1] for d in dists], *[shards[d] for d in dists], *held)

    order, every = [(0, 0)] + deliveries, list(range(rows))
    early, late = order[:-2], order[-2:]

    def products(wanted, packs, spans):
        dense, total = dense_of(packs), None
        for d in deliveries:
            if d not in cols:
                x = lax.optimization_barrier((shards[d], dense))[0] if d in late else shards[d]
                cols[d] = (0, index_of([x], b_tiles))
        for at in range(0, len(early), 2):
            total = step(early[at : at + 2], wanted, dense, total, every, False)
        return [step(late, wanted, dense, total, span, True) for span in spans]

    given = products((a_cols.size, index_of([other], a_tiles)), other_packs, [[i] for i in every])
    given = [give_back(x) for x in given]
    (kept,) = products((None, c_cols), own_packs, [every])
    return jnp.where(working, kept, jnp.concatenate(given, axis=0))


def solution(mesh):
    return jax.shard_map(
        functools.partial(body, mesh.shape["row"], mesh.shape["col"]),
        mesh=mesh,
        in_specs=(
            P(("groups", "row"), "col", None, None),
            P(("groups", "row"), "col"),
            P(("groups", "row"), "col", None, None),
            P(("groups", "row"), "col"),
            P(("groups", "row"), "col"),
        ),
        out_specs=P(("groups", "row"), "col", None, None),
        check_vma=False,
    )
```

```python
import functools

import jax
import jax.numpy as jnp
from jax import lax
from jax.experimental import pallas as pl
from jax.experimental.pallas import tpu as pltpu
from jax.sharding import PartitionSpec as P

COLS_DEV = 16

SMEM = pl.BlockSpec(memory_space=pltpu.SMEM)
VMEM = pl.BlockSpec(memory_space=pltpu.VMEM)
PARAMS = pltpu.CompilerParams(vmem_limit_bytes=32 * 2**20)
FREE = pl.CostEstimate(flops=1, bytes_accessed=1, transcendentals=0)


def pack_kernel(*refs):
    indices, tiles, out = refs[:-2], refs[-2], refs[-1]
    size = tiles.shape[0]
    out[:size, :] = tiles[...]
    row = lax.broadcasted_iota(jnp.int32, (out.shape[0] - size, out.shape[1]), 0)
    found = jnp.zeros(row.shape, jnp.float32)
    at = 0
    for index in indices:
        for i in range(index.shape[0]):
            for k in range(index.shape[1]):
                found = jnp.where(row == at, index[i, k].astype(jnp.float32), found)
                at += 1
    out[size:, :] = found.astype(out.dtype)


def left_kernel(group, index, *refs):
    parts, dense = refs[:-1], refs[-1]
    dense[...] = jnp.zeros_like(dense)
    rows, slots = parts[0].shape[:2]
    for p, part in enumerate(parts):
        for i in range(rows):
            for s in range(slots):
                inner = index[(2 * p + group) * rows + i, s]

                @pl.when(inner >= 0)
                def _():
                    dense[i, inner] = part[i, s]


def step_kernel(starts, span, last, place, *refs):
    parts = len(starts) - 1
    wanted, refs = refs[0], refs[1:]
    cols, refs = refs[:parts], refs[parts:]
    tiles, refs = refs[:parts], refs[parts:]
    dense, refs = refs[0], refs[1:]
    before, out, right, slot = refs if len(refs) == 4 else (None,) + refs
    @pl.when(place[0] >= 0)
    def _():
        first = place[0]
        inner_rows = slot.shape[0]
        block = dense.shape[-1]
        slots = right.shape[2] // block
        inner_slots = tiles[0].shape[0] // block // inner_rows

        def read(ref, start, i, k, width):
            return ref[start[0] + i, start[1] + k] if isinstance(start, tuple) else ref[0, start + i * width + k]

        sums = {i: None if before is None else before[i] for i in span}
        for p in range(parts):
            for m in range(inner_rows):
                for c in range(COLS_DEV):
                    slot[m, c] = -1
                for l in range(inner_slots):
                    slot[m, read(cols[p], starts[1 + p], m, l, inner_slots) - first] = l
            for i in span:
                for j in range(slots):
                    column = read(wanted, starts[0], i, j, slots) - first
                    for m in range(inner_rows):
                        l = slot[m, column]
                        start = pl.multiple_of((m * inner_slots + jnp.maximum(l, 0)) * block, block)
                        tile = tiles[p][pl.ds(start, block), :]
                        right[i, m * block : (m + 1) * block, j * block : (j + 1) * block] = jnp.where(
                            l >= 0, tile, jnp.zeros_like(tile)
                        )
            for i in span:
                left = jnp.concatenate(
                    [dense[i, place[1 + p] * inner_rows + m] for m in range(inner_rows)], axis=1
                )
                product = jnp.dot(left, right[i], preferred_element_type=jnp.float32)
                sums[i] = product if sums[i] is None else sums[i] + product
        for at, i in enumerate(span):
            if last:
                for j in range(slots):
                    out[at, j] = sums[i][:, j * block : (j + 1) * block].astype(out.dtype)
            else:
                out[i] = sums[i]


def parity(k):
    return bin(k).count("1") % 2


def body(row_count, col_count, a_tiles, a_cols, b_tiles, b_cols, c_cols):
    rows, slots = c_cols.shape
    inner_rows = b_tiles.shape[0]
    block = a_tiles.shape[-1]
    dtype = b_tiles.dtype
    r, q = lax.axis_index("row"), lax.axis_index("col")
    first = q * COLS_DEV
    bits = sum((r >> k) & 1 for k in range(row_count.bit_length()))
    working = (bits + q) % 2 == 0

    def works(k, c):
        return parity(k) == c % 2

    def swap(x, axis, n, d):
        return lax.ppermute(x, axis, [(k, k ^ d) for k in range(n)])

    def permute(x, target):
        pairs = []
        for k in range(row_count):
            for c in range(col_count):
                to, at = target(k, c)
                pairs.append((k * col_count + c, to * col_count + at))
        return lax.ppermute(x, ("row", "col"), pairs)

    def deliver(x, d):
        def target(k, c):
            if parity(d):
                return (k, c ^ 1) if works(k, c) else (k ^ d, c)
            return (k ^ d, c) if works(k, c) else (k, c ^ (col_count // 2))

        return permute(x, target)

    def give_back(x):
        return permute(x, lambda k, c: (k ^ 1, c) if works(k, c) else (k, c ^ 1))

    def pack(tiles, *indices):
        size = tiles.size // block
        count = sum(x.size for x in indices)
        return pl.pallas_call(
            pack_kernel,
            out_shape=jax.ShapeDtypeStruct((size + -(-count // 16) * 16, block), dtype),
            in_specs=[SMEM] * len(indices) + [VMEM],
            out_specs=VMEM,
            compiler_params=PARAMS,
            cost_estimate=FREE,
        )(*indices, tiles.reshape(size, block))

    def index_of(packs, tiles):
        return jnp.stack([x[tiles.size // block :, 0] for x in packs]).astype(jnp.int32)

    def across(parts, d):
        while d:
            parts = parts + [swap(part, "col", col_count, d) for part in parts]
            d //= 2
        return parts

    far, end = col_count // 2, row_count - 1
    flat, packed = b_tiles.reshape(-1, block), pack(b_tiles, b_cols)
    index = jnp.concatenate([a_cols, c_cols], axis=1)
    index = jnp.concatenate([index, swap(index, "row", row_count, 1)], axis=0)
    other = swap(a_tiles, "row", row_count, 1)
    shards = {0: flat, end: deliver(flat, end)}
    late_a, late_cols = lax.optimization_barrier((a_tiles, b_cols, other))[:2]
    cols = {0: ((0, 0), b_cols), end: ((0, 0), swap(late_cols, "row", row_count, end))}
    for d in range(end - 1, 0, -1):
        shards[d] = deliver(packed, d)
    own_parts = across([late_a], far)
    other_parts = [other, swap(other, "col", col_count, far)]
    other_parts = list(lax.optimization_barrier((other_parts, shards[end]))[0])
    other_parts = across(other_parts, far // 2)
    around, d = index, far
    while d:
        around = jnp.concatenate([around, swap(around, "col", col_count, d)], axis=0)
        d //= 2

    def dense_of(group, parts):
        return pl.pallas_call(
            functools.partial(left_kernel, group),
            out_shape=jax.ShapeDtypeStruct((rows, inner_rows * row_count, block, block), dtype),
            in_specs=[SMEM] + [VMEM] * len(parts),
            out_specs=VMEM,
            compiler_params=PARAMS,
            cost_estimate=FREE,
        )(around, *parts)

    def step(dists, wanted, dense, before, span, last):
        place = jnp.stack([jnp.where(working, first, -1)] + [r ^ d for d in dists]).astype(jnp.int32)
        if last:
            out = jax.ShapeDtypeStruct((len(span), slots, block, block), dtype)
        else:
            out = jax.ShapeDtypeStruct((rows, block, slots * block), jnp.float32)
        held = [dense] if before is None else [dense, before]
        return pl.pallas_call(
            functools.partial(step_kernel, [wanted[0]] + [cols[d][0] for d in dists], span, last),
            out_shape=out,
            in_specs=[SMEM] * (2 + len(dists)) + [VMEM] * (len(dists) + len(held)),
            out_specs=VMEM,
            scratch_shapes=[
                pltpu.VMEM((rows, inner_rows * block, slots * block), dtype),
                pltpu.SMEM((inner_rows, COLS_DEV), jnp.int32),
            ],
            compiler_params=PARAMS,
            cost_estimate=FREE,
        )(place, wanted[1], *[cols[d][1] for d in dists], *[shards[d] for d in dists], *held)

    order, every = [0] + list(range(end, 0, -1)), list(range(rows))
    early, late = order[:-2], order[-2:]

    def products(wanted, dense, spans):
        total = None
        for d in range(1, end):
            if d not in cols:
                x = lax.optimization_barrier((shards[d], dense))[0] if d in late else shards[d]
                cols[d] = (0, index_of([x], b_tiles))
        for at in range(0, len(early), 2):
            total = step(early[at : at + 2], wanted, dense, total, every, False)
        return [step(late, wanted, dense, total, span, True) for span in spans]

    given = products(((rows, a_cols.shape[1]), index), dense_of(1, other_parts), [[i] for i in every])
    given = [give_back(x) for x in given]
    (kept,) = products(((0, 0), c_cols), dense_of(0, own_parts), [every])
    return jnp.where(working, kept, jnp.concatenate(given, axis=0))


def solution(mesh):
    return jax.shard_map(
        functools.partial(body, mesh.shape["row"], mesh.shape["col"]),
        mesh=mesh,
        in_specs=(
            P(("groups", "row"), "col", None, None),
            P(("groups", "row"), "col"),
            P(("groups", "row"), "col", None, None),
            P(("groups", "row"), "col"),
            P(("groups", "row"), "col"),
        ),
        out_specs=P(("groups", "row"), "col", None, None),
        check_vma=False,
    )
```

```python
import functools

import jax
import jax.numpy as jnp
from jax import lax
from jax.experimental import pallas as pl
from jax.experimental.pallas import tpu as pltpu
from jax.sharding import PartitionSpec as P

COLS_DEV = 16

ANY = pl.BlockSpec(memory_space=pl.ANY)
SMEM = pl.BlockSpec(memory_space=pltpu.SMEM)
VMEM = pl.BlockSpec(memory_space=pltpu.VMEM)
PARAMS = pltpu.CompilerParams(vmem_limit_bytes=32 * 2**20)
FREE = pl.CostEstimate(flops=1, bytes_accessed=1, transcendentals=0)


def pack_kernel(counts, *refs):
    groups = len(counts)
    indices, refs = refs[: sum(counts)], refs[sum(counts) :]
    tiles, outs, rows, sems = refs[:groups], refs[groups : 2 * groups], refs[2 * groups : 3 * groups], refs[3 * groups]
    copies = [
        pltpu.make_async_copy(x, out.at[: x.shape[0]], sems.at[2 * g]) for g, (x, out) in enumerate(zip(tiles, outs))
    ]
    for copy in copies:
        copy.start()
    for g, count in enumerate(counts):
        row = lax.broadcasted_iota(jnp.int32, rows[g].shape, 0)
        found, at = jnp.zeros(row.shape, jnp.float32), 0
        for index in indices[:count]:
            for i in range(index.shape[0]):
                for k in range(index.shape[1]):
                    found = jnp.where(row == at, index[i, k].astype(jnp.float32), found)
                    at += 1
        indices = indices[count:]
        rows[g][...] = found.astype(rows[g].dtype)
        copy = pltpu.make_async_copy(rows[g], outs[g].at[tiles[g].shape[0] :], sems.at[2 * g + 1])
        copy.start()
        copies.append(copy)
    for copy in copies:
        copy.wait()


def left_kernel(slots, index, *refs):
    parts, dense = refs[:-1], refs[-1]
    dense[...] = jnp.zeros_like(dense)
    rows, _, block, _ = dense.shape
    for p, part in enumerate(parts):
        for i in range(rows):
            for s in range(slots):
                inner = index[p, i * slots + s]
                start = (i * slots + s) * block

                @pl.when(inner >= 0)
                def _():
                    dense[i, inner] = part[start : start + block, :]


def step_kernel(starts, span, last, place, *refs):
    parts = len(starts) - 1
    wanted, refs = refs[0], refs[1:]
    cols, refs = refs[:parts], refs[parts:]
    tiles, refs = refs[:parts], refs[parts:]
    dense, refs = refs[0], refs[1:]
    before, out, right, slot = refs if len(refs) == 4 else (None,) + refs
    @pl.when(place[0] >= 0)
    def _():
        first = place[0]
        inner_rows = slot.shape[0]
        block = dense.shape[-1]
        slots = right.shape[2] // block
        inner_slots = tiles[0].shape[0] // block // inner_rows

        def read(ref, start, i, k, width):
            return ref[i, k] if start is None else ref[0, start + i * width + k]

        sums = {i: None if before is None else before[i] for i in span}
        for p in range(parts):
            for m in range(inner_rows):
                for c in range(COLS_DEV):
                    slot[m, c] = -1
                for l in range(inner_slots):
                    slot[m, read(cols[p], starts[1 + p], m, l, inner_slots) - first] = l
            for i in span:
                for j in range(slots):
                    column = read(wanted, starts[0], i, j, slots) - first
                    for m in range(inner_rows):
                        l = slot[m, column]
                        start = pl.multiple_of((m * inner_slots + jnp.maximum(l, 0)) * block, block)
                        tile = tiles[p][pl.ds(start, block), :]
                        right[i, m * block : (m + 1) * block, j * block : (j + 1) * block] = jnp.where(
                            l >= 0, tile, jnp.zeros_like(tile)
                        )
            for i in span:
                left = jnp.concatenate(
                    [dense[i, place[1 + p] * inner_rows + m] for m in range(inner_rows)], axis=1
                )
                product = jnp.dot(left, right[i], preferred_element_type=jnp.float32)
                sums[i] = product if sums[i] is None else sums[i] + product
        for at, i in enumerate(span):
            if last:
                for j in range(slots):
                    out[at, j] = sums[i][:, j * block : (j + 1) * block].astype(out.dtype)
            else:
                out[i] = sums[i]


def parity(k):
    return bin(k).count("1") % 2


def body(row_count, col_count, a_tiles, a_cols, b_tiles, b_cols, c_cols):
    rows, slots = c_cols.shape
    inner_rows = b_tiles.shape[0]
    block = a_tiles.shape[-1]
    dtype = b_tiles.dtype
    r, q = lax.axis_index("row"), lax.axis_index("col")
    first = q * COLS_DEV
    bits = sum((r >> k) & 1 for k in range(row_count.bit_length()))
    working = (bits + q) % 2 == 0

    def works(k, c):
        return parity(k) == c % 2

    def swap(x, axis, n, d):
        return lax.ppermute(x, axis, [(k, k ^ d) for k in range(n)])

    def permute(x, target):
        pairs = []
        for k in range(row_count):
            for c in range(col_count):
                to, at = target(k, c)
                pairs.append((k * col_count + c, to * col_count + at))
        return lax.ppermute(x, ("row", "col"), pairs)

    def deliver(x, d):
        def target(k, c):
            if parity(d):
                return (k, c ^ 1) if works(k, c) else (k ^ d, c)
            return (k ^ d, c) if works(k, c) else (k, c ^ (col_count // 2))

        return permute(x, target)

    def give_back(x):
        return permute(x, lambda k, c: (k ^ 1, c) if works(k, c) else (k, c ^ 1))

    def pack(*groups):
        flat = [x.reshape(-1, block) for x, _ in groups]
        counts = [len(indices) for _, indices in groups]
        tails = [-(-sum(x.size for x in indices) // 16) * 16 for _, indices in groups]
        return pl.pallas_call(
            functools.partial(pack_kernel, counts),
            out_shape=[
                jax.ShapeDtypeStruct((x.shape[0] + more, block), dtype) for x, more in zip(flat, tails)
            ],
            in_specs=[SMEM] * sum(counts) + [ANY] * len(groups),
            out_specs=[ANY] * len(groups),
            scratch_shapes=[pltpu.VMEM((more, block), dtype) for more in tails]
            + [pltpu.SemaphoreType.DMA((2 * len(groups),))],
            compiler_params=pltpu.CompilerParams(vmem_limit_bytes=66 * 10**6),
            cost_estimate=FREE,
        )(*[x for _, indices in groups for x in indices], *flat)

    def index_of(packs, tiles):
        return jnp.stack([x[tiles.size // block :, 0] for x in packs]).astype(jnp.int32)

    def across(parts, d):
        while d:
            parts = parts + [swap(part, "col", col_count, d) for part in parts]
            d //= 2
        return parts

    far, end = col_count // 2, row_count - 1
    own, packed = pack((a_tiles, (a_cols, c_cols)), (b_tiles, (b_cols,)))
    other = swap(own, "row", row_count, 1)
    shards, cols = {0: b_tiles.reshape(-1, block)}, {0: (None, b_cols)}
    for d in range(end, 0, -1):
        shards[d] = deliver(packed, d)
    other_packs = [other, swap(other, "col", col_count, far)]
    late = lax.optimization_barrier((own, other_packs[1]))[0]
    own_packs = across([late], far)
    other_packs = across(other_packs, far // 2)

    def dense_of(packs):
        return pl.pallas_call(
            functools.partial(left_kernel, a_cols.shape[1]),
            out_shape=jax.ShapeDtypeStruct((rows, inner_rows * row_count, block, block), dtype),
            in_specs=[SMEM] + [VMEM] * len(packs),
            out_specs=VMEM,
            compiler_params=PARAMS,
            cost_estimate=FREE,
        )(index_of(packs, a_tiles), *packs)

    def step(dists, wanted, dense, before, span, last):
        place = jnp.stack([jnp.where(working, first, -1)] + [r ^ d for d in dists]).astype(jnp.int32)
        if last:
            out = jax.ShapeDtypeStruct((len(span), slots, block, block), dtype)
        else:
            out = jax.ShapeDtypeStruct((rows, block, slots * block), jnp.float32)
        held = [dense] if before is None else [dense, before]
        return pl.pallas_call(
            functools.partial(step_kernel, [wanted[0]] + [cols[d][0] for d in dists], span, last),
            out_shape=out,
            in_specs=[SMEM] * (2 + len(dists)) + [VMEM] * (len(dists) + len(held)),
            out_specs=VMEM,
            scratch_shapes=[
                pltpu.VMEM((rows, inner_rows * block, slots * block), dtype),
                pltpu.SMEM((inner_rows, COLS_DEV), jnp.int32),
            ],
            compiler_params=PARAMS,
            cost_estimate=FREE,
        )(place, wanted[1], *[cols[d][1] for d in dists], *[shards[d] for d in dists], *held)

    order, every = [0] + list(range(end, 0, -1)), list(range(rows))
    early, late = order[:-3], order[-3:]

    def products(wanted, packs, spans):
        dense, total = dense_of(packs), None
        for d in early[1:]:
            if d not in cols:
                cols[d] = (0, index_of([shards[d]], b_tiles))
        for at in range(0, len(early), 2):
            total = step(early[at : at + 2], wanted, dense, total, every, False)
        for d in late:
            if d not in cols:
                x = lax.optimization_barrier((shards[d], total))[0]
                cols[d] = (0, index_of([x], b_tiles))
        return [step(late, wanted, dense, total, span, True) for span in spans]

    given = products((a_cols.size, index_of([other], a_tiles)), other_packs, [[i] for i in every])
    given = [give_back(x) for x in given]
    (kept,) = products((None, c_cols), own_packs, [every])
    return jnp.where(working, kept, jnp.concatenate(given, axis=0))


def solution(mesh):
    return jax.shard_map(
        functools.partial(body, mesh.shape["row"], mesh.shape["col"]),
        mesh=mesh,
        in_specs=(
            P(("groups", "row"), "col", None, None),
            P(("groups", "row"), "col"),
            P(("groups", "row"), "col", None, None),
            P(("groups", "row"), "col"),
            P(("groups", "row"), "col"),
        ),
        out_specs=P(("groups", "row"), "col", None, None),
        check_vma=False,
    )
```

```python
import functools

import jax
import jax.numpy as jnp
from jax import lax
from jax.experimental import pallas as pl
from jax.experimental.pallas import tpu as pltpu
from jax.sharding import PartitionSpec as P

COLS_DEV = 16

SMEM = pl.BlockSpec(memory_space=pltpu.SMEM)
VMEM = pl.BlockSpec(memory_space=pltpu.VMEM)
PARAMS = pltpu.CompilerParams(vmem_limit_bytes=32 * 2**20)
FREE = pl.CostEstimate(flops=1, bytes_accessed=1, transcendentals=0)


def pack_kernel(*refs):
    indices, tiles, out = refs[:-2], refs[-2], refs[-1]
    size = tiles.shape[0]
    out[:size, :] = tiles[...]
    row = lax.broadcasted_iota(jnp.int32, (out.shape[0] - size, out.shape[1]), 0)
    found = jnp.zeros(row.shape, jnp.float32)
    at = 0
    for index in indices:
        for i in range(index.shape[0]):
            for k in range(index.shape[1]):
                found = jnp.where(row == at, index[i, k].astype(jnp.float32), found)
                at += 1
    out[size:, :] = found.astype(out.dtype)


def left_kernel(slots, index, *refs):
    parts, dense = refs[:-1], refs[-1]
    dense[...] = jnp.zeros_like(dense)
    rows, _, block, _ = dense.shape
    for p, part in enumerate(parts):
        for i in range(rows):
            for s in range(slots):
                inner = index[p, i * slots + s]
                start = (i * slots + s) * block

                @pl.when(inner >= 0)
                def _():
                    dense[i, inner] = part[start : start + block, :]


def step_kernel(starts, span, last, place, *refs):
    parts = len(starts) - 1
    wanted, refs = refs[0], refs[1:]
    cols, refs = refs[:parts], refs[parts:]
    tiles, refs = refs[:parts], refs[parts:]
    dense, refs = refs[0], refs[1:]
    before, out, right, slot = refs if len(refs) == 4 else (None,) + refs
    @pl.when(place[0] >= 0)
    def _():
        first = place[0]
        inner_rows = slot.shape[0]
        block = dense.shape[-1]
        slots = right.shape[2] // block
        inner_slots = tiles[0].shape[0] // block // inner_rows

        def read(ref, start, i, k, width):
            return ref[i, k] if start is None else ref[0, start + i * width + k]

        sums = {i: None if before is None else before[i] for i in span}
        for p in range(parts):
            for m in range(inner_rows):
                for c in range(COLS_DEV):
                    slot[m, c] = -1
                for l in range(inner_slots):
                    slot[m, read(cols[p], starts[1 + p], m, l, inner_slots) - first] = l
            for i in span:
                for j in range(slots):
                    column = read(wanted, starts[0], i, j, slots) - first
                    for m in range(inner_rows):
                        l = slot[m, column]
                        start = pl.multiple_of((m * inner_slots + jnp.maximum(l, 0)) * block, block)
                        tile = tiles[p][pl.ds(start, block), :]
                        right[i, m * block : (m + 1) * block, j * block : (j + 1) * block] = jnp.where(
                            l >= 0, tile, jnp.zeros_like(tile)
                        )
            for i in span:
                left = jnp.concatenate(
                    [dense[i, place[1 + p] * inner_rows + m] for m in range(inner_rows)], axis=1
                )
                product = jnp.dot(left, right[i], preferred_element_type=jnp.float32)
                sums[i] = product if sums[i] is None else sums[i] + product
        for at, i in enumerate(span):
            if last:
                for j in range(slots):
                    out[at, j] = sums[i][:, j * block : (j + 1) * block].astype(out.dtype)
            else:
                out[i] = sums[i]


def parity(k):
    return bin(k).count("1") % 2


def body(row_count, col_count, a_tiles, a_cols, b_tiles, b_cols, c_cols):
    rows, slots = c_cols.shape
    inner_rows = b_tiles.shape[0]
    block = a_tiles.shape[-1]
    dtype = b_tiles.dtype
    r, q = lax.axis_index("row"), lax.axis_index("col")
    first = q * COLS_DEV
    bits = sum((r >> k) & 1 for k in range(row_count.bit_length()))
    working = (bits + q) % 2 == 0

    def works(k, c):
        return parity(k) == c % 2

    def swap(x, axis, n, d):
        return lax.ppermute(x, axis, [(k, k ^ d) for k in range(n)])

    def permute(x, target):
        pairs = []
        for k in range(row_count):
            for c in range(col_count):
                to, at = target(k, c)
                pairs.append((k * col_count + c, to * col_count + at))
        return lax.ppermute(x, ("row", "col"), pairs)

    def deliver(x, d):
        def target(k, c):
            if parity(d):
                return (k, c ^ 1) if works(k, c) else (k ^ d, c)
            return (k ^ d, c) if works(k, c) else (k, c ^ (col_count // 2))

        return permute(x, target)

    def give_back(x):
        return permute(x, lambda k, c: (k ^ 1, c) if works(k, c) else (k, c ^ 1))

    def pack(tiles, *indices):
        size = tiles.size // block
        count = sum(x.size for x in indices)
        return pl.pallas_call(
            pack_kernel,
            out_shape=jax.ShapeDtypeStruct((size + -(-count // 16) * 16, block), dtype),
            in_specs=[SMEM] * len(indices) + [VMEM],
            out_specs=VMEM,
            compiler_params=PARAMS,
            cost_estimate=FREE,
        )(*indices, tiles.reshape(size, block))

    def index_of(packs, tiles):
        return jnp.stack([x[tiles.size // block :, 0] for x in packs]).astype(jnp.int32)

    def across(parts, d):
        while d:
            parts = parts + [swap(part, "col", col_count, d) for part in parts]
            d //= 2
        return parts

    far, end = col_count // 2, row_count - 1
    flat = b_tiles.reshape(-1, block)
    own, packed = pack(a_tiles, a_cols, c_cols), pack(b_tiles, b_cols)
    shards = {0: flat, end: deliver(flat, end)}
    cols = {0: (None, b_cols), end: (None, swap(b_cols, "row", row_count, end))}
    own_packs = [own, swap(own, "col", col_count, far)]
    other = swap(own, "row", row_count, 1)
    ready = packed
    for d in range(end - 1, 0, -1):
        shards[d] = deliver(ready, d)
    other = lax.optimization_barrier((other, shards[end]))[0]
    own_packs, other_packs = across(own_packs, far // 2), across([other], far)
    def dense_of(packs):
        return pl.pallas_call(
            functools.partial(left_kernel, a_cols.shape[1]),
            out_shape=jax.ShapeDtypeStruct((rows, inner_rows * row_count, block, block), dtype),
            in_specs=[SMEM] + [VMEM] * len(packs),
            out_specs=VMEM,
            compiler_params=PARAMS,
            cost_estimate=FREE,
        )(index_of(packs, a_tiles), *packs)

    def step(dists, wanted, dense, before, span, last):
        place = jnp.stack([jnp.where(working, first, -1)] + [r ^ d for d in dists]).astype(jnp.int32)
        if last:
            out = jax.ShapeDtypeStruct((len(span), slots, block, block), dtype)
        else:
            out = jax.ShapeDtypeStruct((rows, block, slots * block), jnp.float32)
        held = [dense] if before is None else [dense, before]
        return pl.pallas_call(
            functools.partial(step_kernel, [wanted[0]] + [cols[d][0] for d in dists], span, last),
            out_shape=out,
            in_specs=[SMEM] * (2 + len(dists)) + [VMEM] * (len(dists) + len(held)),
            out_specs=VMEM,
            scratch_shapes=[
                pltpu.VMEM((rows, inner_rows * block, slots * block), dtype),
                pltpu.SMEM((inner_rows, COLS_DEV), jnp.int32),
            ],
            compiler_params=PARAMS,
            cost_estimate=FREE,
        )(place, wanted[1], *[cols[d][1] for d in dists], *[shards[d] for d in dists], *held)

    order, every = list(range(1, end)) + [0, end], list(range(rows))
    order = order[-2:] + order[:-2]
    early, late = order[:-2], order[-2:]
    for d in range(1, end):
        cols[d] = None

    def products(wanted, packs, spans):
        dense, total = dense_of(packs), None
        for d in range(1, end):
            if cols[d] is None:
                cols[d] = (0, index_of(lax.optimization_barrier(([shards[d]], dense))[0], b_tiles))
        for at in range(0, len(early), 4):
            total = step(early[at : at + 4], wanted, dense, total, every, False)
        return [step(late, wanted, dense, total, span, True) for span in spans]

    given = products((a_cols.size, index_of([other], a_tiles)), other_packs, [[i] for i in every])
    given = [give_back(x) for x in given]
    (kept,) = products((None, c_cols), own_packs, [every])
    return jnp.where(working, kept, jnp.concatenate(given, axis=0))


def solution(mesh):
    return jax.shard_map(
        functools.partial(body, mesh.shape["row"], mesh.shape["col"]),
        mesh=mesh,
        in_specs=(
            P(("groups", "row"), "col", None, None),
            P(("groups", "row"), "col"),
            P(("groups", "row"), "col", None, None),
            P(("groups", "row"), "col"),
            P(("groups", "row"), "col"),
        ),
        out_specs=P(("groups", "row"), "col", None, None),
        check_vma=False,
    )
```

```python
import functools

import jax
import jax.numpy as jnp
from jax import lax
from jax.experimental import pallas as pl
from jax.experimental.pallas import tpu as pltpu
from jax.sharding import PartitionSpec as P

COLS_DEV = 16

SMEM = pl.BlockSpec(memory_space=pltpu.SMEM)
VMEM = pl.BlockSpec(memory_space=pltpu.VMEM)
PARAMS = pltpu.CompilerParams(vmem_limit_bytes=32 * 2**20)
FREE = pl.CostEstimate(flops=1, bytes_accessed=1, transcendentals=0)


def pack_kernel(*refs):
    indices, tiles, out = refs[:-2], refs[-2], refs[-1]
    size = tiles.shape[0]
    out[:size, :] = tiles[...]
    row = lax.broadcasted_iota(jnp.int32, (out.shape[0] - size, out.shape[1]), 0)
    found = jnp.zeros(row.shape, jnp.float32)
    at = 0
    for index in indices:
        for i in range(index.shape[0]):
            for k in range(index.shape[1]):
                found = jnp.where(row == at, index[i, k].astype(jnp.float32), found)
                at += 1
    out[size:, :] = found.astype(out.dtype)


def left_kernel(slots, index, *refs):
    parts, dense = refs[:-1], refs[-1]
    dense[...] = jnp.zeros_like(dense)
    rows, _, block, _ = dense.shape
    for p, part in enumerate(parts):
        for i in range(rows):
            for s in range(slots):
                inner = index[p, i * slots + s]
                start = (i * slots + s) * block

                @pl.when(inner >= 0)
                def _():
                    dense[i, inner] = part[start : start + block, :]


def step_kernel(starts, span, last, place, *refs):
    parts = len(starts) - 1
    wanted, refs = refs[0], refs[1:]
    cols, refs = refs[:parts], refs[parts:]
    tiles, refs = refs[:parts], refs[parts:]
    dense, refs = refs[0], refs[1:]
    before, out, right, slot = refs if len(refs) == 4 else (None,) + refs
    @pl.when(place[0] >= 0)
    def _():
        first = place[0]
        inner_rows = slot.shape[0]
        block = dense.shape[-1]
        slots = right.shape[2] // block
        inner_slots = tiles[0].shape[0] // block // inner_rows

        def read(ref, start, i, k, width):
            return ref[i, k] if start is None else ref[0, start + i * width + k]

        sums = {i: None if before is None else before[i] for i in span}
        for p in range(parts):
            for m in range(inner_rows):
                for c in range(COLS_DEV):
                    slot[m, c] = -1
                for l in range(inner_slots):
                    slot[m, read(cols[p], starts[1 + p], m, l, inner_slots) - first] = l
            for i in span:
                for j in range(slots):
                    column = read(wanted, starts[0], i, j, slots) - first
                    for m in range(inner_rows):
                        l = slot[m, column]
                        start = pl.multiple_of((m * inner_slots + jnp.maximum(l, 0)) * block, block)
                        tile = tiles[p][pl.ds(start, block), :]
                        right[i, m * block : (m + 1) * block, j * block : (j + 1) * block] = jnp.where(
                            l >= 0, tile, jnp.zeros_like(tile)
                        )
            for i in span:
                left = jnp.concatenate(
                    [dense[i, place[1 + p] * inner_rows + m] for m in range(inner_rows)], axis=1
                )
                product = jnp.dot(left, right[i], preferred_element_type=jnp.float32)
                sums[i] = product if sums[i] is None else sums[i] + product
        for at, i in enumerate(span):
            if last:
                for j in range(slots):
                    out[at, j] = sums[i][:, j * block : (j + 1) * block].astype(out.dtype)
            else:
                out[i] = sums[i]


def parity(k):
    return bin(k).count("1") % 2


def body(row_count, col_count, a_tiles, a_cols, b_tiles, b_cols, c_cols):
    rows, slots = c_cols.shape
    inner_rows = b_tiles.shape[0]
    block = a_tiles.shape[-1]
    dtype = b_tiles.dtype
    r, q = lax.axis_index("row"), lax.axis_index("col")
    first = q * COLS_DEV
    bits = sum((r >> k) & 1 for k in range(row_count.bit_length()))
    working = (bits + q) % 2 == 0

    def works(k, c):
        return parity(k) == c % 2

    def swap(x, axis, n, d):
        return lax.ppermute(x, axis, [(k, k ^ d) for k in range(n)])

    def permute(x, target):
        pairs = []
        for k in range(row_count):
            for c in range(col_count):
                to, at = target(k, c)
                pairs.append((k * col_count + c, to * col_count + at))
        return lax.ppermute(x, ("row", "col"), pairs)

    def deliver(x, d):
        def target(k, c):
            if parity(d):
                return (k, c ^ 1) if works(k, c) else (k ^ d, c)
            return (k ^ d, c) if works(k, c) else (k, c ^ (col_count // 2))

        return permute(x, target)

    def give_back(x):
        return permute(x, lambda k, c: (k ^ 1, c) if works(k, c) else (k, c ^ 1))

    def pack(tiles, *indices):
        size = tiles.size // block
        count = sum(x.size for x in indices)
        return pl.pallas_call(
            pack_kernel,
            out_shape=jax.ShapeDtypeStruct((size + -(-count // 16) * 16, block), dtype),
            in_specs=[SMEM] * len(indices) + [VMEM],
            out_specs=VMEM,
            compiler_params=PARAMS,
            cost_estimate=FREE,
        )(*indices, tiles.reshape(size, block))

    def index_of(packs, tiles):
        return jnp.stack([x[tiles.size // block :, 0] for x in packs]).astype(jnp.int32)

    def across(parts, d):
        while d:
            parts = parts + [swap(part, "col", col_count, d) for part in parts]
            d //= 2
        return parts

    far, end = col_count // 2, row_count - 1
    flat = b_tiles.reshape(-1, block)
    own, packed = pack(a_tiles, a_cols, c_cols), pack(b_tiles, b_cols)
    shards = {0: flat, end: deliver(flat, end)}
    own_packs = [own, swap(own, "col", col_count, far)]
    late_cols = lax.optimization_barrier((b_cols, own_packs[1]))[0]
    cols = {0: (None, b_cols), end: (None, swap(late_cols, "row", row_count, end))}
    other = swap(own, "row", row_count, 1)
    ready = lax.optimization_barrier((packed, own_packs[1]))[0]
    for d in range(end - 1, 0, -1):
        shards[d] = deliver(ready if d > 1 else packed, d)
    other = lax.optimization_barrier((other, shards[end]))[0]
    own_packs, other_packs = across(own_packs, far // 2), across([other], far)
    def dense_of(packs):
        return pl.pallas_call(
            functools.partial(left_kernel, a_cols.shape[1]),
            out_shape=jax.ShapeDtypeStruct((rows, inner_rows * row_count, block, block), dtype),
            in_specs=[SMEM] + [VMEM] * len(packs),
            out_specs=VMEM,
            compiler_params=PARAMS,
            cost_estimate=FREE,
        )(index_of(packs, a_tiles), *packs)

    def step(dists, wanted, dense, before, span, last):
        place = jnp.stack([jnp.where(working, first, -1)] + [r ^ d for d in dists]).astype(jnp.int32)
        if last:
            out = jax.ShapeDtypeStruct((len(span), slots, block, block), dtype)
        else:
            out = jax.ShapeDtypeStruct((rows, block, slots * block), jnp.float32)
        held = [dense] if before is None else [dense, before]
        return pl.pallas_call(
            functools.partial(step_kernel, [wanted[0]] + [cols[d][0] for d in dists], span, last),
            out_shape=out,
            in_specs=[SMEM] * (2 + len(dists)) + [VMEM] * (len(dists) + len(held)),
            out_specs=VMEM,
            scratch_shapes=[
                pltpu.VMEM((rows, inner_rows * block, slots * block), dtype),
                pltpu.SMEM((inner_rows, COLS_DEV), jnp.int32),
            ],
            compiler_params=PARAMS,
            cost_estimate=FREE,
        )(place, wanted[1], *[cols[d][1] for d in dists], *[shards[d] for d in dists], *held)

    order, every = list(range(1, end)) + [0, end], list(range(rows))
    early, late = order[:-4], order[-4:]
    for d in range(1, end):
        cols[d] = (0, index_of([shards[d]], b_tiles))

    def products(wanted, packs, spans):
        dense, total = dense_of(packs), None
        for at in range(0, len(early), 4):
            total = step(early[at : at + 4], wanted, dense, total, every, False)
        return [step(late, wanted, dense, total, span, True) for span in spans]

    given = products((a_cols.size, index_of([other], a_tiles)), other_packs, [[i] for i in every])
    given = [give_back(x) for x in given]
    (kept,) = products((None, c_cols), own_packs, [every])
    return jnp.where(working, kept, jnp.concatenate(given, axis=0))


def solution(mesh):
    return jax.shard_map(
        functools.partial(body, mesh.shape["row"], mesh.shape["col"]),
        mesh=mesh,
        in_specs=(
            P(("groups", "row"), "col", None, None),
            P(("groups", "row"), "col"),
            P(("groups", "row"), "col", None, None),
            P(("groups", "row"), "col"),
            P(("groups", "row"), "col"),
        ),
        out_specs=P(("groups", "row"), "col", None, None),
        check_vma=False,
    )
```

```python
import functools

import jax
import jax.numpy as jnp
from jax import lax
from jax.experimental import pallas as pl
from jax.experimental.pallas import tpu as pltpu
from jax.sharding import PartitionSpec as P

COLS_DEV = 16

SMEM = pl.BlockSpec(memory_space=pltpu.SMEM)
VMEM = pl.BlockSpec(memory_space=pltpu.VMEM)
PARAMS = pltpu.CompilerParams(vmem_limit_bytes=32 * 2**20)
FREE = pl.CostEstimate(flops=1, bytes_accessed=1, transcendentals=0)


def pack_kernel(*refs):
    indices, tiles, out = refs[:-2], refs[-2], refs[-1]
    size = tiles.shape[0]
    out[:size, :] = tiles[...]
    row = lax.broadcasted_iota(jnp.int32, (out.shape[0] - size, out.shape[1]), 0)
    found = jnp.zeros(row.shape, jnp.float32)
    at = 0
    for index in indices:
        for i in range(index.shape[0]):
            for k in range(index.shape[1]):
                found = jnp.where(row == at, index[i, k].astype(jnp.float32), found)
                at += 1
    out[size:, :] = found.astype(out.dtype)


def product_kernel(starts, span, parts, place, left_index, wanted, *refs):
    cols, refs = refs[:parts], refs[parts:]
    tiles, refs = refs[:parts], refs[parts:]
    packs, (out, dense, right, slot) = refs[:-4], refs[-4:]

    @pl.when(place[0] >= 0)
    def _():
        first = place[0]
        inner_rows = slot.shape[0]
        block = dense.shape[-1]
        slots = right.shape[2] // block
        inner_slots = tiles[0].shape[0] // block // inner_rows
        rows = right.shape[0]
        left_slots = (packs[0].shape[0] // block) // rows

        def read(ref, start, i, k, width):
            return ref[i, k] if start is None else ref[0, start + i * width + k]

        for i in span:
            dense[i] = jnp.zeros_like(dense[i])
            for p, pack in enumerate(packs):
                for s in range(left_slots):
                    inner = left_index[p, i * left_slots + s]
                    begin = (i * left_slots + s) * block

                    @pl.when(inner >= 0)
                    def _():
                        dense[i, inner] = pack[begin : begin + block, :]

        for m in range(inner_rows):
            for c in range(COLS_DEV):
                slot[m, c] = 0
        sums = {}
        for p in range(parts):
            for m in range(inner_rows):
                for l in range(inner_slots):
                    slot[m, read(cols[p], starts[1 + p], m, l, inner_slots) - first] = l
            for i in span:
                for j in range(slots):
                    column = read(wanted, starts[0], i, j, slots)
                    for m in range(inner_rows):
                        l = slot[m, column - first]
                        hit = read(cols[p], starts[1 + p], m, l, inner_slots) == column
                        begin = pl.multiple_of((m * inner_slots + l) * block, block)
                        tile = tiles[p][pl.ds(begin, block), :]
                        right[i, m * block : (m + 1) * block, j * block : (j + 1) * block] = jnp.where(
                            hit, tile, jnp.zeros_like(tile)
                        )
            for i in span:
                left = jnp.concatenate(
                    [dense[i, place[1 + p] * inner_rows + m] for m in range(inner_rows)], axis=1
                )
                product = jnp.dot(left, right[i], preferred_element_type=jnp.float32)
                sums[i] = sums[i] + product if i in sums else product
        for at, i in enumerate(span):
            for j in range(slots):
                out[at, j] = sums[i][:, j * block : (j + 1) * block].astype(out.dtype)


def parity(k):
    return bin(k).count("1") % 2


def body(row_count, col_count, a_tiles, a_cols, b_tiles, b_cols, c_cols):
    rows, slots = c_cols.shape
    inner_rows = b_tiles.shape[0]
    block = a_tiles.shape[-1]
    dtype = b_tiles.dtype
    r, q = lax.axis_index("row"), lax.axis_index("col")
    first = q * COLS_DEV
    bits = sum((r >> k) & 1 for k in range(row_count.bit_length()))
    working = (bits + q) % 2 == 0

    def works(k, c):
        return parity(k) == c % 2

    def swap(x, axis, n, d):
        return lax.ppermute(x, axis, [(k, k ^ d) for k in range(n)])

    def permute(x, target):
        pairs = []
        for k in range(row_count):
            for c in range(col_count):
                to, at = target(k, c)
                pairs.append((k * col_count + c, to * col_count + at))
        return lax.ppermute(x, ("row", "col"), pairs)

    def deliver(x, d):
        def target(k, c):
            if parity(d):
                return (k, c ^ 1) if works(k, c) else (k ^ d, c)
            return (k ^ d, c) if works(k, c) else (k, c ^ (col_count // 2))

        return permute(x, target)

    def give_back(x):
        return permute(x, lambda k, c: (k ^ 1, c) if works(k, c) else (k, c ^ 1))

    def pack(tiles, *indices):
        size = tiles.size // block
        count = sum(x.size for x in indices)
        return pl.pallas_call(
            pack_kernel,
            out_shape=jax.ShapeDtypeStruct((size + -(-count // 16) * 16, block), dtype),
            in_specs=[SMEM] * len(indices) + [VMEM],
            out_specs=VMEM,
            compiler_params=PARAMS,
            cost_estimate=FREE,
        )(*indices, tiles.reshape(size, block))

    def index_of(packs, tiles):
        return jnp.stack([x[tiles.size // block :, 0] for x in packs]).astype(jnp.int32)

    def across(parts, d):
        while d:
            parts = parts + [swap(part, "col", col_count, d) for part in parts]
            d //= 2
        return parts

    far, end = col_count // 2, row_count - 1
    flat = b_tiles.reshape(-1, block)
    own, packed = pack(a_tiles, a_cols, c_cols), pack(b_tiles, b_cols)
    shards = {0: flat, end: deliver(flat, end)}
    cols = {0: (None, b_cols), end: (None, swap(b_cols, "row", row_count, end))}
    own_packs = [own, swap(own, "col", col_count, far)]
    other = swap(own, "row", row_count, 1)
    ready = lax.optimization_barrier((packed, own_packs[1]))[0]
    near = [swap(own, "col", col_count, d) for d in [far // 2] if d]
    for d in range(end - 1, 0, -1):
        if d == 1:
            ready = lax.optimization_barrier((ready, near))[0]
        shards[d] = deliver(ready, d)
    other = lax.optimization_barrier((other, shards[end]))[0]
    own_packs = own_packs + near + [swap(own_packs[1], "col", col_count, d) for d in [far // 2] if d]
    own_packs = across(own_packs, far // 4)
    other_packs = across([other], far)
    order, every = list(range(1, end)) + [0, end], list(range(rows))
    for d in range(1, end):
        cols[d] = (0, index_of([shards[d]], b_tiles))
    place = jnp.stack([jnp.where(working, first, -1)] + [r ^ d for d in order]).astype(jnp.int32)

    def products(wanted, packs, spans):
        index = index_of(packs, a_tiles)
        starts = [wanted[0]] + [cols[d][0] for d in order]
        return [
            pl.pallas_call(
                functools.partial(product_kernel, starts, span, len(order)),
                out_shape=jax.ShapeDtypeStruct((len(span), slots, block, block), dtype),
                in_specs=[SMEM] * (3 + len(order)) + [VMEM] * (len(order) + len(packs)),
                out_specs=VMEM,
                scratch_shapes=[
                    pltpu.VMEM((rows, inner_rows * row_count, block, block), dtype),
                    pltpu.VMEM((rows, inner_rows * block, slots * block), dtype),
                    pltpu.SMEM((inner_rows, COLS_DEV), jnp.int32),
                ],
                compiler_params=PARAMS,
                cost_estimate=FREE,
            )(place, index, wanted[1], *[cols[d][1] for d in order], *[shards[d] for d in order], *packs)
            for span in spans
        ]

    given = products((a_cols.size, index_of([other], a_tiles)), other_packs, [[i] for i in every])
    given = [give_back(x) for x in given]
    (kept,) = products((None, c_cols), own_packs, [every])
    return jnp.where(working, kept, jnp.concatenate(given, axis=0))


def solution(mesh):
    return jax.shard_map(
        functools.partial(body, mesh.shape["row"], mesh.shape["col"]),
        mesh=mesh,
        in_specs=(
            P(("groups", "row"), "col", None, None),
            P(("groups", "row"), "col"),
            P(("groups", "row"), "col", None, None),
            P(("groups", "row"), "col"),
            P(("groups", "row"), "col"),
        ),
        out_specs=P(("groups", "row"), "col", None, None),
        check_vma=False,
    )
```

```python
import functools

import jax
import jax.numpy as jnp
from jax import lax
from jax.experimental import pallas as pl
from jax.experimental.pallas import tpu as pltpu
from jax.sharding import PartitionSpec as P

COLS_DEV = 16

SMEM = pl.BlockSpec(memory_space=pltpu.SMEM)
VMEM = pl.BlockSpec(memory_space=pltpu.VMEM)
PARAMS = pltpu.CompilerParams(vmem_limit_bytes=32 * 2**20)
FREE = pl.CostEstimate(flops=1, bytes_accessed=1, transcendentals=0)


def pack_kernel(*refs):
    indices, tiles, out = refs[:-2], refs[-2], refs[-1]
    size = tiles.shape[0]
    out[:size, :] = tiles[...]
    row = lax.broadcasted_iota(jnp.int32, (out.shape[0] - size, out.shape[1]), 0)
    found = jnp.zeros(row.shape, jnp.float32)
    at = 0
    for index in indices:
        for i in range(index.shape[0]):
            for k in range(index.shape[1]):
                found = jnp.where(row == at, index[i, k].astype(jnp.float32), found)
                at += 1
    out[size:, :] = found.astype(out.dtype)


def product_kernel(starts, span, parts, place, left_index, wanted, *refs):
    cols, refs = refs[:parts], refs[parts:]
    tiles, refs = refs[:parts], refs[parts:]
    packs, (out, dense, right, slot) = refs[:-4], refs[-4:]

    @pl.when(place[0] >= 0)
    def _():
        first = place[0]
        inner_rows = slot.shape[0] // parts
        block = dense.shape[-1]
        slots = right.shape[3] // block
        inner_slots = tiles[0].shape[0] // block // inner_rows
        rows = right.shape[1]
        left_slots = (packs[0].shape[0] // block) // rows

        def read(ref, start, i, k, width):
            return ref[i, k] if start is None else ref[0, start + i * width + k]

        for i in span:
            dense[i] = jnp.zeros_like(dense[i])
            for p, pack in enumerate(packs):
                for s in range(left_slots):
                    inner = left_index[p, i * left_slots + s]
                    begin = (i * left_slots + s) * block

                    @pl.when(inner >= 0)
                    def _():
                        dense[i, inner] = pack[begin : begin + block, :]

        for p in range(parts):
            for m in range(inner_rows):
                for c in range(COLS_DEV):
                    slot[p * inner_rows + m, c] = -1
        for p in range(parts):
            for m in range(inner_rows):
                for l in range(inner_slots):
                    slot[p * inner_rows + m, read(cols[p], starts[1 + p], m, l, inner_slots) - first] = l
        sums = {}
        for p in range(parts):
            for i in span:
                for j in range(slots):
                    column = read(wanted, starts[0], i, j, slots) - first
                    for m in range(inner_rows):
                        l = slot[p * inner_rows + m, column]
                        begin = pl.multiple_of((m * inner_slots + jnp.maximum(l, 0)) * block, block)
                        tile = tiles[p][pl.ds(begin, block), :]
                        right[p % 2, i, m * block : (m + 1) * block, j * block : (j + 1) * block] = jnp.where(
                            l >= 0, tile, jnp.zeros_like(tile)
                        )
            for i in span:
                left = jnp.concatenate(
                    [dense[i, place[1 + p] * inner_rows + m] for m in range(inner_rows)], axis=1
                )
                product = jnp.dot(left, right[p % 2, i], preferred_element_type=jnp.float32)
                sums[i] = sums[i] + product if i in sums else product
        for at, i in enumerate(span):
            for j in range(slots):
                out[at, j] = sums[i][:, j * block : (j + 1) * block].astype(out.dtype)


def parity(k):
    return bin(k).count("1") % 2


def body(row_count, col_count, a_tiles, a_cols, b_tiles, b_cols, c_cols):
    rows, slots = c_cols.shape
    inner_rows = b_tiles.shape[0]
    block = a_tiles.shape[-1]
    dtype = b_tiles.dtype
    r, q = lax.axis_index("row"), lax.axis_index("col")
    first = q * COLS_DEV
    bits = sum((r >> k) & 1 for k in range(row_count.bit_length()))
    working = (bits + q) % 2 == 0

    def works(k, c):
        return parity(k) == c % 2

    def swap(x, axis, n, d):
        return lax.ppermute(x, axis, [(k, k ^ d) for k in range(n)])

    def permute(x, target):
        pairs = []
        for k in range(row_count):
            for c in range(col_count):
                to, at = target(k, c)
                pairs.append((k * col_count + c, to * col_count + at))
        return lax.ppermute(x, ("row", "col"), pairs)

    def deliver(x, d):
        def target(k, c):
            if parity(d):
                return (k, c ^ 1) if works(k, c) else (k ^ d, c)
            return (k ^ d, c) if works(k, c) else (k, c ^ (col_count // 2))

        return permute(x, target)

    def give_back(x):
        return permute(x, lambda k, c: (k ^ 1, c) if works(k, c) else (k, c ^ 1))

    def pack(tiles, *indices):
        size = tiles.size // block
        count = sum(x.size for x in indices)
        return pl.pallas_call(
            pack_kernel,
            out_shape=jax.ShapeDtypeStruct((size + -(-count // 16) * 16, block), dtype),
            in_specs=[SMEM] * len(indices) + [VMEM],
            out_specs=VMEM,
            compiler_params=PARAMS,
            cost_estimate=FREE,
        )(*indices, tiles.reshape(size, block))

    def index_of(packs, tiles):
        return jnp.stack([x[tiles.size // block :, 0] for x in packs]).astype(jnp.int32)

    def across(parts, d):
        while d:
            parts = parts + [swap(part, "col", col_count, d) for part in parts]
            d //= 2
        return parts

    far, end = col_count // 2, row_count - 1
    flat = b_tiles.reshape(-1, block)
    own, packed = pack(a_tiles, a_cols), pack(b_tiles, b_cols, c_cols)
    shards = {0: flat, end: deliver(flat, end)}
    cols = {0: (None, b_cols), end: (None, swap(b_cols, "row", row_count, end))}
    own_packs = [own, swap(own, "col", col_count, far)]
    other = swap(own, "row", row_count, 1)
    ready = lax.optimization_barrier((packed, own_packs[1]))[0]
    near = [swap(own, "col", col_count, d) for d in [far // 2] if d]
    for d in range(end - 1, 0, -1):
        if d == 1:
            ready = lax.optimization_barrier((ready, near))[0]
        shards[d] = deliver(ready, d)
    other = lax.optimization_barrier((other, shards[end]))[0]
    own_packs = own_packs + near + [swap(own_packs[1], "col", col_count, d) for d in [far // 2] if d]
    own_packs = across(own_packs, far // 4)
    other_packs = across([other], far)
    order, every = list(range(1, end)) + [0, end], list(range(rows))
    for d in range(1, end):
        cols[d] = (0, index_of([shards[d]], b_tiles))
    place = jnp.stack([jnp.where(working, first, -1)] + [r ^ d for d in order]).astype(jnp.int32)

    def products(wanted, packs, spans):
        index = index_of(packs, a_tiles)
        starts = [wanted[0]] + [cols[d][0] for d in order]
        return [
            pl.pallas_call(
                functools.partial(product_kernel, starts, span, len(order)),
                out_shape=jax.ShapeDtypeStruct((len(span), slots, block, block), dtype),
                in_specs=[SMEM] * (3 + len(order)) + [VMEM] * (len(order) + len(packs)),
                out_specs=VMEM,
                scratch_shapes=[
                    pltpu.VMEM((rows, inner_rows * row_count, block, block), dtype),
                    pltpu.VMEM((2, rows, inner_rows * block, slots * block), dtype),
                    pltpu.SMEM((len(order) * inner_rows, COLS_DEV), jnp.int32),
                ],
                compiler_params=PARAMS,
                cost_estimate=FREE,
            )(place, index, wanted[1], *[cols[d][1] for d in order], *[shards[d] for d in order], *packs)
            for span in spans
        ]

    given = products((b_cols.size, cols[1][1]), other_packs, [[i] for i in every])
    given = [give_back(x) for x in given]
    (kept,) = products((None, c_cols), own_packs, [every])
    return jnp.where(working, kept, jnp.concatenate(given, axis=0))


def solution(mesh):
    return jax.shard_map(
        functools.partial(body, mesh.shape["row"], mesh.shape["col"]),
        mesh=mesh,
        in_specs=(
            P(("groups", "row"), "col", None, None),
            P(("groups", "row"), "col"),
            P(("groups", "row"), "col", None, None),
            P(("groups", "row"), "col"),
            P(("groups", "row"), "col"),
        ),
        out_specs=P(("groups", "row"), "col", None, None),
        check_vma=False,
    )
```

```python
import functools

import jax
import jax.numpy as jnp
from jax import lax
from jax.experimental import pallas as pl
from jax.experimental.pallas import tpu as pltpu
from jax.sharding import PartitionSpec as P

COLS_DEV = 16

SMEM = pl.BlockSpec(memory_space=pltpu.SMEM)
VMEM = pl.BlockSpec(memory_space=pltpu.VMEM)
PARAMS = pltpu.CompilerParams(vmem_limit_bytes=32 * 2**20)
FREE = pl.CostEstimate(flops=1, bytes_accessed=1, transcendentals=0)


def pack_kernel(*refs):
    indices, tiles, out = refs[:-2], refs[-2], refs[-1]
    size = tiles.shape[0]
    out[:size, :] = tiles[...]
    row = lax.broadcasted_iota(jnp.int32, (out.shape[0] - size, out.shape[1]), 0)
    found = jnp.zeros(row.shape, jnp.float32)
    at = 0
    for index in indices:
        for i in range(index.shape[0]):
            for k in range(index.shape[1]):
                found = jnp.where(row == at, index[i, k].astype(jnp.float32), found)
                at += 1
    out[size:, :] = found.astype(out.dtype)


def product_kernel(starts, span, columns, parts, place, left_index, wanted, *refs):
    cols, refs = refs[:parts], refs[parts:]
    tiles, refs = refs[:parts], refs[parts:]
    packs, (out, dense, right, slot) = refs[:-4], refs[-4:]

    @pl.when(place[0] >= 0)
    def _():
        first = place[0]
        inner_rows = slot.shape[0]
        block = dense.shape[-1]
        slots = right.shape[2] // block
        inner_slots = tiles[0].shape[0] // block // inner_rows
        rows = right.shape[0]
        left_slots = (packs[0].shape[0] // block) // rows

        def read(ref, start, i, k, width):
            return ref[i, k] if start is None else ref[0, start + i * width + k]

        for i in span:
            dense[i] = jnp.zeros_like(dense[i])
            for p, pack in enumerate(packs):
                for s in range(left_slots):
                    inner = left_index[p, i * left_slots + s]
                    begin = (i * left_slots + s) * block

                    @pl.when(inner >= 0)
                    def _():
                        dense[i, inner] = pack[begin : begin + block, :]

        for m in range(inner_rows):
            for c in range(COLS_DEV):
                slot[m, c] = 0
        sums = {}
        for p in range(parts):
            for m in range(inner_rows):
                for l in range(inner_slots):
                    slot[m, read(cols[p], starts[1 + p], m, l, inner_slots) - first] = l
            for i in span:
                for at, j in enumerate(columns):
                    column = read(wanted, starts[0], i, j, slots)
                    for m in range(inner_rows):
                        l = slot[m, column - first]
                        hit = read(cols[p], starts[1 + p], m, l, inner_slots) == column
                        begin = pl.multiple_of((m * inner_slots + l) * block, block)
                        tile = tiles[p][pl.ds(begin, block), :]
                        right[i, m * block : (m + 1) * block, at * block : (at + 1) * block] = jnp.where(
                            hit, tile, jnp.zeros_like(tile)
                        )
            for i in span:
                left = jnp.concatenate(
                    [dense[i, place[1 + p] * inner_rows + m] for m in range(inner_rows)], axis=1
                )
                product = jnp.dot(left, right[i, :, : len(columns) * block], preferred_element_type=jnp.float32)
                sums[i] = sums[i] + product if i in sums else product
        for at, i in enumerate(span):
            for j in range(len(columns)):
                out[at, j] = sums[i][:, j * block : (j + 1) * block].astype(out.dtype)


def parity(k):
    return bin(k).count("1") % 2


def body(row_count, col_count, a_tiles, a_cols, b_tiles, b_cols, c_cols):
    rows, slots = c_cols.shape
    inner_rows = b_tiles.shape[0]
    block = a_tiles.shape[-1]
    dtype = b_tiles.dtype
    r, q = lax.axis_index("row"), lax.axis_index("col")
    first = q * COLS_DEV
    bits = sum((r >> k) & 1 for k in range(row_count.bit_length()))
    working = (bits + q) % 2 == 0

    def works(k, c):
        return parity(k) == c % 2

    def swap(x, axis, n, d):
        return lax.ppermute(x, axis, [(k, k ^ d) for k in range(n)])

    def permute(x, target):
        pairs = []
        for k in range(row_count):
            for c in range(col_count):
                to, at = target(k, c)
                pairs.append((k * col_count + c, to * col_count + at))
        return lax.ppermute(x, ("row", "col"), pairs)

    def deliver(x, d):
        def target(k, c):
            if parity(d):
                return (k, c ^ 1) if works(k, c) else (k ^ d, c)
            return (k ^ d, c) if works(k, c) else (k, c ^ (col_count // 2))

        return permute(x, target)

    def give_back(x):
        return permute(x, lambda k, c: (k ^ 1, c) if works(k, c) else (k, c ^ 1))

    def pack(tiles, *indices):
        size = tiles.size // block
        count = sum(x.size for x in indices)
        return pl.pallas_call(
            pack_kernel,
            out_shape=jax.ShapeDtypeStruct((size + -(-count // 16) * 16, block), dtype),
            in_specs=[SMEM] * len(indices) + [VMEM],
            out_specs=VMEM,
            compiler_params=PARAMS,
            cost_estimate=FREE,
        )(*indices, tiles.reshape(size, block))

    def index_of(packs, tiles):
        return jnp.stack([x[tiles.size // block :, 0] for x in packs]).astype(jnp.int32)

    def across(parts, d):
        while d:
            parts = parts + [swap(part, "col", col_count, d) for part in parts]
            d //= 2
        return parts

    far, end = col_count // 2, row_count - 1
    flat = b_tiles.reshape(-1, block)
    own, packed = pack(a_tiles, a_cols, c_cols), pack(b_tiles, b_cols)
    shards = {0: flat, end: deliver(flat, end)}
    cols = {0: (None, b_cols), end: (None, swap(b_cols, "row", row_count, end))}
    own_packs = [own, swap(own, "col", col_count, far)]
    other = swap(own, "row", row_count, 1)
    ready = lax.optimization_barrier((packed, own_packs[1]))[0]
    near = [swap(own, "col", col_count, d) for d in [far // 2] if d]
    for d in range(end - 1, 0, -1):
        if d == 1:
            ready = lax.optimization_barrier((ready, near))[0]
        shards[d] = deliver(ready, d)
    other = lax.optimization_barrier((other, shards[end]))[0]
    own_packs = own_packs + near + [swap(own_packs[1], "col", col_count, d) for d in [far // 2] if d]
    own_packs = across(own_packs, far // 4)
    other_packs = across([other], far)
    order, every = list(range(1, end)) + [0, end], list(range(rows))
    for d in range(1, end):
        cols[d] = (0, index_of([shards[d]], b_tiles))
    place = jnp.stack([jnp.where(working, first, -1)] + [r ^ d for d in order]).astype(jnp.int32)

    def products(wanted, packs, pieces):
        index = index_of(packs, a_tiles)
        starts = [wanted[0]] + [cols[d][0] for d in order]
        return [
            pl.pallas_call(
                functools.partial(product_kernel, starts, span, columns, len(order)),
                out_shape=jax.ShapeDtypeStruct((len(span), len(columns), block, block), dtype),
                in_specs=[SMEM] * (3 + len(order)) + [VMEM] * (len(order) + len(packs)),
                out_specs=VMEM,
                scratch_shapes=[
                    pltpu.VMEM((rows, inner_rows * row_count, block, block), dtype),
                    pltpu.VMEM((rows, inner_rows * block, slots * block), dtype),
                    pltpu.SMEM((inner_rows, COLS_DEV), jnp.int32),
                ],
                compiler_params=PARAMS,
                cost_estimate=FREE,
            )(place, index, wanted[1], *[cols[d][1] for d in order], *[shards[d] for d in order], *packs)
            for span, columns in pieces
        ]

    half = list(range(slots // 2)), list(range(slots // 2, slots))
    pieces = [([i], columns) for i in every for columns in half]
    given = products((a_cols.size, index_of([other], a_tiles)), other_packs, pieces)
    given = [give_back(x) for x in given]
    given = [jnp.concatenate(given[2 * i : 2 * i + 2], axis=1) for i in every]
    (kept,) = products((None, c_cols), own_packs, [(every, list(range(slots)))])
    return jnp.where(working, kept, jnp.concatenate(given, axis=0))


def solution(mesh):
    return jax.shard_map(
        functools.partial(body, mesh.shape["row"], mesh.shape["col"]),
        mesh=mesh,
        in_specs=(
            P(("groups", "row"), "col", None, None),
            P(("groups", "row"), "col"),
            P(("groups", "row"), "col", None, None),
            P(("groups", "row"), "col"),
            P(("groups", "row"), "col"),
        ),
        out_specs=P(("groups", "row"), "col", None, None),
        check_vma=False,
    )
```

```python
import functools

import jax
import jax.numpy as jnp
from jax import lax
from jax.experimental import pallas as pl
from jax.experimental.pallas import tpu as pltpu
from jax.sharding import PartitionSpec as P

COLS_DEV = 16

SMEM = pl.BlockSpec(memory_space=pltpu.SMEM)
VMEM = pl.BlockSpec(memory_space=pltpu.VMEM)
PARAMS = pltpu.CompilerParams(vmem_limit_bytes=32 * 2**20)
FREE = pl.CostEstimate(flops=1, bytes_accessed=1, transcendentals=0)


def pack_kernel(*refs):
    indices, tiles, out = refs[:-2], refs[-2], refs[-1]
    size = tiles.shape[0]
    out[:size, :] = tiles[...]
    row = lax.broadcasted_iota(jnp.int32, (out.shape[0] - size, out.shape[1]), 0)
    found = jnp.zeros(row.shape, jnp.float32)
    at = 0
    for index in indices:
        for i in range(index.shape[0]):
            for k in range(index.shape[1]):
                found = jnp.where(row == at, index[i, k].astype(jnp.float32), found)
                at += 1
    out[size:, :] = found.astype(out.dtype)


def product_kernel(starts, span, which, place, left_index, wanted, *refs):
    parts, arrays = len(which), max(which) + 1
    cols, refs = [refs[k] for k in which], refs[arrays:]
    tiles, refs = refs[:parts], refs[parts:]
    packs, (out, dense, right, slot) = refs[:-4], refs[-4:]

    @pl.when(place[0] >= 0)
    def _():
        first = place[0]
        inner_rows = slot.shape[0]
        block = dense.shape[-1]
        slots = right.shape[2] // block
        inner_slots = tiles[0].shape[0] // block // inner_rows
        rows = right.shape[0]
        left_slots = (packs[0].shape[0] // block) // rows
        spare = dense.shape[1] - 1

        def read(ref, start, i, k, width):
            return ref[i, k] if start is None else ref[start[0], start[1] + i * width + k]

        for i in span:
            dense[i] = jnp.zeros_like(dense[i])
            for p, pack in enumerate(packs):
                for s in range(left_slots):
                    inner = left_index[p, i * left_slots + s]
                    begin = (i * left_slots + s) * block
                    dense[i, jnp.where(inner >= 0, inner, spare)] = pack[begin : begin + block, :]

        for m in range(inner_rows):
            for c in range(COLS_DEV):
                slot[m, c] = 0
        sums = {}
        for p in range(parts):
            for m in range(inner_rows):
                for l in range(inner_slots):
                    slot[m, read(cols[p], starts[1 + p], m, l, inner_slots) - first] = l
            for i in span:
                for j in range(slots):
                    column = read(wanted, starts[0], i, j, slots)
                    for m in range(inner_rows):
                        l = slot[m, column - first]
                        hit = read(cols[p], starts[1 + p], m, l, inner_slots) == column
                        begin = pl.multiple_of((m * inner_slots + l) * block, block)
                        tile = tiles[p][pl.ds(begin, block), :]
                        right[i, m * block : (m + 1) * block, j * block : (j + 1) * block] = jnp.where(
                            hit, tile, jnp.zeros_like(tile)
                        )
            for i in span:
                left = jnp.concatenate(
                    [dense[i, place[1 + p] * inner_rows + m] for m in range(inner_rows)], axis=1
                )
                product = jnp.dot(left, right[i], preferred_element_type=jnp.float32)
                sums[i] = sums[i] + product if i in sums else product
        for at, i in enumerate(span):
            for j in range(slots):
                out[at, j] = sums[i][:, j * block : (j + 1) * block].astype(out.dtype)


def parity(k):
    return bin(k).count("1") % 2


def body(row_count, col_count, a_tiles, a_cols, b_tiles, b_cols, c_cols):
    rows, slots = c_cols.shape
    inner_rows = b_tiles.shape[0]
    block = a_tiles.shape[-1]
    dtype = b_tiles.dtype
    r, q = lax.axis_index("row"), lax.axis_index("col")
    first = q * COLS_DEV
    bits = sum((r >> k) & 1 for k in range(row_count.bit_length()))
    working = (bits + q) % 2 == 0

    def works(k, c):
        return parity(k) == c % 2

    def swap(x, axis, n, d):
        return lax.ppermute(x, axis, [(k, k ^ d) for k in range(n)])

    def permute(x, target):
        pairs = []
        for k in range(row_count):
            for c in range(col_count):
                to, at = target(k, c)
                pairs.append((k * col_count + c, to * col_count + at))
        return lax.ppermute(x, ("row", "col"), pairs)

    def deliver(x, d):
        def target(k, c):
            if parity(d):
                return (k, c ^ 1) if works(k, c) else (k ^ d, c)
            return (k ^ d, c) if works(k, c) else (k, c ^ (col_count // 2))

        return permute(x, target)

    def give_back(x):
        return permute(x, lambda k, c: (k ^ 1, c) if works(k, c) else (k, c ^ 1))

    def pack(tiles, *indices):
        size = tiles.size // block
        count = sum(x.size for x in indices)
        return pl.pallas_call(
            pack_kernel,
            out_shape=jax.ShapeDtypeStruct((size + -(-count // 16) * 16, block), dtype),
            in_specs=[SMEM] * len(indices) + [VMEM],
            out_specs=VMEM,
            compiler_params=PARAMS,
            cost_estimate=FREE,
        )(*indices, tiles.reshape(size, block))

    def index_of(packs, tiles):
        return jnp.stack([x[tiles.size // block :, 0] for x in packs]).astype(jnp.int32)

    def across(parts, d):
        while d:
            parts = parts + [swap(part, "col", col_count, d) for part in parts]
            d //= 2
        return parts

    far, end = col_count // 2, row_count - 1
    flat = b_tiles.reshape(-1, block)
    own, packed = pack(a_tiles, a_cols, c_cols), pack(b_tiles, b_cols)
    shards = {0: flat, end: deliver(flat, end)}
    cols = {0: (None, b_cols), end: (None, swap(b_cols, "row", row_count, end))}
    own_packs = [own, swap(own, "col", col_count, far)]
    other = swap(own, "row", row_count, 1)
    ready = lax.optimization_barrier((packed, own_packs[1]))[0]
    near = [swap(own, "col", col_count, d) for d in [far // 2] if d]
    for d in range(end - 1, 0, -1):
        if d == 1:
            ready = lax.optimization_barrier((ready, near))[0]
        shards[d] = deliver(ready, d)
    other = lax.optimization_barrier((other, shards[end]))[0]
    own_packs = own_packs + near + [swap(own_packs[1], "col", col_count, d) for d in [far // 2] if d]
    own_packs = across(own_packs, far // 4)
    other_packs = across([other], far)
    order, every = list(range(1, end)) + [0, end], list(range(rows))
    behind = index_of([shards[d] for d in range(1, end)], b_tiles)
    for d in range(1, end):
        cols[d] = ((d - 1, 0), behind)
    place = jnp.stack([jnp.where(working, first, -1)] + [r ^ d for d in order]).astype(jnp.int32)

    def products(wanted, packs, spans):
        index = index_of(packs, a_tiles)
        starts = [wanted[0]] + [cols[d][0] for d in order]
        arrays = [b_cols, cols[end][1]] + ([behind] if end > 1 else [])
        which = [{0: 0, end: 1}.get(d, 2) for d in order]
        return [
            pl.pallas_call(
                functools.partial(product_kernel, starts, span, which),
                out_shape=jax.ShapeDtypeStruct((len(span), slots, block, block), dtype),
                in_specs=[SMEM] * (3 + len(arrays)) + [VMEM] * (len(order) + len(packs)),
                out_specs=VMEM,
                scratch_shapes=[
                    pltpu.VMEM((rows, inner_rows * row_count + 1, block, block), dtype),
                    pltpu.VMEM((rows, inner_rows * block, slots * block), dtype),
                    pltpu.SMEM((inner_rows, COLS_DEV), jnp.int32),
                ],
                compiler_params=PARAMS,
                cost_estimate=FREE,
            )(place, index, wanted[1], *arrays, *[shards[d] for d in order], *packs)
            for span in spans
        ]

    given = products(((0, a_cols.size), index_of([other], a_tiles)), other_packs, [[i] for i in every])
    given = [give_back(x) for x in given]
    (kept,) = products((None, c_cols), own_packs, [every])
    return jnp.where(working, kept, jnp.concatenate(given, axis=0))


def solution(mesh):
    return jax.shard_map(
        functools.partial(body, mesh.shape["row"], mesh.shape["col"]),
        mesh=mesh,
        in_specs=(
            P(("groups", "row"), "col", None, None),
            P(("groups", "row"), "col"),
            P(("groups", "row"), "col", None, None),
            P(("groups", "row"), "col"),
            P(("groups", "row"), "col"),
        ),
        out_specs=P(("groups", "row"), "col", None, None),
        check_vma=False,
    )
```

```python
import functools

import jax
import jax.numpy as jnp
from jax import lax
from jax.experimental import pallas as pl
from jax.experimental.pallas import tpu as pltpu
from jax.sharding import PartitionSpec as P

COLS_DEV = 16

SMEM = pl.BlockSpec(memory_space=pltpu.SMEM)
VMEM = pl.BlockSpec(memory_space=pltpu.VMEM)
PARAMS = pltpu.CompilerParams(vmem_limit_bytes=32 * 2**20)
FREE = pl.CostEstimate(flops=1, bytes_accessed=1, transcendentals=0)


def pack_kernel(*refs):
    indices, tiles, out = refs[:-2], refs[-2], refs[-1]
    size = tiles.shape[0]
    out[:size, :] = tiles[...]
    row = lax.broadcasted_iota(jnp.int32, (out.shape[0] - size, out.shape[1]), 0)
    found = jnp.zeros(row.shape, jnp.float32)
    at = 0
    for index in indices:
        for i in range(index.shape[0]):
            for k in range(index.shape[1]):
                found = jnp.where(row == at, index[i, k].astype(jnp.float32), found)
                at += 1
    out[size:, :] = found.astype(out.dtype)


def product_kernel(starts, span, which, place, left_index, *refs):
    parts, arrays = len(which), max(which) + 1
    cols, refs = [refs[k] for k in which], refs[arrays:]
    tiles, refs = refs[:parts], refs[parts:]
    packs, (out, dense, right, slot) = refs[:-4], refs[-4:]

    @pl.when(place[0] >= 0)
    def _():
        first = place[0]
        inner_rows = slot.shape[0]
        block = dense.shape[-1]
        slots = right.shape[2] // block
        inner_slots = tiles[0].shape[0] // block // inner_rows
        rows = right.shape[0]
        left_slots = (packs[0].shape[0] // block) // rows
        spare = dense.shape[1] - 1

        def read(ref, start, i, k, width):
            return ref[i, k] if start is None else ref[start[0], start[1] + i * width + k]

        for i in span:
            dense[i] = jnp.zeros_like(dense[i])
            for p, pack in enumerate(packs):
                for s in range(left_slots):
                    inner = left_index[p, i * left_slots + s]
                    begin = (i * left_slots + s) * block
                    dense[i, jnp.where(inner >= 0, inner, spare)] = pack[begin : begin + block, :]

        for m in range(inner_rows):
            for c in range(COLS_DEV):
                slot[m, c] = 0
        sums = {}
        for p in range(parts):
            for m in range(inner_rows):
                for l in range(inner_slots):
                    slot[m, read(cols[p], starts[1 + p], m, l, inner_slots) - first] = l
            for i in span:
                for j in range(slots):
                    column = read(left_index, starts[0], i, j, slots)
                    for m in range(inner_rows):
                        l = slot[m, column - first]
                        hit = read(cols[p], starts[1 + p], m, l, inner_slots) == column
                        begin = pl.multiple_of((m * inner_slots + l) * block, block)
                        tile = tiles[p][pl.ds(begin, block), :]
                        right[i, m * block : (m + 1) * block, j * block : (j + 1) * block] = jnp.where(
                            hit, tile, jnp.zeros_like(tile)
                        )
            for i in span:
                left = jnp.concatenate(
                    [dense[i, place[1 + p] * inner_rows + m] for m in range(inner_rows)], axis=1
                )
                product = jnp.dot(left, right[i], preferred_element_type=jnp.float32)
                sums[i] = sums[i] + product if i in sums else product
        for at, i in enumerate(span):
            for j in range(slots):
                out[at, j] = sums[i][:, j * block : (j + 1) * block].astype(out.dtype)


def parity(k):
    return bin(k).count("1") % 2


def body(row_count, col_count, a_tiles, a_cols, b_tiles, b_cols, c_cols):
    rows, slots = c_cols.shape
    inner_rows = b_tiles.shape[0]
    block = a_tiles.shape[-1]
    dtype = b_tiles.dtype
    r, q = lax.axis_index("row"), lax.axis_index("col")
    first = q * COLS_DEV
    bits = sum((r >> k) & 1 for k in range(row_count.bit_length()))
    working = (bits + q) % 2 == 0

    def works(k, c):
        return parity(k) == c % 2

    def swap(x, axis, n, d):
        return lax.ppermute(x, axis, [(k, k ^ d) for k in range(n)])

    def permute(x, target):
        pairs = []
        for k in range(row_count):
            for c in range(col_count):
                to, at = target(k, c)
                pairs.append((k * col_count + c, to * col_count + at))
        return lax.ppermute(x, ("row", "col"), pairs)

    def deliver(x, d):
        def target(k, c):
            if parity(d):
                return (k, c ^ 1) if works(k, c) else (k ^ d, c)
            return (k ^ d, c) if works(k, c) else (k, c ^ (col_count // 2))

        return permute(x, target)

    def give_back(x):
        return permute(x, lambda k, c: (k ^ 1, c) if works(k, c) else (k, c ^ 1))

    def pack(tiles, *indices):
        size = tiles.size // block
        count = sum(x.size for x in indices)
        return pl.pallas_call(
            pack_kernel,
            out_shape=jax.ShapeDtypeStruct((size + -(-count // 16) * 16, block), dtype),
            in_specs=[SMEM] * len(indices) + [VMEM],
            out_specs=VMEM,
            compiler_params=PARAMS,
            cost_estimate=FREE,
        )(*indices, tiles.reshape(size, block))

    def index_of(packs, tiles):
        return jnp.stack([x[tiles.size // block :, 0] for x in packs]).astype(jnp.int32)

    def across(parts, d):
        while d:
            parts = parts + [swap(part, "col", col_count, d) for part in parts]
            d //= 2
        return parts

    far, end = col_count // 2, row_count - 1
    flat = b_tiles.reshape(-1, block)
    own, packed = pack(a_tiles, a_cols, c_cols), pack(b_tiles, b_cols)
    shards = {0: flat, end: deliver(flat, end)}
    cols = {0: (None, b_cols), end: (None, swap(b_cols, "row", row_count, end))}
    own_packs = [own, swap(own, "col", col_count, far)]
    other = swap(own, "row", row_count, 1)
    ready = lax.optimization_barrier((packed, own_packs[1]))[0]
    near = [swap(own, "col", col_count, d) for d in [far // 2] if d]
    for d in range(end - 1, 0, -1):
        if d == 1:
            ready = lax.optimization_barrier((ready, near))[0]
        shards[d] = deliver(ready, d)
    other = lax.optimization_barrier((other, shards[end]))[0]
    own_packs = own_packs + near + [swap(own_packs[1], "col", col_count, d) for d in [far // 2] if d]
    own_packs = across(own_packs, far // 4)
    other_packs = across([other], far)
    order, every = list(range(1, end)) + [0, end], list(range(rows))
    behind = index_of([shards[d] for d in range(1, end)], b_tiles)
    for d in range(1, end):
        cols[d] = ((d - 1, 0), behind)
    place = jnp.stack([jnp.where(working, first, -1)] + [r ^ d for d in order]).astype(jnp.int32)

    def products(packs, spans):
        index = index_of(packs, a_tiles)
        starts = [(0, a_cols.size)] + [cols[d][0] for d in order]
        arrays = [b_cols, cols[end][1]] + ([behind] if end > 1 else [])
        which = [{0: 0, end: 1}.get(d, 2) for d in order]
        return [
            pl.pallas_call(
                functools.partial(product_kernel, starts, span, which),
                out_shape=jax.ShapeDtypeStruct((len(span), slots, block, block), dtype),
                in_specs=[SMEM] * (2 + len(arrays)) + [VMEM] * (len(order) + len(packs)),
                out_specs=VMEM,
                scratch_shapes=[
                    pltpu.VMEM((rows, inner_rows * row_count + 1, block, block), dtype),
                    pltpu.VMEM((rows, inner_rows * block, slots * block), dtype),
                    pltpu.SMEM((inner_rows, COLS_DEV), jnp.int32),
                ],
                compiler_params=PARAMS,
                cost_estimate=FREE,
            )(place, index, *arrays, *[shards[d] for d in order], *packs)
            for span in spans
        ]

    given = products(other_packs, [[i] for i in every])
    given = [give_back(x) for x in given]
    (kept,) = products(own_packs, [every])
    return jnp.where(working, kept, jnp.concatenate(given, axis=0))


def solution(mesh):
    return jax.shard_map(
        functools.partial(body, mesh.shape["row"], mesh.shape["col"]),
        mesh=mesh,
        in_specs=(
            P(("groups", "row"), "col", None, None),
            P(("groups", "row"), "col"),
            P(("groups", "row"), "col", None, None),
            P(("groups", "row"), "col"),
            P(("groups", "row"), "col"),
        ),
        out_specs=P(("groups", "row"), "col", None, None),
        check_vma=False,
    )
```

```python
import functools

import jax
import jax.numpy as jnp
from jax import lax
from jax.experimental import pallas as pl
from jax.experimental.pallas import tpu as pltpu
from jax.sharding import PartitionSpec as P

COLS_DEV = 16

SMEM = pl.BlockSpec(memory_space=pltpu.SMEM)
VMEM = pl.BlockSpec(memory_space=pltpu.VMEM)
PARAMS = pltpu.CompilerParams(vmem_limit_bytes=32 * 2**20)
FREE = pl.CostEstimate(flops=1, bytes_accessed=1, transcendentals=0)


def pack_kernel(*refs):
    indices, tiles, out = refs[:-2], refs[-2], refs[-1]
    size = tiles.shape[0]
    out[:size, :] = tiles[...]
    row = lax.broadcasted_iota(jnp.int32, (out.shape[0] - size, out.shape[1]), 0)
    found = jnp.zeros(row.shape, jnp.float32)
    at = 0
    for index in indices:
        for i in range(index.shape[0]):
            for k in range(index.shape[1]):
                found = jnp.where(row == at, index[i, k].astype(jnp.float32), found)
                at += 1
    out[size:, :] = found.astype(out.dtype)


def product_kernel(starts, span, which, place, left_index, *refs):
    parts, arrays = len(which), max(which) + 1
    cols, refs = [refs[k] for k in which], refs[arrays:]
    tiles, refs = refs[:parts], refs[parts:]
    packs, (out, dense, right, slot) = refs[:-4], refs[-4:]

    @pl.when(place[0] >= 0)
    def _():
        first = place[0]
        inner_rows = slot.shape[0]
        block = dense.shape[-1]
        slots = right.shape[2] // block
        inner_slots = tiles[0].shape[0] // block // inner_rows
        rows = right.shape[0]
        left_slots = (packs[0].shape[0] // block) // rows
        spare = dense.shape[1] - 1

        def read(ref, start, i, k, width):
            return ref[i, k] if start is None else ref[start[0], start[1] + i * width + k]

        for i in span:
            dense[i] = jnp.zeros_like(dense[i])
            for p, pack in enumerate(packs):
                for s in range(left_slots):
                    inner = left_index[p, i * left_slots + s]
                    begin = (i * left_slots + s) * block
                    dense[i, jnp.where(inner >= 0, inner, spare)] = pack[begin : begin + block, :]

        for m in range(inner_rows):
            for c in range(COLS_DEV):
                slot[m, c] = 0
        sums = {}
        for p in range(parts):
            for m in range(inner_rows):
                for l in range(inner_slots):
                    slot[m, read(cols[p], starts[1 + p], m, l, inner_slots) - first] = l
            for i in span:
                for j in range(slots):
                    column = read(left_index, starts[0], i, j, slots)
                    for m in range(inner_rows):
                        l = slot[m, column - first]
                        hit = read(cols[p], starts[1 + p], m, l, inner_slots) == column
                        begin = pl.multiple_of((m * inner_slots + l) * block, block)
                        tile = tiles[p][pl.ds(begin, block), :]
                        right[i, m * block : (m + 1) * block, j * block : (j + 1) * block] = jnp.where(
                            hit, tile, jnp.zeros_like(tile)
                        )
            for i in span:
                left = jnp.concatenate(
                    [dense[i, place[1 + p] * inner_rows + m] for m in range(inner_rows)], axis=1
                )
                product = jnp.dot(left, right[i], preferred_element_type=jnp.float32)
                sums[i] = sums[i] + product if i in sums else product
        for at, i in enumerate(span):
            for j in range(slots):
                out[at, j] = sums[i][:, j * block : (j + 1) * block].astype(out.dtype)


def choose_kernel(place, kept, *refs):
    given, out, sems = refs[:-2], refs[-2], refs[-1]

    @pl.when(place[0] >= 0)
    def _():
        copy = pltpu.make_async_copy(kept, out, sems.at[0])
        copy.start()
        copy.wait()

    @pl.when(place[0] < 0)
    def _():
        copies = [pltpu.make_async_copy(x, out.at[i : i + 1], sems.at[i]) for i, x in enumerate(given)]
        for copy in copies:
            copy.start()
        for copy in copies:
            copy.wait()


def parity(k):
    return bin(k).count("1") % 2


def body(row_count, col_count, a_tiles, a_cols, b_tiles, b_cols, c_cols):
    rows, slots = c_cols.shape
    inner_rows = b_tiles.shape[0]
    block = a_tiles.shape[-1]
    dtype = b_tiles.dtype
    r, q = lax.axis_index("row"), lax.axis_index("col")
    first = q * COLS_DEV
    bits = sum((r >> k) & 1 for k in range(row_count.bit_length()))
    working = (bits + q) % 2 == 0

    def works(k, c):
        return parity(k) == c % 2

    def swap(x, axis, n, d):
        return lax.ppermute(x, axis, [(k, k ^ d) for k in range(n)])

    def permute(x, target):
        pairs = []
        for k in range(row_count):
            for c in range(col_count):
                to, at = target(k, c)
                pairs.append((k * col_count + c, to * col_count + at))
        return lax.ppermute(x, ("row", "col"), pairs)

    def deliver(x, d):
        def target(k, c):
            if parity(d):
                return (k, c ^ 1) if works(k, c) else (k ^ d, c)
            return (k ^ d, c) if works(k, c) else (k, c ^ (col_count // 2))

        return permute(x, target)

    def give_back(x):
        return permute(x, lambda k, c: (k ^ 1, c) if works(k, c) else (k, c ^ 1))

    def pack(tiles, *indices):
        size = tiles.size // block
        count = sum(x.size for x in indices)
        return pl.pallas_call(
            pack_kernel,
            out_shape=jax.ShapeDtypeStruct((size + -(-count // 16) * 16, block), dtype),
            in_specs=[SMEM] * len(indices) + [VMEM],
            out_specs=VMEM,
            compiler_params=PARAMS,
            cost_estimate=FREE,
        )(*indices, tiles.reshape(size, block))

    def index_of(packs, tiles):
        return jnp.stack([x[tiles.size // block :, 0] for x in packs]).astype(jnp.int32)

    def across(parts, d):
        while d:
            parts = parts + [swap(part, "col", col_count, d) for part in parts]
            d //= 2
        return parts

    far, end = col_count // 2, row_count - 1
    flat = b_tiles.reshape(-1, block)
    own, packed = pack(a_tiles, a_cols, c_cols), pack(b_tiles, b_cols)
    shards = {0: flat, end: deliver(flat, end)}
    cols = {0: (None, b_cols), end: (None, swap(b_cols, "row", row_count, end))}
    own_packs = [own, swap(own, "col", col_count, far)]
    other = swap(own, "row", row_count, 1)
    ready = lax.optimization_barrier((packed, own_packs[1]))[0]
    near = [swap(own, "col", col_count, d) for d in [far // 2] if d]
    for d in range(end - 1, 0, -1):
        if d == 1:
            ready = lax.optimization_barrier((ready, near))[0]
        shards[d] = deliver(ready, d)
    other = lax.optimization_barrier((other, shards[end]))[0]
    own_packs = own_packs + near + [swap(own_packs[1], "col", col_count, d) for d in [far // 2] if d]
    own_packs = across(own_packs, far // 4)
    other_packs = across([other], far)
    order, every = list(range(1, end)) + [0, end], list(range(rows))
    behind = index_of([shards[d] for d in range(1, end)], b_tiles)
    for d in range(1, end):
        cols[d] = ((d - 1, 0), behind)
    place = jnp.stack([jnp.where(working, first, -1)] + [r ^ d for d in order]).astype(jnp.int32)

    def products(packs, spans):
        index = index_of(packs, a_tiles)
        starts = [(0, a_cols.size)] + [cols[d][0] for d in order]
        arrays = [b_cols, cols[end][1]] + ([behind] if end > 1 else [])
        which = [{0: 0, end: 1}.get(d, 2) for d in order]
        return [
            pl.pallas_call(
                functools.partial(product_kernel, starts, span, which),
                out_shape=jax.ShapeDtypeStruct((len(span), slots, block, block), dtype),
                in_specs=[SMEM] * (2 + len(arrays)) + [VMEM] * (len(order) + len(packs)),
                out_specs=VMEM,
                scratch_shapes=[
                    pltpu.VMEM((rows, inner_rows * row_count + 1, block, block), dtype),
                    pltpu.VMEM((rows, inner_rows * block, slots * block), dtype),
                    pltpu.SMEM((inner_rows, COLS_DEV), jnp.int32),
                ],
                compiler_params=PARAMS,
                cost_estimate=FREE,
            )(place, index, *arrays, *[shards[d] for d in order], *packs)
            for span in spans
        ]

    given = products(other_packs, [[i] for i in every])
    given = [give_back(x) for x in given]
    (kept,) = products(own_packs, [every])
    return pl.pallas_call(
        choose_kernel,
        out_shape=jax.ShapeDtypeStruct((rows, slots, block, block), dtype),
        in_specs=[SMEM] + [VMEM] * (1 + rows),
        out_specs=pl.BlockSpec(memory_space=pl.ANY),
        scratch_shapes=[pltpu.SemaphoreType.DMA((rows,))],
        compiler_params=PARAMS,
        cost_estimate=FREE,
    )(place, kept, *given)


def solution(mesh):
    return jax.shard_map(
        functools.partial(body, mesh.shape["row"], mesh.shape["col"]),
        mesh=mesh,
        in_specs=(
            P(("groups", "row"), "col", None, None),
            P(("groups", "row"), "col"),
            P(("groups", "row"), "col", None, None),
            P(("groups", "row"), "col"),
            P(("groups", "row"), "col"),
        ),
        out_specs=P(("groups", "row"), "col", None, None),
        check_vma=False,
    )
```

```python
import functools

import jax
import jax.numpy as jnp
from jax import lax
from jax.experimental import pallas as pl
from jax.experimental.pallas import tpu as pltpu
from jax.sharding import PartitionSpec as P

COLS_DEV = 16

SMEM = pl.BlockSpec(memory_space=pltpu.SMEM)
VMEM = pl.BlockSpec(memory_space=pltpu.VMEM)
PARAMS = pltpu.CompilerParams(vmem_limit_bytes=32 * 2**20)
FREE = pl.CostEstimate(flops=1, bytes_accessed=1, transcendentals=0)


def pack_kernel(*refs):
    indices, tiles, out = refs[:-2], refs[-2], refs[-1]
    size = tiles.shape[0]
    out[:size, :] = tiles[...]
    row = lax.broadcasted_iota(jnp.int32, (out.shape[0] - size, out.shape[1]), 0)
    found = jnp.zeros(row.shape, jnp.float32)
    at = 0
    for index in indices:
        for i in range(index.shape[0]):
            for k in range(index.shape[1]):
                found = jnp.where(row == at, index[i, k].astype(jnp.float32), found)
                at += 1
    out[size:, :] = found.astype(out.dtype)


def product_kernel(starts, span, which, place, left_index, *refs):
    parts, arrays = len(which), max(which) + 1
    cols, refs = [refs[k] for k in which], refs[arrays:]
    tiles, refs = refs[:parts], refs[parts:]
    packs, (out, dense, right, slot) = refs[:-4], refs[-4:]

    @pl.when(place[0] >= 0)
    def _():
        first = place[0]
        inner_rows = slot.shape[0]
        block = dense.shape[-1]
        slots = right.shape[2] // block
        inner_slots = tiles[0].shape[0] // block // inner_rows
        rows = right.shape[0]
        left_slots = (packs[0].shape[0] // block) // rows
        spare = dense.shape[1] - 1

        def read(ref, start, i, k, width):
            return ref[i, k] if start is None else ref[start[0], start[1] + i * width + k]

        for i in span:
            dense[i] = jnp.zeros_like(dense[i])
            for p, pack in enumerate(packs):
                for s in range(left_slots):
                    inner = left_index[p, i * left_slots + s]
                    begin = (i * left_slots + s) * block
                    dense[i, jnp.where(inner >= 0, inner, spare)] = pack[begin : begin + block, :]

        for m in range(inner_rows):
            for c in range(COLS_DEV):
                slot[m, c] = 0
        sums = {}
        for p in range(parts):
            for m in range(inner_rows):
                for l in range(inner_slots):
                    slot[m, read(cols[p], starts[1 + p], m, l, inner_slots) - first] = l
            for i in span:
                for j in range(slots):
                    column = read(left_index, starts[0], i, j, slots)
                    for m in range(inner_rows):
                        l = slot[m, column - first]
                        hit = read(cols[p], starts[1 + p], m, l, inner_slots) == column
                        begin = pl.multiple_of((m * inner_slots + l) * block, block)
                        tile = tiles[p][pl.ds(begin, block), :]
                        right[i, (p % 4 * inner_rows + m) * block : (p % 4 * inner_rows + m + 1) * block, j * block : (j + 1) * block] = jnp.where(
                            hit, tile, jnp.zeros_like(tile)
                        )
            if p % 4 != 3 and p + 1 < parts:
                continue
            held = range(p - p % 4, p + 1)
            for i in span:
                left = jnp.concatenate(
                    [dense[i, place[1 + h] * inner_rows + m] for h in held for m in range(inner_rows)], axis=1
                )
                product = jnp.dot(
                    left, right[i, : len(held) * inner_rows * block], preferred_element_type=jnp.float32
                )
                sums[i] = sums[i] + product if i in sums else product
        for at, i in enumerate(span):
            for j in range(slots):
                out[at, j] = sums[i][:, j * block : (j + 1) * block].astype(out.dtype)


def parity(k):
    return bin(k).count("1") % 2


def body(row_count, col_count, a_tiles, a_cols, b_tiles, b_cols, c_cols):
    rows, slots = c_cols.shape
    inner_rows = b_tiles.shape[0]
    block = a_tiles.shape[-1]
    dtype = b_tiles.dtype
    r, q = lax.axis_index("row"), lax.axis_index("col")
    first = q * COLS_DEV
    bits = sum((r >> k) & 1 for k in range(row_count.bit_length()))
    working = (bits + q) % 2 == 0

    def works(k, c):
        return parity(k) == c % 2

    def swap(x, axis, n, d):
        return lax.ppermute(x, axis, [(k, k ^ d) for k in range(n)])

    def permute(x, target):
        pairs = []
        for k in range(row_count):
            for c in range(col_count):
                to, at = target(k, c)
                pairs.append((k * col_count + c, to * col_count + at))
        return lax.ppermute(x, ("row", "col"), pairs)

    def deliver(x, d):
        def target(k, c):
            if parity(d):
                return (k, c ^ 1) if works(k, c) else (k ^ d, c)
            return (k ^ d, c) if works(k, c) else (k, c ^ (col_count // 2))

        return permute(x, target)

    def give_back(x):
        return permute(x, lambda k, c: (k ^ 1, c) if works(k, c) else (k, c ^ 1))

    def pack(tiles, *indices):
        size = tiles.size // block
        count = sum(x.size for x in indices)
        return pl.pallas_call(
            pack_kernel,
            out_shape=jax.ShapeDtypeStruct((size + -(-count // 16) * 16, block), dtype),
            in_specs=[SMEM] * len(indices) + [VMEM],
            out_specs=VMEM,
            compiler_params=PARAMS,
            cost_estimate=FREE,
        )(*indices, tiles.reshape(size, block))

    def index_of(packs, tiles):
        return jnp.stack([x[tiles.size // block :, 0] for x in packs]).astype(jnp.int32)

    def across(parts, d):
        while d:
            parts = parts + [swap(part, "col", col_count, d) for part in parts]
            d //= 2
        return parts

    far, end = col_count // 2, row_count - 1
    flat = b_tiles.reshape(-1, block)
    own, packed = pack(a_tiles, a_cols, c_cols), pack(b_tiles, b_cols)
    shards = {0: flat, end: deliver(flat, end)}
    cols = {0: (None, b_cols), end: (None, swap(b_cols, "row", row_count, end))}
    own_packs = [own, swap(own, "col", col_count, far)]
    other = swap(own, "row", row_count, 1)
    ready = lax.optimization_barrier((packed, own_packs[1]))[0]
    near = [swap(own, "col", col_count, d) for d in [far // 2] if d]
    for d in range(end - 1, 0, -1):
        if d == 1:
            ready = lax.optimization_barrier((ready, near))[0]
        shards[d] = deliver(ready, d)
    other = lax.optimization_barrier((other, shards[end]))[0]
    own_packs = own_packs + near + [swap(own_packs[1], "col", col_count, d) for d in [far // 2] if d]
    own_packs = across(own_packs, far // 4)
    other_packs = across([other], far)
    order, every = list(range(1, end)) + [0, end], list(range(rows))
    behind = index_of([shards[d] for d in range(1, end)], b_tiles)
    for d in range(1, end):
        cols[d] = ((d - 1, 0), behind)
    place = jnp.stack([jnp.where(working, first, -1)] + [r ^ d for d in order]).astype(jnp.int32)

    def products(packs, spans):
        index = index_of(packs, a_tiles)
        starts = [(0, a_cols.size)] + [cols[d][0] for d in order]
        arrays = [b_cols, cols[end][1]] + ([behind] if end > 1 else [])
        which = [{0: 0, end: 1}.get(d, 2) for d in order]
        return [
            pl.pallas_call(
                functools.partial(product_kernel, starts, span, which),
                out_shape=jax.ShapeDtypeStruct((len(span), slots, block, block), dtype),
                in_specs=[SMEM] * (2 + len(arrays)) + [VMEM] * (len(order) + len(packs)),
                out_specs=VMEM,
                scratch_shapes=[
                    pltpu.VMEM((rows, inner_rows * row_count + 1, block, block), dtype),
                    pltpu.VMEM((rows, min(4, len(order)) * inner_rows * block, slots * block), dtype),
                    pltpu.SMEM((inner_rows, COLS_DEV), jnp.int32),
                ],
                compiler_params=PARAMS,
                cost_estimate=FREE,
            )(place, index, *arrays, *[shards[d] for d in order], *packs)
            for span in spans
        ]

    given = products(other_packs, [[i] for i in every])
    given = [give_back(x) for x in given]
    (kept,) = products(own_packs, [every])
    return jnp.where(working, kept, jnp.concatenate(given, axis=0))


def solution(mesh):
    return jax.shard_map(
        functools.partial(body, mesh.shape["row"], mesh.shape["col"]),
        mesh=mesh,
        in_specs=(
            P(("groups", "row"), "col", None, None),
            P(("groups", "row"), "col"),
            P(("groups", "row"), "col", None, None),
            P(("groups", "row"), "col"),
            P(("groups", "row"), "col"),
        ),
        out_specs=P(("groups", "row"), "col", None, None),
        check_vma=False,
    )
```
